32 devices in a mesh: dp: 8 (over z, y), tensor: 4 (over x, core).
Axes of the slice: x: 2, y: 2, z: 4, core: 2. Of those that a mesh axis runs over, the one named last changes fastest.
Arguments:
- tokens: bfloat16 [16384, 768], P('dp'), may hold values from -6 to 6
- cotangent: bfloat16 [16384, 768], P('dp'), may hold values from -6 to 6
- row_lengths: int32 [32], P('dp'), may hold values from 64 to 512
- present: int32 [32, 64], P('dp'), may hold values 0 or 1
- groups: int32 [32, 512], P('dp'), may hold values from 0 to 63, never falling along the last dimension, each value on 1 to 16 neighbouring positions
- attn_weight: float32 [3, 768, 768], P(None, 'dp', 'tensor'), may hold values from -0.21875 to 0.21875
- attn_first: float32 [3, 768, 768], P(None, 'dp', 'tensor'), may hold values from -24 to 24
- attn_second: float32 [3, 768, 768], P(None, 'dp', 'tensor'), may hold values from 64 to 256
- mix_weight: float32 [768, 768], P('tensor', 'dp'), may hold values from -2.5 to 2.5
- mix_first: float32 [768, 768], P('tensor', 'dp'), may hold values from -32 to 32
- mix_second: float32 [768, 768], P('tensor', 'dp'), may hold values from 128 to 512
- up_weight: float32 [768, 3072], P('dp', 'tensor'), may hold values from -0.21875 to 0.21875
- up_first: float32 [768, 3072], P('dp', 'tensor'), may hold values from -96 to 96
- up_second: float32 [768, 3072], P('dp', 'tensor'), may hold values from 1024 to 4096
- down_weight: float32 [3072, 768], P('tensor', 'dp'), may hold values from -0.109375 to 0.109375
- down_first: float32 [3072, 768], P('tensor', 'dp'), may hold values from -192 to 192
- down_second: float32 [3072, 768], P('tensor', 'dp'), may hold values from 4096 to 16384
- head_bias: float32 [2, 768], P(None, ('tensor', 'dp')), may hold values from -4 to 4
- head_first: float32 [2, 768], P(None, ('tensor', 'dp')), may hold values from -512 to 512
- head_second: float32 [2, 768], P(None, ('tensor', 'dp')), may hold values from 8192 to 32768
- wide_bias: float32 [3072], P(('tensor', 'dp')), may hold values from -4 to 4
- wide_first: float32 [3072], P(('tensor', 'dp')), may hold values from -512 to 512
- wide_second: float32 [3072], P(('tensor', 'dp')), may hold values from 8192 to 32768
- norm_gains: float32 [2, 768], P(None, 'dp'), may hold values from 0.5 to 1.5
- gain_first: float32 [2, 768], P(None, 'dp'), may hold values from -512 to 512
- gain_second: float32 [2, 768], P(None, 'dp'), may hold values from 8192 to 32768
- shift_bias: float32 [4, 768], P(None, 'dp'), may hold values from -4 to 4
- shift_first: float32 [4, 768], P(None, 'dp'), may hold values from -512 to 512
- shift_second: float32 [4, 768], P(None, 'dp'), may hold values from 8192 to 32768
Outputs:
- layer_out: bfloat16 [16384, 768], P('dp')
- tokens_grad: bfloat16 [16384, 768], P('dp')
- attn_weight_new: float32 [3, 768, 768], P(None, 'dp', 'tensor')
- attn_first_new: float32 [3, 768, 768], P(None, 'dp', 'tensor')
- attn_second_new: float32 [3, 768, 768], P(None, 'dp', 'tensor')
- mix_weight_new: float32 [768, 768], P('tensor', 'dp')
- mix_first_new: float32 [768, 768], P('tensor', 'dp')
- mix_second_new: float32 [768, 768], P('tensor', 'dp')
- up_weight_new: float32 [768, 3072], P('dp', 'tensor')
- up_first_new: float32 [768, 3072], P('dp', 'tensor')
- up_second_new: float32 [768, 3072], P('dp', 'tensor')
- down_weight_new: float32 [3072, 768], P('tensor', 'dp')
- down_first_new: float32 [3072, 768], P('tensor', 'dp')
- down_second_new: float32 [3072, 768], P('tensor', 'dp')
- head_bias_new: float32 [2, 768], P(None, ('tensor', 'dp'))
- head_first_new: float32 [2, 768], P(None, ('tensor', 'dp'))
- head_second_new: float32 [2, 768], P(None, ('tensor', 'dp'))
- wide_bias_new: float32 [3072], P(('tensor', 'dp'))
- wide_first_new: float32 [3072], P(('tensor', 'dp'))
- wide_second_new: float32 [3072], P(('tensor', 'dp'))
- norm_gains_new: float32 [2, 768], P(None, 'dp')
- gain_first_new: float32 [2, 768], P(None, 'dp')
- gain_second_new: float32 [2, 768], P(None, 'dp')
- shift_bias_new: float32 [4, 768], P(None, 'dp')
- shift_first_new: float32 [4, 768], P(None, 'dp')
- shift_second_new: float32 [4, 768], P(None, 'dp')
- norm_pairs: float32 [2, 15], replicated
The draws below stay inside these ranges and needn't reach their ends.
Inputs may be any that keep to these rules, and one draw needn't show every extreme that they name: Along a row the group ids never fall; every one of the 64 groups holds 1 to 16 slots.
All inputs are finite; a program needn't handle non-finite values. No bound on the sum of `present` on one device may be relied on, other than what follows from the above.
Results may differ from the reference program's by a relative error of at most 0.023.
Values may be sent and summed in bfloat16 or wider, within the bound.
No kernel may reach another device: no remote copies, remote signals or barrier semaphores. Data moves between devices by JAX's collectives and lax.ppermute only.
A program may use at most 128 MiB of HBM per device.

```python
import math
import jax
import jax.numpy as jnp
import numpy as np
from jax import lax

D = 768
HEADS = 12
HEAD = 64
FF = 3072
SEQ = 512
FEATS = 64
MIN_LEN = 64
MOST_TOK = 16
ROWS = 32
TOKENS = 16384
GRAD_SQ = 8192
ATTN_SQ = 64
MIX_SQ = 128
UP_SQ = 1024
DOWN_SQ = 4096
N_TENSOR = 4


def draw_row_lengths(key, part):
    drawn = jax.random.randint(key, (ROWS,), MIN_LEN, SEQ + 1)
    return drawn.at[0].set(SEQ).at[1].set(MIN_LEN)


def set_ends(values, key, smallest, high):
    longest = values.shape.index(max(values.shape))
    spots = []
    for shift in (0, 1):
        where = [jax.random.randint(jax.random.fold_in(key, axis), (), 0, length) for axis, length in enumerate(values.shape)]
        where[longest] = (where[longest] + shift) % values.shape[longest]
        spots.append(tuple(where))
    return values.at[spots[0]].set(smallest).at[spots[1]].set(high)


def block_levels(own_key, dims, cuts, low, top_value):
    loudness = 1.0
    for dim, shards_of in cuts:
        draws = jax.random.uniform(jax.random.fold_in(jax.random.fold_in(own_key, 6), dim), (shards_of,), jnp.float32, low / len(cuts), top_value / len(cuts))
        loudness = loudness * jnp.repeat(jnp.exp(draws), dims[dim] // shards_of).reshape((-1,) + (1,) * (len(dims) - 1 - dim))
    return loudness


def profile(count, total, limit, lean):
    portions = [(1 << 20) // math.isqrt(standing ** lean) + 1 for standing in range(2, count + 1)]
    spare, holding = total - limit - (count - 1), [1] * (count - 1)
    while spare > 0:
        free = [i for i in range(count - 1) if holding[i] < limit]
        whole, remaining = sum([portions[i] for i in free]), spare
        for i in free:
            extra = min(limit - holding[i], max(1, remaining * portions[i] // whole), spare)
            holding[i] = holding[i] + extra
            spare = spare - extra
    return np.array([limit] + holding)


def ragged(stream_key, number_of, total, limit, lean):
    if number_of == 2:
        one = jax.random.randint(stream_key, (), max(1, total - limit), min(limit, total - 1) + 1)
        return jnp.stack([one, total - one])
    sizes = jnp.asarray(profile(number_of, total, limit, lean), jnp.int32)
    pairs = (number_of - 1) // 2
    donor, taker = sizes[1:1 + 2 * pairs:2], sizes[2:2 + 2 * pairs:2]
    margin = jnp.minimum(donor - 1, limit - taker)
    passed = jax.random.randint(jax.random.fold_in(stream_key, 1), (pairs,), 0, 1 << 20) % (margin + 1)
    sizes = sizes.at[1:1 + 2 * pairs:2].set(donor - passed).at[2:2 + 2 * pairs:2].set(taker + passed)
    return sizes[jax.random.permutation(jax.random.fold_in(stream_key, 2), number_of)]


def centred(own_key, shape, width, most, split=(), dtype=jnp.bfloat16):
    values = width * jax.random.normal(own_key, shape, jnp.float32)
    if split:
        values = values * block_levels(own_key, shape, split, -0.22, 0.18)
    return jnp.clip(values, -most, most).astype(dtype)


def setup_inputs(seed: int = 0) -> dict:
    seeds = jax.random.split(jax.random.key(seed), 30)
    tokens = centred(seeds[0], (TOKENS, D), 1.0, 6.0, ((0, 8),))
    cotangent = centred(seeds[1], (TOKENS, D), 1.0, 6.0, ((0, 8),))
    row_lengths = draw_row_lengths(jax.random.fold_in(seeds[29], 71), 0)
    present = set_ends((jax.random.randint(seeds[3], (ROWS, FEATS), 0, 20) < 11).astype(jnp.int32), jax.random.fold_in(seeds[3], 1), 0, 1)
    groups = jax.vmap(lambda own: jnp.searchsorted(jnp.cumsum(ragged(own, FEATS, SEQ, MOST_TOK, 0)), jnp.arange(SEQ), side="right"))(jax.random.split(seeds[4], ROWS)).reshape((ROWS, SEQ)).astype(jnp.int32)
    attn_weight = centred(seeds[5], (3, D, D), D ** -0.5, 0.21875, ((1, 8), (2, 4)), jnp.float32)
    attn_first = centred(seeds[6], (3, D, D), (0.5 * ATTN_SQ ** 0.5), 24.0, ((1, 8), (2, 4)), jnp.float32)
    attn_second = jnp.clip(jnp.exp(math.log(256.0) - 1.3862944 * jax.random.uniform(seeds[7], (3, D, D), jnp.float32) ** block_levels(seeds[7], (3, D, D), ((1, 8), (2, 4)), -0.2, 0.2)), 64.0, 256.0)
    mix_weight = centred(seeds[8], (D, D), (D // 128) ** -0.5, 2.5, ((0, 4), (1, 8)), jnp.float32)
    mix_first = centred(seeds[9], (D, D), (0.5 * MIX_SQ ** 0.5), 32.0, ((0, 4), (1, 8)), jnp.float32)
    mix_second = jnp.clip(jnp.exp(math.log(512.0) - 1.3862944 * jax.random.uniform(seeds[10], (D, D), jnp.float32) ** block_levels(seeds[10], (D, D), ((0, 4), (1, 8)), -0.2, 0.2)), 128.0, 512.0)
    up_weight = centred(seeds[11], (D, FF), D ** -0.5, 0.21875, ((0, 8), (1, 4)), jnp.float32)
    up_first = centred(seeds[12], (D, FF), (0.5 * UP_SQ ** 0.5), 96.0, ((0, 8), (1, 4)), jnp.float32)
    up_second = jnp.clip(jnp.exp(math.log(4096.0) - 1.3862944 * jax.random.uniform(seeds[13], (D, FF), jnp.float32) ** block_levels(seeds[13], (D, FF), ((0, 8), (1, 4)), -0.2, 0.2)), 1024.0, 4096.0)
    down_weight = centred(seeds[14], (FF, D), FF ** -0.5, 0.109375, ((0, 4), (1, 8)), jnp.float32)
    down_first = centred(seeds[15], (FF, D), (0.5 * DOWN_SQ ** 0.5), 192.0, ((0, 4), (1, 8)), jnp.float32)
    down_second = jnp.clip(jnp.exp(math.log(16384.0) - 1.3862944 * jax.random.uniform(seeds[16], (FF, D), jnp.float32) ** block_levels(seeds[16], (FF, D), ((0, 4), (1, 8)), -0.2, 0.2)), 4096.0, 16384.0)
    head_bias = centred(seeds[17], (2, D), 0.3, 4.0, ((1, 32),), jnp.float32)
    head_first = centred(seeds[18], (2, D), (GRAD_SQ ** 0.5), 512.0, ((1, 32),), jnp.float32)
    head_second = jnp.clip(jnp.exp(math.log(32768.0) - 1.3862944 * jax.random.uniform(seeds[19], (2, D), jnp.float32) ** block_levels(seeds[19], (2, D), ((1, 32),), -0.2, 0.2)), 8192.0, 32768.0)
    wide_bias = centred(seeds[20], (FF,), 0.3, 4.0, ((0, 32),), jnp.float32)
    wide_first = centred(seeds[21], (FF,), (GRAD_SQ ** 0.5), 512.0, ((0, 32),), jnp.float32)
    wide_second = jnp.clip(jnp.exp(math.log(32768.0) - 1.3862944 * jax.random.uniform(seeds[22], (FF,), jnp.float32) ** block_levels(seeds[22], (FF,), ((0, 32),), -0.2, 0.2)), 8192.0, 32768.0)
    norm_gains = jnp.clip(1.0 + 0.1 * jax.random.normal(seeds[23], (2, D), jnp.float32), 0.5, 1.5)
    gain_first = centred(seeds[24], (2, D), (GRAD_SQ ** 0.5), 512.0, ((1, 8),), jnp.float32)
    gain_second = jnp.clip(jnp.exp(math.log(32768.0) - 1.3862944 * jax.random.uniform(seeds[25], (2, D), jnp.float32) ** block_levels(seeds[25], (2, D), ((1, 8),), -0.2, 0.2)), 8192.0, 32768.0)
    shift_bias = centred(seeds[26], (4, D), 0.3, 4.0, ((1, 8),), jnp.float32)
    shift_first = centred(seeds[27], (4, D), (GRAD_SQ ** 0.5), 512.0, ((1, 8),), jnp.float32)
    shift_second = jnp.clip(jnp.exp(math.log(32768.0) - 1.3862944 * jax.random.uniform(seeds[28], (4, D), jnp.float32) ** block_levels(seeds[28], (4, D), ((1, 8),), -0.2, 0.2)), 8192.0, 32768.0)
    return dict(tokens=tokens, cotangent=cotangent, row_lengths=row_lengths, present=present, groups=groups, attn_weight=attn_weight, attn_first=attn_first, attn_second=attn_second, mix_weight=mix_weight, mix_first=mix_first, mix_second=mix_second, up_weight=up_weight, up_first=up_first, up_second=up_second, down_weight=down_weight, down_first=down_first, down_second=down_second, head_bias=head_bias, head_first=head_first, head_second=head_second, wide_bias=wide_bias, wide_first=wide_first, wide_second=wide_second, norm_gains=norm_gains, gain_first=gain_first, gain_second=gain_second, shift_bias=shift_bias, shift_first=shift_first, shift_second=shift_second)


HIGH = lax.Precision.HIGHEST

@jax.custom_vjp
def low(v):
    return lax.optimization_barrier(v.astype(jnp.bfloat16)).astype(jnp.float32)

@jax.custom_vjp
def low_back(v):
    return v

def low_keep(v):
    return (low(v), None)

def low_pass(kept, grad):
    return (grad,)

def back_keep(v):
    return (v, None)

def back_low(kept, grad):
    return (low(grad),)
low.defvjp(low_keep, low_pass)
low_back.defvjp(back_keep, back_low)

def layer_norm(summed):
    center = summed - lax.optimization_barrier(jnp.mean(summed, axis=-1, keepdims=True))
    spread = lax.optimization_barrier(jnp.mean(center * center, axis=-1, keepdims=True))
    return center * lax.rsqrt(spread + 1e-05)

def visibility(length, present_row, group_row):
    positions = jnp.arange(SEQ)
    key_open = (positions < length) & (present_row[group_row] == 1)
    return key_open[None, :] | (group_row[:, None] == group_row[None, :])

def attend_item(row_item):
    queries, key_rows, value_rows, visible = row_item
    scores = jnp.einsum('qhd,khd->hqk', queries, key_rows, precision=HIGH) * HEAD ** (-0.5)
    scores = low_back(jnp.where(visible[None], scores, -1e+30))
    largest = lax.optimization_barrier(jnp.max(scores, axis=-1, keepdims=True))
    exponent = jnp.exp(scores - largest)
    softmax_probs = exponent / lax.optimization_barrier(jnp.sum(exponent, axis=-1, keepdims=True))
    return jnp.einsum('hqk,khd->qhd', low(softmax_probs), value_rows, precision=HIGH)

def forward(params, token_rows, lengths, present, groups):
    attn_matrix, mix_matrix, up_matrix, down_matrix, head_shift, wide_shift, gain_rows, shift_rows = params
    row_count = lengths.shape[0]
    head_width = D // N_TENSOR
    unit_width = FF // N_TENSOR
    query_parts, key_parts, value_parts = ([], [], [])
    for tensor_group in range(N_TENSOR):
        window = slice(tensor_group * head_width, (tensor_group + 1) * head_width)
        own_input = low_back(token_rows)
        query_parts.append(low(low_back(jnp.dot(own_input, attn_matrix[0][:, window], precision=HIGH) + head_shift[0][window])))
        key_parts.append(low(low_back(jnp.dot(own_input, attn_matrix[1][:, window], precision=HIGH))))
        value_parts.append(low(low_back(jnp.dot(own_input, attn_matrix[2][:, window], precision=HIGH) + head_shift[1][window])))
    row_shape = (row_count, SEQ, HEADS, HEAD)
    queries = jnp.concatenate(query_parts, axis=1).reshape(row_shape)
    key_rows = jnp.concatenate(key_parts, axis=1).reshape(row_shape)
    value_rows = jnp.concatenate(value_parts, axis=1).reshape(row_shape)
    visible = jax.vmap(visibility)(lengths, present, groups)
    context = lax.map(jax.checkpoint(attend_item), (queries, key_rows, value_rows, visible))
    context = low(low_back(context.reshape(row_count * SEQ, D)))
    attended = shift_rows[0]
    for tensor_group in range(N_TENSOR):
        window = slice(tensor_group * head_width, (tensor_group + 1) * head_width)
        attended = attended + low(low_back(jnp.dot(context[:, window], mix_matrix[window, :], precision=HIGH)))
    normed = layer_norm(token_rows + attended) * gain_rows[0] + shift_rows[1]
    mixed = shift_rows[2]
    for tensor_group in range(N_TENSOR):
        unit_window = slice(tensor_group * unit_width, (tensor_group + 1) * unit_width)
        own_input = low_back(low(normed))
        hidden = low_back(jnp.dot(own_input, up_matrix[:, unit_window], precision=HIGH) + wide_shift[unit_window])
        active = low(jax.nn.gelu(hidden, approximate=False))
        mixed = mixed + low(low_back(jnp.dot(active, down_matrix[unit_window, :], precision=HIGH)))
    return layer_norm(normed + mixed) * gain_rows[1] + shift_rows[3]

def square_sums(array, piece_count):
    if piece_count == 1:
        return [jnp.sum(array * array)]
    return [jnp.sum(array[member] * array[member]) for member in range(piece_count)]

def trust_factor(trust, offset, piece_count, rank_count):
    if piece_count == 1:
        return trust[offset]
    return trust[offset:offset + piece_count].reshape((piece_count,) + (1,) * (rank_count - 1))

def reference(tokens, cotangent, row_lengths, present, groups, attn_weight, attn_first, attn_second, mix_weight, mix_first, mix_second, up_weight, up_first, up_second, down_weight, down_first, down_second, head_bias, head_first, head_second, wide_bias, wide_first, wide_second, norm_gains, gain_first, gain_second, shift_bias, shift_first, shift_second):
    masters = (attn_weight, mix_weight, up_weight, down_weight, head_bias, wide_bias, norm_gains, shift_bias)
    firsts = (attn_first, mix_first, up_first, down_first, head_first, wide_first, gain_first, shift_first)
    seconds = (attn_second, mix_second, up_second, down_second, head_second, wide_second, gain_second, shift_second)
    params = tuple((master.astype(jnp.bfloat16).astype(jnp.float32) for master in masters))
    block_rows = math.gcd(ROWS, max(1, 4096 // SEQ))
    block_count = ROWS // block_rows
    token_blocks = tokens.astype(jnp.float32).reshape(block_count, block_rows * SEQ, D)
    cot_blocks = cotangent.astype(jnp.float32).reshape(block_count, block_rows * SEQ, D)
    length_blocks = row_lengths.reshape(block_count, block_rows)
    present_blocks = present.reshape(block_count, block_rows, FEATS)
    group_blocks = groups.reshape(block_count, block_rows, SEQ)

    def one_block(totals, block_item):
        token_rows, cot_rows, lengths, present_rows, group_rows = block_item

        def local_forward(param_tuple, input_rows):
            return forward(param_tuple, input_rows, lengths, present_rows, group_rows)
        output, pullback = jax.vjp(local_forward, params, token_rows)
        param_grads, token_grads = pullback(cot_rows)
        totals = jax.tree.map(jnp.add, totals, param_grads)
        return (totals, (output.astype(jnp.bfloat16), token_grads.astype(jnp.bfloat16)))
    zero_grads = jax.tree.map(jnp.zeros_like, params)
    gradients, (outputs, input_grads) = lax.scan(one_block, zero_grads, (token_blocks, cot_blocks, length_blocks, present_blocks, group_blocks))
    layer_out = outputs.reshape(TOKENS, D)
    tokens_grad = input_grads.reshape(TOKENS, D)
    piece_counts = (3, 1, 1, 1, 2, 1, 2, 4)
    new_firsts, new_seconds, updates, weight_sq, update_sq = ([], [], [], [], [])
    for master, first_old, second_old, gradient, piece_count in zip(masters, firsts, seconds, gradients, piece_counts):
        first_new = 0.5 * first_old + 0.5 * gradient
        second_new = 0.5 * second_old + 0.5 * gradient * gradient
        update = first_new / (jnp.sqrt(second_new) + 1e-06) + 0.01 * master
        new_firsts.append(first_new)
        new_seconds.append(second_new)
        updates.append(update)
        weight_sq.extend(square_sums(master, piece_count))
        update_sq.extend(square_sums(update, piece_count))
    norm_pairs = jnp.sqrt(jnp.stack([jnp.stack(weight_sq), jnp.stack(update_sq)]))
    trust = norm_pairs[0] / (norm_pairs[1] + 1e-06)
    new_masters = []
    offset = 0
    for master, update, piece_count in zip(masters, updates, piece_counts):
        factor = trust_factor(trust, offset, piece_count, master.ndim)
        new_masters.append(master - 0.5 * factor * update)
        offset = offset + piece_count
    return (layer_out, tokens_grad, new_masters[0], new_firsts[0], new_seconds[0], new_masters[1], new_firsts[1], new_seconds[1], new_masters[2], new_firsts[2], new_seconds[2], new_masters[3], new_firsts[3], new_seconds[3], new_masters[4], new_firsts[4], new_seconds[4], new_masters[5], new_firsts[5], new_seconds[5], new_masters[6], new_firsts[6], new_seconds[6], new_masters[7], new_firsts[7], new_seconds[7], norm_pairs)
```

```python
import functools

import jax
import jax.numpy as jnp
from jax import lax
from jax.experimental import pallas as pl
from jax.experimental.pallas import tpu as pltpu
from jax.sharding import PartitionSpec as P

HEAD = 64
BF = jnp.bfloat16
F32 = jnp.float32
NN = (((1,), (0,)), ((), ()))
NT = (((1,), (1,)), ((), ()))
TN = (((0,), (0,)), ((), ()))


def mm(a, b, dims):
    return lax.dot_general(a, b, dims, preferred_element_type=F32)


class GenericComm:
    def __init__(self, dp, tensor):
        self.dp, self.tensor = dp, tensor

    def gather(self, shard):
        rows = lax.all_gather(shard, "dp", axis=0, tiled=True)
        return lax.all_gather(rows, "tensor", axis=0)

    def scatter(self, blocks):
        stacked = jnp.stack(blocks)
        own = lax.psum_scatter(stacked, "tensor", scatter_dimension=0)
        return lax.psum_scatter(own, "dp", scatter_dimension=0, tiled=True).astype(F32)

    def gather_small(self, vector):
        return lax.all_gather(lax.all_gather(vector, "dp", axis=0), "tensor", axis=0)

    def scatter_small(self, vectors):
        own = lax.psum_scatter(vectors, "tensor", scatter_dimension=0)
        return lax.psum_scatter(own, "dp", scatter_dimension=0)

    def total(self, values):
        return lax.psum(values, ("dp", "tensor"))

    def gather_rows(self, rows):
        return lax.all_gather(rows, "tensor", axis=0, tiled=True)


class GridComm:
    def __init__(self):
        self.z = lax.axis_index("dp") // 2
        self.y = lax.axis_index("dp") % 2

    @staticmethod
    def send(array, dp_xor, tensor_xor):
        pairs = [
            (d * 4 + t, (d ^ dp_xor) * 4 + (t ^ tensor_xor)) for d in range(8) for t in range(4)
        ]
        return lax.ppermute(array, ("dp", "tensor"), pairs)

    def send_core(self, array):
        return self.send(array, 0, 1)

    def send_x(self, array):
        return self.send(array, 0, 2)

    def send_y(self, array):
        return self.send(array, 1, 0)

    def send_z(self, array, k):
        return self.send(array, 2 * k, 0)

    def gather_pieces(self, shard):
        own = jnp.stack([shard] + [self.send_z(shard, k) for k in (1, 2, 3)])
        from_x = self.send_x(own)
        from_y = self.send_y(own)
        diag_low = self.send_x(from_y[:2])
        diag_high = self.send_y(from_x[2:])
        near = [own, from_y]
        far = [from_x, diag_low, diag_high]
        return [
            near,
            [self.send_core(a) for a in near],
            far,
            [self.send_core(a) for a in far],
        ]

    def gather(self, shard):
        pieces = self.gather_pieces(shard)
        return place(pieces, self.z, self.y, shard.shape)

    def split(self, block):
        view = block.reshape(4, 2, block.shape[0] // 8, block.shape[1])
        own = lax.dynamic_index_in_dim(view, self.y, 1, keepdims=False)
        other = lax.dynamic_index_in_dim(view, 1 - self.y, 1, keepdims=False)
        return own, other

    def scatter(self, blocks):
        near_own, near_other = self.split(blocks[0])
        far_own, far_other = self.split(blocks[2])
        near_got = self.send_core(blocks[1])
        far_got = self.send_core(blocks[3])
        near_got_own, near_got_other = self.split(near_got)
        far_got_own, far_got_other = self.split(far_got)
        diag = add(far_other, far_got_other)
        diag_low = self.send_x(diag[:2])
        diag_high = self.send_y(diag[2:])
        zeros = jnp.zeros_like(diag_low)
        to_y = add(near_other, near_got_other, jnp.concatenate([diag_low, zeros]))
        to_x = add(far_own, far_got_own, jnp.concatenate([zeros, diag_high]))
        from_x = self.send_x(to_x)
        from_y = self.send_y(to_y)
        own = add(near_own, near_got_own, from_x, from_y)
        parts = [lax.dynamic_index_in_dim(own, self.z ^ k, 0, keepdims=False) for k in range(4)]
        total = parts[0].astype(F32)
        for k in (1, 2, 3):
            total = total + self.send_z(parts[k], k).astype(F32)
        return total

    def gather_small(self, vector):
        own = jnp.stack([vector] + [self.send_z(vector, k) for k in (1, 2, 3)])
        own = jnp.stack([own, self.send_y(own)], axis=1)
        own = jnp.stack([own, self.send_x(own)])
        own = jnp.stack([own, self.send_core(own)], axis=1)
        own = own.reshape((4, 2, 2, 2) + vector.shape)
        own = swap_if(self.z >= 2, own, 1)
        own = swap_if(self.z % 2 == 1, own, 2)
        own = swap_if(self.y == 1, own, 3)
        return own.reshape((4, 8) + vector.shape)

    def scatter_small(self, vectors):
        shape = vectors.shape[2:]
        near = vectors[0::2] + self.send_core(vectors[1::2])
        own = near[0] + self.send_x(near[1])
        own = own.reshape((4, 2) + shape)
        mine = lax.dynamic_index_in_dim(own, self.y, 1, keepdims=False)
        other = lax.dynamic_index_in_dim(own, 1 - self.y, 1, keepdims=False)
        mine = mine + self.send_y(other)
        parts = [lax.dynamic_index_in_dim(mine, self.z ^ k, 0, keepdims=False) for k in range(4)]
        total = parts[0]
        for k in (1, 2, 3):
            total = total + self.send_z(parts[k], k)
        return total

    def total(self, values):
        values = values + self.send_core(values)
        values = values + self.send_x(values)
        values = values + self.send_y(values)
        values = values + self.send_z(values, 1)
        return values + self.send_z(values, 2)

    def gather_rows(self, rows):
        far = self.send_x(rows)
        pieces = [rows, self.send_core(rows), far, self.send_core(far)]
        return place_rows(pieces, lax.axis_index("tensor"))


def swap_if(flag, array, axis):
    return jnp.where(flag, jnp.flip(array, axis), array)


def place_rows(pieces, rank):
    n = pieces[0].shape[0]

    def kernel(rank_ref, *refs):
        out_ref, sems = refs[len(pieces)], refs[len(pieces) + 1]
        copies = [
            pltpu.make_async_copy(refs[p], out_ref.at[rank_ref[0] ^ p], sems.at[p])
            for p in range(len(pieces))
        ]
        for copy in copies:
            copy.start()
        for copy in copies:
            copy.wait()

    out = pl.pallas_call(
        kernel,
        out_shape=jax.ShapeDtypeStruct((len(pieces),) + pieces[0].shape, pieces[0].dtype),
        in_specs=[pl.BlockSpec(memory_space=pltpu.SMEM)]
        + [pl.BlockSpec(memory_space=pl.ANY)] * len(pieces),
        out_specs=pl.BlockSpec(memory_space=pl.ANY),
        scratch_shapes=[pltpu.SemaphoreType.DMA((len(pieces),))],
        cost_estimate=pl.CostEstimate(flops=0, bytes_accessed=8 << 20, transcendentals=0),
    )(rank.reshape(1).astype(jnp.int32), *pieces)
    return out.reshape((len(pieces) * n,) + pieces[0].shape[1:])


def add(*arrays):
    total = arrays[0].astype(F32)
    for array in arrays[1:]:
        total = total + array.astype(F32)
    return total.astype(BF)


def place(pieces, z, y, shard_shape):
    flat = [array for group in pieces for array in group]
    plan = []
    index = 0
    for p, group in enumerate(pieces):
        chunk = 0
        for array in group:
            for offset in range(array.shape[0]):
                plan.append((index, offset, p, chunk // 4, chunk % 4))
                chunk += 1
            index += 1

    def kernel(where_ref, *refs):
        sources, out_ref, sems = refs[: len(flat)], refs[len(flat)], refs[len(flat) + 1]
        z_at, y_at = where_ref[0], where_ref[1]
        copies = []
        for number, (source, offset, p, y_rel, z_rel) in enumerate(plan):
            row = (z_at ^ z_rel) * 2 + (y_at ^ y_rel)
            copies.append(
                pltpu.make_async_copy(
                    sources[source].at[offset], out_ref.at[p, row], sems.at[number]
                )
            )
        for copy in copies:
            copy.start()
        for copy in copies:
            copy.wait()

    out = pl.pallas_call(
        kernel,
        out_shape=jax.ShapeDtypeStruct((len(pieces), 8) + tuple(shard_shape), BF),
        in_specs=[pl.BlockSpec(memory_space=pltpu.SMEM)]
        + [pl.BlockSpec(memory_space=pl.ANY)] * len(flat),
        out_specs=pl.BlockSpec(memory_space=pl.ANY),
        scratch_shapes=[pltpu.SemaphoreType.DMA((len(plan),))],
        cost_estimate=pl.CostEstimate(flops=0, bytes_accessed=10 << 20, transcendentals=0),
    )(jnp.stack([z, y]).astype(jnp.int32), *flat)
    return out.reshape(len(pieces), 8 * shard_shape[0], shard_shape[1])


def attn_fwd_kernel(
    tok_ref, w_ref, bias_ref, gq_ref, gk_ref, open_ref,
    qkv_ref, ctx_ref, e_ref, inv_ref, att_ref, mask_ref,
):
    step = pl.program_id(0)
    width = ctx_ref.shape[2]

    @pl.when(step == 0)
    def _():
        seen = (open_ref[...] == 1) | (gq_ref[...] == gk_ref[...])
        mask_ref[...] = jnp.where(seen, 0.0, -1e30)
        att_ref[...] = jnp.zeros_like(att_ref)

    qkv = mm(tok_ref[...], w_ref[0, :, : 3 * width], NN)
    qkv = (qkv + bias_ref[0]).astype(BF)
    qkv_ref[0] = qkv
    lane = lax.broadcasted_iota(jnp.int32, (qkv.shape[0], 128), 1)
    contexts = []
    inv_all = jnp.zeros((qkv.shape[0], 128), F32)
    for h in range(width // HEAD):
        q = qkv[:, h * HEAD : (h + 1) * HEAD] * jnp.asarray(HEAD**-0.5, BF)
        k = qkv[:, width + h * HEAD : width + (h + 1) * HEAD]
        v = qkv[:, 2 * width + h * HEAD : 2 * width + (h + 1) * HEAD]
        s = mm(q, k, NT) + mask_ref[...]
        e = jnp.exp(s - jnp.max(s, axis=-1, keepdims=True)).astype(BF)
        e_ref[0, h] = e
        v_one = jnp.concatenate([v, jnp.ones_like(v)], axis=1)
        r = mm(e, v_one, NN)
        inv = 1.0 / r[:, HEAD : HEAD + 1]
        contexts.append((r[:, :HEAD] * inv).astype(BF))
        inv_all = jnp.where(lane == h, inv, inv_all)
    ctx = jnp.concatenate(contexts, axis=1)
    ctx_ref[0] = ctx
    inv_ref[0] = inv_all
    att_ref[...] += mm(ctx, w_ref[0, :, 3 * width :], NT)


def attn_fwd(tok, w, bias, groups, key_open):
    blocks, d, wide = w.shape
    n = tok.shape[0]
    width = wide // 4
    heads = width // HEAD
    full = lambda *s: pl.BlockSpec(s, lambda i: (0,) * len(s))
    per = lambda *s: pl.BlockSpec((1,) + s, lambda i: (i,) + (0,) * len(s))
    return pl.pallas_call(
        attn_fwd_kernel,
        grid=(blocks,),
        in_specs=[
            full(n, d), per(d, wide), per(1, 3 * width), full(n, 1), full(1, n), full(1, n),
        ],
        out_specs=[
            per(n, 3 * width), per(n, width), per(heads, n, n), per(n, 128), full(n, d),
        ],
        out_shape=[
            jax.ShapeDtypeStruct((blocks, n, 3 * width), BF),
            jax.ShapeDtypeStruct((blocks, n, width), BF),
            jax.ShapeDtypeStruct((blocks, heads, n, n), BF),
            jax.ShapeDtypeStruct((blocks, n, 128), F32),
            jax.ShapeDtypeStruct((n, d), F32),
        ],
        scratch_shapes=[pltpu.VMEM((n, n), F32)],
        compiler_params=pltpu.CompilerParams(vmem_limit_bytes=40 << 20),
        cost_estimate=pl.CostEstimate(
            flops=14 << 30, bytes_accessed=16 << 20, transcendentals=12 * n * n
        ),
    )(tok, w, bias, groups.reshape(n, 1), groups.reshape(1, n), key_open.reshape(1, n))


def attn_bwd_kernel(
    da_ref, w_ref, qkv_ref, ctx_ref, e_ref, inv_ref, ds1_ref, dqkv_ref, sum_ref, tg_ref
):
    step = pl.program_id(0)
    width = ctx_ref.shape[2]

    @pl.when(step == 0)
    def _():
        tg_ref[...] = ds1_ref[...]

    dctx = mm(da_ref[...], w_ref[0, :, 3 * width :], NN).astype(BF).astype(F32)
    scale = HEAD**-0.5
    dqs, dks, dvs = [], [], []
    for h in range(width // HEAD):
        q = qkv_ref[0, :, h * HEAD : (h + 1) * HEAD]
        k = qkv_ref[0, :, width + h * HEAD : width + (h + 1) * HEAD]
        v = qkv_ref[0, :, 2 * width + h * HEAD : 2 * width + (h + 1) * HEAD]
        e = e_ref[0, h]
        inv = inv_ref[0, :, h : h + 1]
        do = dctx[:, h * HEAD : (h + 1) * HEAD] * inv
        ctx = ctx_ref[0, :, h * HEAD : (h + 1) * HEAD].astype(F32)
        delta = jnp.sum(do * ctx, axis=-1, keepdims=True)
        do_low = do.astype(BF)
        dp = mm(do_low, v, NT)
        ds = (e.astype(F32) * (dp - delta)).astype(BF)
        dvs.append(mm(e, do_low, TN))
        dqs.append(mm(ds, k, NN) * scale)
        dks.append(mm(ds, q, TN) * scale)
    dqkv = jnp.concatenate(dqs + dks + dvs, axis=1).astype(BF)
    dqkv_ref[0] = dqkv
    sum_ref[0] = jnp.sum(dqkv.astype(F32), axis=0, keepdims=True)
    tg_ref[...] += mm(dqkv, w_ref[0, :, : 3 * width], NT)


def attn_bwd(da, w, qkv, ctx, e, inv, ds1):
    blocks, d, wide = w.shape
    n = da.shape[0]
    width = wide // 4
    heads = width // HEAD
    full = lambda *s: pl.BlockSpec(s, lambda i: (0,) * len(s))
    per = lambda *s: pl.BlockSpec((1,) + s, lambda i: (i,) + (0,) * len(s))
    return pl.pallas_call(
        attn_bwd_kernel,
        grid=(blocks,),
        in_specs=[
            full(n, d), per(d, wide), per(n, 3 * width), per(n, width), per(heads, n, n),
            per(n, 128), full(n, d),
        ],
        out_specs=[per(n, 3 * width), per(1, 3 * width), full(n, d)],
        out_shape=[
            jax.ShapeDtypeStruct((blocks, n, 3 * width), BF),
            jax.ShapeDtypeStruct((blocks, 1, 3 * width), F32),
            jax.ShapeDtypeStruct((n, d), F32),
        ],
        compiler_params=pltpu.CompilerParams(vmem_limit_bytes=40 << 20),
        cost_estimate=pl.CostEstimate(
            flops=20 << 30, bytes_accessed=16 << 20, transcendentals=0
        ),
    )(da, w, qkv, ctx, e, inv, ds1)


def layer_norm(summed):
    center = summed - jnp.mean(summed, axis=-1, keepdims=True)
    spread = jnp.mean(center * center, axis=-1, keepdims=True)
    scaled = lax.rsqrt(spread + 1e-05)
    return (center * scaled, scaled)


def norm_back(upstream, normal, scaled):
    inner_sum = (
        upstream
        - jnp.mean(upstream, axis=-1, keepdims=True)
        - normal * jnp.mean(upstream * normal, axis=-1, keepdims=True)
    )
    return scaled * inner_sum


def square_sums(array, piece_count, weight_factor):
    if piece_count == 1:
        return [jnp.sum(array * array) * weight_factor]
    return [jnp.sum(array[member] * array[member]) * weight_factor for member in range(piece_count)]


def trust_factor(trust, offset, piece_count, rank_count):
    if piece_count == 1:
        return trust[offset]
    return trust[offset : offset + piece_count].reshape((piece_count,) + (1,) * (rank_count - 1))


def on_device(
    dp_size, tensor_size,
    tokens, cotangent, row_lengths, present, groups,
    attn_weight, attn_first, attn_second,
    mix_weight, mix_first, mix_second,
    up_weight, up_first, up_second,
    down_weight, down_first, down_second,
    head_bias, head_first, head_second,
    wide_bias, wide_first, wide_second,
    norm_gains, gain_first, gain_second,
    shift_bias, shift_first, shift_second,
):
    comm = GridComm() if (dp_size, tensor_size) == (8, 4) else GenericComm(dp_size, tensor_size)
    rank = lax.axis_index("tensor")
    row_count, n = groups.shape
    assert row_count == tensor_size
    d = tokens.shape[1]
    width = attn_weight.shape[2]
    head_own, wide_own, gain_own = head_bias.shape[1], wide_bias.shape[0], norm_gains.shape[1]

    attn_shard = jnp.concatenate(
        [attn_weight[0], attn_weight[1], attn_weight[2], mix_weight.T], axis=1
    ).astype(BF)
    up_shard = up_weight.astype(BF)
    down_shard = down_weight.T.astype(BF)
    small = jnp.concatenate(
        [head_bias.reshape(-1), wide_bias, norm_gains.reshape(-1), shift_bias.reshape(-1)]
    )
    small = small.astype(BF).astype(F32)
    cuts = (2 * head_own, wide_own, 2 * gain_own, 4 * gain_own)
    pad = -sum(cuts) % 1024
    small = jnp.pad(small, (0, pad)).reshape(-1, 128)

    small_all = comm.gather_small(small).reshape(tensor_size, dp_size, -1)
    attn_all = comm.gather(attn_shard)
    up_all = comm.gather(up_shard)
    down_all = comm.gather(down_shard)

    at = [0, cuts[0], cuts[0] + cuts[1], cuts[0] + cuts[1] + cuts[2], sum(cuts)]
    heads_low = small_all[:, :, at[0] : at[1]].reshape(tensor_size, dp_size, 2, head_own)
    heads_low = heads_low.transpose(0, 2, 1, 3).reshape(tensor_size, 2, width)
    wide_low = small_all[:, :, at[1] : at[2]].reshape(tensor_size, 1, -1)
    gains = small_all[0, :, at[2] : at[3]].reshape(dp_size, 2, gain_own)
    gains = gains.transpose(1, 0, 2).reshape(2, d)
    shifts = small_all[0, :, at[3] : at[4]].reshape(dp_size, 4, gain_own)
    shifts = shifts.transpose(1, 0, 2).reshape(4, d)

    tok = lax.dynamic_slice_in_dim(tokens, rank * n, n, 0)
    cot = lax.dynamic_slice_in_dim(cotangent, rank * n, n, 0)
    group_row = lax.dynamic_index_in_dim(groups, rank, 0, keepdims=False)
    present_row = lax.dynamic_index_in_dim(present, rank, 0, keepdims=False)
    length = lax.dynamic_index_in_dim(row_lengths, rank, 0, keepdims=False)
    feature_ids = jnp.arange(present_row.shape[0])
    present_key = jnp.sum(
        (group_row[:, None] == feature_ids[None, :]) * present_row[None, :], axis=1
    )
    key_open = ((jnp.arange(n) < length) & (present_key == 1)).astype(jnp.int32)

    qkv_bias = jnp.concatenate(
        [heads_low[:, :1], jnp.zeros_like(heads_low[:, :1]), heads_low[:, 1:]], axis=2
    )
    qkv, ctx, e, inv, attended = attn_fwd(tok, attn_all, qkv_bias, group_row, key_open)
    normal_one, scaled_one = layer_norm(tok.astype(F32) + attended + shifts[0])
    normed = normal_one * gains[0] + shifts[1]
    normed_low = normed.astype(BF)
    hidden = jnp.einsum("td,pdf->ptf", normed_low, up_all, preferred_element_type=F32) + wide_low
    active, gelu_back = jax.vjp(functools.partial(jax.nn.gelu, approximate=False), hidden)
    active_low = active.astype(BF)
    mixed = jnp.einsum("ptf,pdf->td", active_low, down_all, preferred_element_type=F32)
    normal_two, scaled_two = layer_norm(normed + mixed + shifts[2])
    layer_out = (normal_two * gains[1] + shifts[3]).astype(BF)
    layer_out_all = comm.gather_rows(layer_out)
    upstream = cot.astype(F32)
    gain_two_grad = jnp.sum(upstream * normal_two, axis=0)
    shift_three_grad = jnp.sum(upstream, axis=0)
    back_two = norm_back(upstream * gains[1], normal_two, scaled_two)
    shift_two_grad = jnp.sum(back_two, axis=0)
    df = back_two.astype(BF)
    down_grads = [mm(df, active_low[p], TN).astype(BF) for p in range(tensor_size)]
    down_sum = comm.scatter(down_grads)
    active_grad = jnp.einsum("td,pdf->ptf", df, down_all, preferred_element_type=F32)
    dh = gelu_back(active_grad)[0].astype(BF)
    wide_grad = jnp.sum(dh.astype(F32), axis=1)
    up_grads = [mm(normed_low, dh[p], TN).astype(BF) for p in range(tensor_size)]
    up_sum = comm.scatter(up_grads)
    normed_grad = back_two + jnp.einsum("ptf,pdf->td", dh, up_all, preferred_element_type=F32)
    gain_one_grad = jnp.sum(normed_grad * normal_one, axis=0)
    shift_one_grad = jnp.sum(normed_grad, axis=0)
    back_one = norm_back(normed_grad * gains[0], normal_one, scaled_one)
    shift_zero_grad = jnp.sum(back_one, axis=0)
    da = back_one.astype(BF)
    dqkv, dqkv_sum, tokens_grad = attn_bwd(da, attn_all, qkv, ctx, e, inv, back_one)
    tokens_grad_all = comm.gather_rows(tokens_grad.astype(BF))
    attn_grads = [
        jnp.concatenate([mm(tok, dqkv[p], TN), mm(da, ctx[p], TN)], axis=1).astype(BF)
        for p in range(tensor_size)
    ]
    attn_sum = comm.scatter(attn_grads)

    head_grad = jnp.stack([dqkv_sum[:, 0, :width], dqkv_sum[:, 0, 2 * width :]], axis=1)
    head_grad = head_grad.reshape(tensor_size, 2, dp_size, head_own).transpose(0, 2, 1, 3)
    wide_part = wide_grad.reshape(tensor_size, dp_size, wide_own)
    vectors = jnp.stack(
        [
            gain_one_grad, gain_two_grad,
            shift_zero_grad, shift_one_grad, shift_two_grad, shift_three_grad,
        ]
    )
    vectors = vectors.reshape(6, dp_size, gain_own).transpose(1, 0, 2).reshape(1, dp_size, -1)
    small_grad = jnp.concatenate(
        [
            head_grad.reshape(tensor_size, dp_size, -1),
            wide_part,
            jnp.broadcast_to(vectors, (tensor_size,) + vectors.shape[1:]),
        ],
        axis=2,
    )
    small_grad = jnp.pad(small_grad, ((0, 0), (0, 0), (0, pad)))
    small_sum = comm.scatter_small(
        small_grad.reshape((tensor_size, dp_size) + small.shape)
    ).reshape(-1)

    reduced = (
        jnp.stack([attn_sum[:, k * width : (k + 1) * width] for k in range(3)]),
        attn_sum[:, 3 * width :].T,
        up_sum,
        down_sum.T,
        small_sum[at[0] : at[1]].reshape(head_bias.shape),
        small_sum[at[1] : at[2]],
        small_sum[at[2] : at[3]].reshape(norm_gains.shape),
        small_sum[at[3] : at[4]].reshape(shift_bias.shape),
    )
    masters = (
        attn_weight, mix_weight, up_weight, down_weight,
        head_bias, wide_bias, norm_gains, shift_bias,
    )
    firsts = (
        attn_first, mix_first, up_first, down_first,
        head_first, wide_first, gain_first, shift_first,
    )
    seconds = (
        attn_second, mix_second, up_second, down_second,
        head_second, wide_second, gain_second, shift_second,
    )
    piece_counts = (3, 1, 1, 1, 2, 1, 2, 4)
    share = 1.0 / tensor_size
    weight_factors = (1.0, 1.0, 1.0, 1.0, 1.0, 1.0, share, share)
    new_firsts, new_seconds, updates, weight_sq, update_sq = ([], [], [], [], [])
    for master, first_old, second_old, gradient, piece_count, weight_factor in zip(
        masters, firsts, seconds, reduced, piece_counts, weight_factors
    ):
        first_new = 0.5 * first_old + 0.5 * gradient
        second_new = 0.5 * second_old + 0.5 * gradient * gradient
        update = first_new / (jnp.sqrt(second_new) + 1e-06) + 0.01 * master
        new_firsts.append(first_new)
        new_seconds.append(second_new)
        updates.append(update)
        weight_sq.extend(square_sums(master, piece_count, weight_factor))
        update_sq.extend(square_sums(update, piece_count, weight_factor))
    square_totals = comm.total(jnp.stack([jnp.stack(weight_sq), jnp.stack(update_sq)]))
    norm_pairs = jnp.sqrt(square_totals)
    trust = norm_pairs[0] / (norm_pairs[1] + 1e-06)
    out = [layer_out_all, tokens_grad_all]
    offset = 0
    for index, (master, update, piece_count) in enumerate(zip(masters, updates, piece_counts)):
        factor = trust_factor(trust, offset, piece_count, master.ndim)
        out.extend([master - 0.5 * factor * update, new_firsts[index], new_seconds[index]])
        offset = offset + piece_count
    return tuple(out) + (norm_pairs,)


def solution(mesh):
    rows = P("dp", None)
    attn, mix, up = P(None, "dp", "tensor"), P("tensor", "dp"), P("dp", "tensor")
    head, wide, col = P(None, ("tensor", "dp")), P(("tensor", "dp")), P(None, "dp")
    params = tuple(spec for spec in (attn, mix, up, mix, head, wide, col, col) for _ in range(3))
    return jax.shard_map(
        functools.partial(on_device, mesh.shape["dp"], mesh.shape["tensor"]),
        mesh=mesh,
        in_specs=(rows, rows, P("dp"), rows, rows) + params,
        out_specs=(rows, rows) + params + (P(),),
        check_vma=False,
    )
```

```python
import functools

import jax
import jax.numpy as jnp
from jax import lax
from jax.experimental import pallas as pl
from jax.experimental.pallas import tpu as pltpu
from jax.sharding import PartitionSpec as P

HEAD = 64
BF = jnp.bfloat16
F32 = jnp.float32
NN = (((1,), (0,)), ((), ()))
NT = (((1,), (1,)), ((), ()))
TN = (((0,), (0,)), ((), ()))
VMEM_LIMIT = 58 << 20


def mm(a, b, dims):
    return lax.dot_general(a, b, dims, preferred_element_type=F32)


def full(*shape):
    return pl.BlockSpec(shape, lambda i: (0,) * len(shape))


def per(*shape):
    return pl.BlockSpec((1,) + shape, lambda i: (i,) + (0,) * len(shape))


ANY = pl.BlockSpec(memory_space=pl.ANY)
SCALARS = pl.BlockSpec(memory_space=pltpu.SMEM)


def out(shape, dtype=F32):
    return jax.ShapeDtypeStruct(shape, dtype)


def call(kernel, grid, in_specs, out_specs, out_shape, scratch=(), heavy=True):
    return pl.pallas_call(
        kernel,
        grid=(grid,),
        in_specs=in_specs,
        out_specs=out_specs,
        out_shape=out_shape,
        scratch_shapes=list(scratch),
        compiler_params=pltpu.CompilerParams(vmem_limit_bytes=VMEM_LIMIT),
        cost_estimate=pl.CostEstimate(
            flops=500 << 30 if heavy else 0, bytes_accessed=1000, transcendentals=0
        ),
    )


class Pieces:
    def __init__(self, arrays, plan, where, blocks, rows, lanes):
        self.arrays, self.plan, self.where = arrays, plan, where
        self.blocks, self.rows, self.lanes = blocks, rows, lanes

    def scratch(self):
        if self.plan is None:
            shape, count = (self.blocks, self.rows, self.lanes), 1
        else:
            shape, count = (self.blocks, 4, 2, self.rows // 8, self.lanes), 4
        return [pltpu.VMEM(shape, BF), pltpu.SemaphoreType.DMA((self.blocks, count))]

    def start(self, refs, where_ref, buffer, sems, ps=None):
        for p in range(self.blocks) if ps is None else ps:
            if self.plan is None:
                pltpu.make_async_copy(refs[0].at[p], buffer.at[p], sems.at[p, 0]).start()
                continue
            for number, (array, y_rel, pair_rel) in enumerate(self.plan[p]):
                pair = (where_ref[0] // 2) ^ pair_rel
                target = buffer.at[p, pl.ds(pair * 2, 2), where_ref[1] ^ y_rel]
                pltpu.make_async_copy(refs[array], target, sems.at[p, number]).start()

    def wait(self, refs, p, buffer, sems):
        if self.plan is None:
            pltpu.make_async_copy(refs[0].at[0], buffer.at[p], sems.at[p, 0]).wait()
            return
        for number in range(4):
            target = buffer.at[p, pl.ds(0, 2), 0]
            pltpu.make_async_copy(refs[0], target, sems.at[p, number]).wait()

    def read(self, buffer, p, first, last):
        if self.plan is None:
            return buffer[p, :, first:last]
        return buffer[p, :, :, :, first:last].reshape(self.rows, last - first)


def tie(array, deps):
    return lax.optimization_barrier((array, tuple(deps)))[0] if deps else array


class GenericComm:
    small_inside = False

    def __init__(self, dp, tensor):
        self.dp, self.tensor = dp, tensor
        self.where = jnp.zeros((2,), jnp.int32)

    def gather(self, shard):
        return GenericGather(self, shard)

    def gather_small(self, vector):
        return lax.all_gather(lax.all_gather(vector, "dp", axis=0), "tensor", axis=0)

    def scatter_small(self, vectors):
        own = lax.psum_scatter(vectors, "tensor", scatter_dimension=0)
        return lax.psum_scatter(own, "dp", scatter_dimension=0)

    def total(self, values):
        return lax.psum(values, ("dp", "tensor"))

    def reduction(self, lefts, halves=False):
        return GenericReduction(self, lefts)

    def block_sets(self):
        return [range(self.tensor)]


class GenericGather:
    def __init__(self, comm, shard):
        self.comm, self.shard = comm, shard

    def z(self, deps):
        return []

    def xy(self, deps):
        return []

    def diagonal(self, deps):
        pass

    def core(self):
        rows = lax.all_gather(self.shard, "dp", axis=0, tiled=True)
        blocks = lax.all_gather(rows, "tensor", axis=0)
        return Pieces([blocks], None, self.comm.where, *blocks.shape)


class GenericReduction:
    def __init__(self, comm, lefts):
        self.comm, self.lefts = comm, lefts

    def core(self, rights, extra=None):
        self.rights = rights
        return []

    def split(self, rights, extra=None):
        return []

    def neighbour(self):
        return []

    def last(self):
        stacked = grads(list(zip(self.lefts, self.rights)), range(self.comm.tensor))
        own = lax.psum_scatter(stacked, "tensor", scatter_dimension=0)
        return [lax.psum_scatter(own, "dp", scatter_dimension=0, tiled=True).astype(F32)]


class GridComm:
    small_inside = True

    def __init__(self):
        self.z = lax.axis_index("dp") // 2
        self.y = lax.axis_index("dp") % 2
        self.where = jnp.stack([self.z, self.y]).astype(jnp.int32)

    @staticmethod
    def send(array, dp_xor, tensor_xor):
        pairs = [
            (d * 4 + t, (d ^ dp_xor) * 4 + (t ^ tensor_xor)) for d in range(8) for t in range(4)
        ]
        return lax.ppermute(array, ("dp", "tensor"), pairs)

    def send_core(self, array):
        return self.send(array, 0, 1)

    def send_x(self, array):
        return self.send(array, 0, 2)

    def send_y(self, array):
        return self.send(array, 1, 0)

    def send_z(self, array, k):
        return self.send(array, 2 * k, 0)

    def gather(self, shard):
        return GridGather(self, shard)

    def total(self, values):
        values = values + self.send_core(values)
        values = values + self.send_x(values)
        values = values + self.send_y(values)
        values = values + self.send_z(values, 1)
        return values + self.send_z(values, 2)

    def reduction(self, lefts, halves=False):
        return (HalvesReduction if halves else Reduction)(self, lefts)

    def block_sets(self):
        return [(1, 3), (0, 2)]


class GridGather:
    def __init__(self, comm, shard):
        self.comm, self.shard = comm, shard

    def z(self, deps):
        shard = tie(self.shard, deps)
        self.by_z = [shard] + [self.comm.send_z(shard, k) for k in (1, 2, 3)]
        return self.by_z[1:]

    def xy(self, deps):
        even = self.comm.z % 2 == 0
        by_z = self.by_z
        low = jnp.where(even, jnp.stack(by_z[:2]), jnp.stack(by_z[1::-1]))
        high = jnp.where(even, jnp.stack(by_z[2:]), jnp.stack(by_z[:1:-1]))
        low, high = tie(low, deps), tie(high, deps)
        x_low, y_low = self.comm.send_x(low), self.comm.send_y(low)
        x_high, y_high = self.comm.send_x(high), self.comm.send_y(high)
        self.near, self.far = [low, high, y_low, y_high], [x_low, x_high]
        return [x_high, y_high]

    def diagonal(self, deps):
        y_low, x_high = tie(self.near[2], deps), tie(self.far[1], deps)
        self.far += [self.comm.send_x(y_low), self.comm.send_y(x_high)]

    def core(self):
        near_core = [self.comm.send_core(a) for a in self.near]
        far_core = [self.comm.send_core(a) for a in self.far]
        arrays = self.near + near_core + self.far + far_core
        plan = [[(4 * p + c, c // 2, c % 2) for c in range(4)] for p in range(4)]
        rows, lanes = self.shard.shape
        return Pieces(arrays, plan, self.comm.where, 4, 8 * rows, lanes)


class Reduction:
    def __init__(self, comm, lefts):
        self.comm, self.lefts = comm, lefts

    def core(self, rights, extra=None):
        odd = grads(list(zip(self.lefts, rights)), (1, 3), extra)
        self.core_got = self.comm.send_core(odd)
        return [odd]

    def split(self, rights):
        terms = list(zip(self.lefts, rights))
        to_y, self.keep = grads_split_y(terms, self.core_got, self.comm.where)
        self.y_got = self.comm.send_y(to_y)
        return [self.keep]

    def neighbour(self):
        to_x = add(self.keep[1], self.y_got[1])
        self.x_got = self.comm.send_x(to_x)
        return [to_x]

    def last(self):
        addends = [(self.keep, 0), (self.y_got, 0), (self.x_got[None], 0)]
        parts = combine([addends, addends], [(0, 1), (2, 3)], self.comm.where)
        return [parts[0]] + [self.comm.send_z(parts[k], k) for k in (1, 2, 3)]


class HalvesReduction:
    def __init__(self, comm, lefts):
        self.comm, self.lefts = comm, lefts

    def core(self, rights, extra=None):
        odd = grads(list(zip(self.lefts, rights)), (1, 3), extra)
        self.core_got = self.comm.send_core(odd)
        return [odd]

    def split(self, rights, extra=None):
        terms = list(zip(self.lefts, rights))
        split = grads_split(terms, self.core_got, self.comm.where, extra)
        x_first, y_first, self.x_second, self.y_second, self.mine = split
        self.x_got, self.y_got = self.comm.send_x(x_first), self.comm.send_y(y_first)
        return [self.mine]

    def neighbour(self):
        x_second = add(self.x_second, self.y_got[:2])
        y_second = add(self.y_second, self.x_got[:2])
        self.x_got2, self.y_got2 = self.comm.send_x(x_second), self.comm.send_y(y_second)
        return [x_second, y_second]

    def last(self):
        mine = self.mine[None]
        low = [(mine, 0), (self.x_got[None], 2), (self.y_got2[None], 0)]
        high = [(mine, 2), (self.y_got[None], 2), (self.x_got2[None], 0)]
        parts = combine([low, high], None, self.comm.where)
        return [parts[0]] + [self.comm.send_z(parts[k], k) for k in (1, 2, 3)]


def add(*arrays):
    total = arrays[0].astype(F32)
    for array in arrays[1:]:
        total = total + array.astype(F32)
    return total.astype(BF)


def block_of(right, p):
    if not isinstance(right, list):
        return right, p
    for ps, array in right:
        if p in ps:
            return array, list(ps).index(p)
    raise KeyError(p)


def grads(terms, ps, extra=None):
    ps = list(ps)
    d, n = terms[0][0].shape
    firsts = [block_of(right, ps[0]) for _, right in terms]
    steps = [block_of(right, ps[1])[1] - first for (_, right), (_, first) in zip(terms, firsts)]
    lanes = [array.shape[2] for array, _ in firsts]

    def kernel(*refs):
        at = 0
        for number, wide in enumerate(lanes):
            left, right = refs[2 * number], refs[2 * number + 1]
            refs[-1][0, :, at : at + wide] = mm(left[...], right[0], NN).astype(BF)
            at += wide
        if extra is not None:
            refs[-1][0, :, at:] = jnp.zeros((d, 128), BF)
            for c in range(8):
                refs[-1][0, c * (d // 8) : c * (d // 8) + 16, at:] = refs[-2][0, c]

    specs, args = [], []
    for (left, _), (array, first), step, wide in zip(terms, firsts, steps, lanes):
        specs.append(full(d, n))
        specs.append(
            pl.BlockSpec((1, n, wide), lambda i, first=first, step=step: (first + step * i, 0, 0))
        )
        args += [left, array]
    wide = sum(lanes)
    if extra is not None:
        specs.append(per(8, 16, 128))
        args.append(extra)
        wide += 128
    return call(
        kernel, len(ps), specs, per(d, wide), out((len(ps), d, wide), BF),
    )(*args)


def split_call(terms, got, where, write, outs, extra=None):
    d, n = terms[0][0].shape
    rows = d // 8
    count = len(terms)
    evens = [[block_of(right, p) for p in (0, 2)] for _, right in terms]
    lanes = [pair[0][0].shape[2] for pair in evens]

    def kernel(where_ref, *refs):
        got_ref = refs[3 * count]
        y = where_ref[1]

        def part(p, y_at):
            at = 0
            columns = []
            for number, width in enumerate(lanes):
                left, right = refs[3 * number], refs[3 * number + 1 + p // 2]
                lhs = left[:, y_at].reshape(4 * rows, n)
                value = mm(lhs, right[0], NN).reshape(4, rows, width)
                value = value + got_ref[p // 2, :, y_at, :, at : at + width].astype(F32)
                columns.append((at, width, value.astype(BF)))
                at += width
            if extra is not None:
                value = got_ref[p // 2, :, y_at, :, at:].astype(F32)
                top = value[:, 0:16] + refs[3 * count + 1][p // 2, :, y_at].astype(F32)
                value = jnp.concatenate([top, value[:, 16:]], axis=1)
                columns.append((at, 128, value.astype(BF)))
            return columns

        write(part, y, refs[3 * count + 1 + (extra is not None) :])

    specs, args = [SCALARS], [where]
    for (left, _), pair, width in zip(terms, evens, lanes):
        specs.append(full(4, 2, rows, n))
        args.append(left.reshape(4, 2, rows, n))
        for array, index in pair:
            specs.append(pl.BlockSpec((1, n, width), lambda i, index=index: (index, 0, 0)))
            args.append(array)
    wide = got.shape[2]
    specs.append(full(2, 4, 2, rows, wide))
    args.append(got.reshape(2, 4, 2, rows, wide))
    if extra is not None:
        specs.append(full(2, 4, 2, 16, 128))
        args.append(extra.reshape(2, 4, 2, 16, 128))
    shapes = [shape + (rows, wide) for shape in outs]
    return call(
        kernel, 1, specs, [full(*shape) for shape in shapes], [out(shape, BF) for shape in shapes],
    )(*args)


def grads_split_y(terms, got, where):
    def write(part, y, refs):
        for number, y_at in enumerate((1 - y, y)):
            for p in (2, 0):
                for at, width, value in part(p, y_at):
                    refs[number][p // 2, :, :, at : at + width] = value

    return split_call(terms, got, where, write, [(2, 4), (2, 4)])


def grads_split(terms, got, where, extra=None):
    def write(part, y, refs):
        x_first, y_first, x_second, y_second, mine = refs
        for at, width, value in part(2, 1 - y):
            x_first[0:2, :, at : at + width] = value[0:2]
            y_first[0:2, :, at : at + width] = value[2:4]
        for at, width, value in part(2, y):
            x_first[2:4, :, at : at + width] = value[0:2]
            x_second[:, :, at : at + width] = value[2:4]
        for at, width, value in part(0, 1 - y):
            y_first[2:4, :, at : at + width] = value[2:4]
            y_second[:, :, at : at + width] = value[0:2]
        for at, width, value in part(0, y):
            mine[:, :, at : at + width] = value

    return split_call(terms, got, where, write, [(4,), (4,), (2,), (2,), (4,)], extra)


def pack_vectors(ps, qkv_sum, wide_grad, sums_one, sums_two, sizes):
    head_own, wide_own, gain_own, dp_size = sizes
    width = qkv_sum.shape[2] // 3
    stride = ps[1] - ps[0]

    def kernel(qkv_ref, wide_ref, one_ref, two_ref, out_ref):
        out_ref[...] = jnp.zeros_like(out_ref)
        rows = [
            (qkv_ref[0, :, 0:width], head_own), (qkv_ref[0, :, 2 * width :], head_own),
            (wide_ref[0], wide_own), (one_ref[0:1], gain_own), (two_ref[0:1], gain_own),
            (one_ref[2:3], gain_own), (one_ref[1:2], gain_own), (two_ref[2:3], gain_own),
            (two_ref[1:2], gain_own),
        ]
        for c in range(dp_size):
            for number, (row, own) in enumerate(rows):
                out_ref[0, c, number : number + 1, 0:own] = row[:, c * own : (c + 1) * own]

    return call(
        kernel, 2,
        [
            per(1, 3 * width), pl.BlockSpec((1, 1, wide_own * dp_size), lambda i: (ps[0] + stride * i, 0, 0)),
            full(*sums_one.shape), full(*sums_two.shape),
        ],
        per(dp_size, 16, 128), out((2, dp_size, 16, 128)), heavy=False,
    )(qkv_sum, wide_grad, sums_one, sums_two).astype(BF)


def combine(halves, rows_of, where):
    arrays = []
    for array in [array for half in halves for array, _ in half]:
        if not any(array is other for other in arrays):
            arrays.append(array)
    index = lambda array: [array is other for other in arrays].index(True)
    plans = [
        [(index(array), rows_of[h][0] if rows_of else first) for array, first in half]
        for h, half in enumerate(halves)
    ]
    chunk = arrays[0].shape[2:]

    def kernel(where_ref, *refs):
        o0, o1, o2, o3, total = refs[len(arrays) :]
        for h, plan in enumerate(plans):
            for j in range(2):
                number, first = plan[0]
                value = refs[number][0, first + j].astype(F32)
                for number, first in plan[1:]:
                    value = value + refs[number][0, first + j].astype(F32)
                total[2 * h + j] = value
        z = where_ref[0]
        o0[...] = total[z]
        o1[...] = total[z ^ 1].astype(BF)
        o2[...] = total[z ^ 2].astype(BF)
        o3[...] = total[z ^ 3].astype(BF)

    return call(
        kernel, 1,
        [SCALARS] + [full(1, *a.shape[1:]) for a in arrays],
        [full(*chunk)] * 4,
        [out(chunk), out(chunk, BF), out(chunk, BF), out(chunk, BF)],
        [pltpu.VMEM((4,) + chunk, F32)],
        heavy=False,
    )(where, *arrays)


def norm(summed):
    center = summed - jnp.mean(summed, axis=-1, keepdims=True)
    spread = jnp.mean(center * center, axis=-1, keepdims=True)
    scaled = lax.rsqrt(spread + 1e-05)
    return (center * scaled, scaled)


def norm_back(upstream, normal, scaled):
    inner_sum = (
        upstream
        - jnp.mean(upstream, axis=-1, keepdims=True)
        - normal * jnp.mean(upstream * normal, axis=-1, keepdims=True)
    )
    return scaled * inner_sum


G1, G2, BO, B1, C2, B2 = range(6)


def attn_fwd(pieces, width, small, tok, groups, key_open):
    n, d = tok.shape
    blocks = pieces.blocks
    heads = width // HEAD
    count = len(pieces.arrays)
    (head_own, wide_own, gain_own, dp_size), given = small
    units = wide_own * dp_size

    def kernel(where_ref, tok_ref, gq_ref, gk_ref, open_ref, *refs):
        w_refs, refs = refs[:count], refs[count:]
        if given is not None:
            bias_in, rows_in, wide_in = refs[:3]
            refs = refs[3:]
        qkv_ref, ctx_ref, e_ref, inv_ref, n1_ref, rstd_ref, low_ref, low_t_ref, tok_t_ref = refs[:9]
        rows_ref, wide_ref, att_ref, mask_ref, w_ref, sems = refs[9:]
        step = pl.program_id(0)

        @pl.when(step == 0)
        def _():
            pieces.start(w_refs, where_ref, w_ref, sems)
            seen = (open_ref[...] == 1) | (gq_ref[...] == gk_ref[...])
            mask_ref[...] = jnp.where(seen, 0.0, -1e30)
            att_ref[...] = jnp.zeros_like(att_ref)
            tok_t_ref[...] = tok_ref[...].T

        pieces.wait(w_refs, step, w_ref, sems)
        if given is None:
            first = 4 * width
            vectors = [
                w_ref[step, c // 2, c % 2, 0:16, first : first + 128].astype(F32)
                for c in range(dp_size)
            ]

            def line(row, used):
                return jnp.concatenate([v[row : row + 1, :used] for v in vectors], axis=1)

            bias_q, bias_v = line(0, head_own), line(1, head_own)
            wide_ref[0] = line(2, wide_own)

            @pl.when(step == 0)
            def _():
                for row in range(6):
                    rows_ref[row : row + 1] = line(3 + row, gain_own)

        else:
            bias_q, bias_v = bias_in[0, 0:1], bias_in[0, 1:2]
            wide_ref[0] = wide_in[0]
            rows_ref[0:6] = rows_in[...]

        qkv = mm(tok_ref[...], pieces.read(w_ref, step, 0, 3 * width), NN)
        lane = lax.broadcasted_iota(jnp.int32, (n, 128), 1)
        q_all = (qkv[:, :width] + bias_q).astype(BF)
        k_all = qkv[:, width : 2 * width].astype(BF)
        v_all = (qkv[:, 2 * width :] + bias_v).astype(BF)
        qkv_ref[0] = jnp.concatenate([q_all, k_all, v_all], axis=1)
        contexts = []
        inv_all = jnp.zeros((n, 128), F32)
        for h in range(heads):
            q = q_all[:, h * HEAD : (h + 1) * HEAD] * jnp.asarray(HEAD**-0.5, BF)
            k = k_all[:, h * HEAD : (h + 1) * HEAD]
            v = v_all[:, h * HEAD : (h + 1) * HEAD]
            s = mm(q, k, NT) + mask_ref[...]
            e = jnp.exp(s - jnp.max(s, axis=-1, keepdims=True)).astype(BF)
            e_ref[0, h] = e
            v_one = jnp.concatenate([v, jnp.ones_like(v)], axis=1)
            r = mm(e, v_one, NN)
            inv = 1.0 / r[:, HEAD : HEAD + 1]
            contexts.append((r[:, :HEAD] * inv).astype(BF))
            inv_all = jnp.where(lane == h, inv, inv_all)
        ctx = jnp.concatenate(contexts, axis=1)
        ctx_ref[0] = ctx
        inv_ref[0] = inv_all
        att_ref[...] += mm(ctx, pieces.read(w_ref, step, 3 * width, 4 * width), NT)

        @pl.when(step == blocks - 1)
        def _():
            summed = tok_ref[...].astype(F32) + (att_ref[...] + rows_ref[BO : BO + 1])
            normal, scaled = norm(summed)
            n1_ref[...] = normal
            rstd_ref[...] = scaled
            normed = normal * rows_ref[G1 : G1 + 1] + rows_ref[B1 : B1 + 1]
            low = normed.astype(BF)
            low_ref[...] = low
            low_t_ref[...] = low.T

    specs = [SCALARS, full(n, d), full(n, 1), full(1, n), full(1, n)] + [ANY] * count
    args = [pieces.where, tok, groups.reshape(n, 1), groups.reshape(1, n), key_open.reshape(1, n)]
    args += pieces.arrays
    if given is not None:
        biases = given[:, :, 0:2, :head_own].transpose(0, 2, 1, 3).reshape(blocks, 2, width)
        wide_low = given[:, :, 2, :wide_own].reshape(blocks, 1, units)
        specs += [per(2, width), full(6, d), per(1, units)]
        args += [
            biases, given[0, :, 3:9, :gain_own].transpose(1, 0, 2).reshape(6, d), wide_low,
        ]
    return call(
        kernel, blocks, specs,
        [
            per(n, 3 * width), per(n, width), per(heads, n, n), per(n, 128),
            full(n, d), full(n, 1), full(n, d), full(d, n), full(d, n), full(8, d), per(1, units),
        ],
        [
            out((blocks, n, 3 * width), BF), out((blocks, n, width), BF),
            out((blocks, heads, n, n), BF), out((blocks, n, 128)),
            out((n, d)), out((n, 1)), out((n, d), BF), out((d, n), BF), out((d, n), BF),
            out((8, d)), out((blocks, 1, units)),
        ],
        [pltpu.VMEM((n, d), F32), pltpu.VMEM((n, n), F32)] + pieces.scratch(),
    )(*args)


def ffn_up(pieces, low, wide_bias):
    n, d = low.shape
    blocks, units, count = pieces.blocks, pieces.lanes, len(pieces.arrays)

    def kernel(where_ref, low_ref, bias_ref, *refs):
        w_refs, (act_ref, slope_ref, w_ref, sems) = refs[:count], refs[count:]
        step = pl.program_id(0)

        @pl.when(step == 0)
        def _():
            pieces.start(w_refs, where_ref, w_ref, sems)

        pieces.wait(w_refs, step, w_ref, sems)
        h = mm(low_ref[...], pieces.read(w_ref, step, 0, units), NN) + bias_ref[0]
        cdf = 0.5 * (1.0 + lax.erf(h * (0.5**0.5)))
        act_ref[0] = (h * cdf).astype(BF)
        density = jnp.exp(h * h * -0.5) * 0.3989422804014327
        slope_ref[0] = (cdf + h * density).astype(BF)

    return call(
        kernel, blocks,
        [SCALARS, full(n, d), per(1, units)] + [ANY] * count,
        [per(n, units), per(n, units)],
        [out((blocks, n, units), BF), out((blocks, n, units), BF)],
        pieces.scratch(),
    )(pieces.where, low, wide_bias, *pieces.arrays)


def ffn_down(pieces, act, n1, cot, rows):
    n, d = n1.shape
    blocks, units, count = pieces.blocks, pieces.lanes, len(pieces.arrays)

    def kernel(where_ref, act_ref, n1_ref, cot_ref, rows_ref, *refs):
        w_refs, refs = refs[:count], refs[count:]
        y_ref, ds_ref, df_ref, df_t_ref, sum_ref, acc_ref, w_ref, sems = refs
        step = pl.program_id(0)

        @pl.when(step == 0)
        def _():
            pieces.start(w_refs, where_ref, w_ref, sems)
            normed = n1_ref[...] * rows_ref[G1 : G1 + 1] + rows_ref[B1 : B1 + 1]
            acc_ref[...] = normed + rows_ref[C2 : C2 + 1]

        pieces.wait(w_refs, step, w_ref, sems)
        acc_ref[...] += mm(act_ref[0], pieces.read(w_ref, step, 0, units), NT)

        @pl.when(step == blocks - 1)
        def _():
            normal, scaled = norm(acc_ref[...])
            gain = rows_ref[G2 : G2 + 1]
            y_ref[...] = (normal * gain + rows_ref[B2 : B2 + 1]).astype(BF)
            upstream = cot_ref[...].astype(F32)
            ds = norm_back(upstream * gain, normal, scaled)
            ds_ref[...] = ds
            df = ds.astype(BF)
            df_ref[...] = df
            df_t_ref[...] = df.T
            sum_ref[...] = jnp.zeros_like(sum_ref)
            sum_ref[0:1] = jnp.sum(upstream * normal, axis=0, keepdims=True)
            sum_ref[1:2] = jnp.sum(upstream, axis=0, keepdims=True)
            sum_ref[2:3] = jnp.sum(ds, axis=0, keepdims=True)

    return call(
        kernel, blocks,
        [SCALARS, per(n, units), full(n, d), full(n, d), full(*rows.shape)] + [ANY] * count,
        [full(n, d), full(n, d), full(n, d), full(d, n), full(8, d)],
        [out((n, d), BF), out((n, d)), out((n, d), BF), out((d, n), BF), out((8, d))],
        [pltpu.VMEM((n, d), F32)] + pieces.scratch(),
    )(pieces.where, act, n1, cot, rows, *pieces.arrays)


def ffn_bwd(up, down, df, slope, ds2, n1, rstd, rows):
    n, d = n1.shape
    blocks, units = up.blocks, up.lanes
    up_count, down_count = len(up.arrays), len(down.arrays)

    def kernel(where_ref, df_ref, slope_ref, ds2_ref, n1_ref, rstd_ref, rows_ref, *refs):
        up_refs, down_refs = refs[:up_count], refs[up_count : up_count + down_count]
        refs = refs[up_count + down_count :]
        dh_ref, dc_ref, ds_ref, da_ref, da_t_ref, sum_ref = refs[:6]
        acc_ref, wu_ref, sems_u, wd_ref, sems_d = refs[6:]
        step = pl.program_id(0)

        @pl.when(step == 0)
        def _():
            down.start(down_refs, where_ref, wd_ref, sems_d)
            up.start(up_refs, where_ref, wu_ref, sems_u)
            acc_ref[...] = ds2_ref[...]

        down.wait(down_refs, step, wd_ref, sems_d)
        up.wait(up_refs, step, wu_ref, sems_u)
        dact = mm(df_ref[...], down.read(wd_ref, step, 0, units), NN)
        dh = (dact * slope_ref[0].astype(F32)).astype(BF)
        dh_ref[0] = dh
        dc_ref[0] = jnp.sum(dh.astype(F32), axis=0, keepdims=True)
        acc_ref[...] += mm(dh, up.read(wu_ref, step, 0, units), NT)

        @pl.when(step == blocks - 1)
        def _():
            dnormed = acc_ref[...]
            normal = n1_ref[...]
            ds = norm_back(dnormed * rows_ref[G1 : G1 + 1], normal, rstd_ref[...])
            ds_ref[...] = ds
            da = ds.astype(BF)
            da_ref[...] = da
            da_t_ref[...] = da.T
            sum_ref[...] = jnp.zeros_like(sum_ref)
            sum_ref[0:1] = jnp.sum(dnormed * normal, axis=0, keepdims=True)
            sum_ref[1:2] = jnp.sum(dnormed, axis=0, keepdims=True)
            sum_ref[2:3] = jnp.sum(ds, axis=0, keepdims=True)

    return call(
        kernel, blocks,
        [SCALARS, full(n, d), per(n, units), full(n, d), full(n, d), full(n, 1), full(*rows.shape)]
        + [ANY] * (up_count + down_count),
        [per(n, units), per(1, units), full(n, d), full(n, d), full(d, n), full(8, d)],
        [
            out((blocks, n, units), BF), out((blocks, 1, units)), out((n, d)),
            out((n, d), BF), out((d, n), BF), out((8, d)),
        ],
        [pltpu.VMEM((n, d), F32)] + up.scratch() + down.scratch(),
    )(up.where, df, slope, ds2, n1, rstd, rows, *up.arrays, *down.arrays)


def attn_bwd(pieces, width, ps, da, qkv, ctx, e, inv, back, last):
    n, d = back.shape
    ps = list(ps)
    count = len(pieces.arrays)
    heads = width // HEAD
    stride = ps[1] - ps[0]
    at = lambda i: ps[0] + stride * i

    def kernel(where_ref, da_ref, qkv_ref, ctx_ref, e_ref, inv_ref, back_ref, *refs):
        w_refs, (dqkv_ref, sum_ref, tg_ref, acc_ref, w_ref, sems) = refs[:count], refs[count:]
        step = pl.program_id(0)

        @pl.when(step == 0)
        def _():
            pieces.start(w_refs, where_ref, w_ref, sems, ps)
            acc_ref[...] = back_ref[...]

        pieces.wait(w_refs, at(step), w_ref, sems)
        dctx = mm(da_ref[...], pieces.read(w_ref, at(step), 3 * width, 4 * width), NN)
        dctx = dctx.astype(BF).astype(F32)
        scale = HEAD**-0.5
        dqs, dks, dvs = [], [], []
        for h in range(heads):
            q = qkv_ref[0, :, h * HEAD : (h + 1) * HEAD]
            k = qkv_ref[0, :, width + h * HEAD : width + (h + 1) * HEAD]
            v = qkv_ref[0, :, 2 * width + h * HEAD : 2 * width + (h + 1) * HEAD]
            e = e_ref[0, h]
            do = dctx[:, h * HEAD : (h + 1) * HEAD] * inv_ref[0, :, h : h + 1]
            ctx = ctx_ref[0, :, h * HEAD : (h + 1) * HEAD].astype(F32)
            delta = jnp.sum(do * ctx, axis=-1, keepdims=True)
            do_low = do.astype(BF)
            dp = mm(do_low, v, NT)
            ds = (e.astype(F32) * (dp - delta)).astype(BF)
            dvs.append(mm(e, do_low, TN))
            dqs.append(mm(ds, k, NN) * scale)
            dks.append(mm(ds, q, TN) * scale)
        dqkv = jnp.concatenate(dqs + dks + dvs, axis=1).astype(BF)
        dqkv_ref[0] = dqkv
        sum_ref[0] = jnp.sum(dqkv.astype(F32), axis=0, keepdims=True)
        acc_ref[...] += mm(dqkv, pieces.read(w_ref, at(step), 0, 3 * width), NT)

        @pl.when(step == len(ps) - 1)
        def _():
            tg_ref[...] = acc_ref[...].astype(tg_ref.dtype)

    def of(*shape):
        return pl.BlockSpec((1,) + shape, lambda i: (at(i),) + (0,) * len(shape))

    return call(
        kernel, len(ps),
        [SCALARS, full(n, d), of(n, 3 * width), of(n, width), of(heads, n, n), of(n, 128), full(n, d)]
        + [ANY] * count,
        [per(n, 3 * width), per(1, 3 * width), full(n, d)],
        [
            out((len(ps), n, 3 * width), BF), out((len(ps), 1, 3 * width)),
            out((n, d), BF if last else F32),
        ],
        [pltpu.VMEM((n, d), F32)] + pieces.scratch(),
    )(pieces.where, da, qkv, ctx, e, inv, back, *pieces.arrays)


def lamb(gradient, master, first, second):
    first_new = 0.5 * first + 0.5 * gradient
    second_new = 0.5 * second + 0.5 * gradient * gradient
    update = first_new / (jnp.sqrt(second_new) + 1e-06) + 0.01 * master
    return first_new, second_new, update


def whole_sum(array):
    return jnp.sum(jnp.sum(array * array, axis=1, keepdims=True), axis=0, keepdims=True)


def chunk_sum(refs, lanes):
    total = refs[0][:, lanes[0] : lanes[1]]
    for ref in refs[1:]:
        total = total + ref[:, lanes[0] : lanes[1]].astype(F32)
    return total


def lamb_matrix(parts, master, first, second):
    count = len(parts)

    def kernel(*refs):
        m_ref, f_ref, s_ref, fn_ref, sn_ref, u_ref, sum_ref = refs[count:]
        gradient = chunk_sum(refs[:count], (0, master.shape[1]))
        fn_ref[...], sn_ref[...], update = lamb(gradient, m_ref[...], f_ref[...], s_ref[...])
        u_ref[...] = update
        sum_ref[0:1] = jnp.broadcast_to(whole_sum(m_ref[...]), (1, 128))
        sum_ref[1:2] = jnp.broadcast_to(whole_sum(update), (1, 128))

    shape = master.shape
    return call(
        kernel, 1,
        [full(*a.shape) for a in parts] + [full(*shape)] * 3,
        [full(*shape)] * 3 + [full(8, 128)],
        [out(shape)] * 3 + [out((8, 128))],
        heavy=False,
    )(*parts, master, first, second)


def lamb_last(parts, attn, mix, small_grad, small, early, share):
    count = len(parts)
    width = attn[0].shape[2]
    shapes = [group[0].shape for group in small]

    def kernel(*refs):
        part_refs, refs = refs[:count], refs[count:]
        m_ref, f_ref, s_ref, mm_ref, mf_ref, ms_ref = refs[:6]
        small_refs, early_refs, refs = refs[6:18], refs[18:20], refs[20:]
        if small_grad is not None:
            small_total, refs = refs[0][...], refs[1:]
        else:
            small_total = part_refs[0][0:16, 4 * width : 4 * width + 128]
            for ref in part_refs[1:]:
                small_total = small_total + ref[0:16, 4 * width : 4 * width + 128].astype(F32)
        fn_ref, sn_ref, u_ref, mfn_ref, msn_ref, mu_ref = refs[:6]
        small_out, su_ref, sum_ref, pack = refs[6:14], refs[14], refs[15], refs[16]
        row = lax.broadcasted_iota(jnp.int32, (8, 128), 0)
        lane = lax.broadcasted_iota(jnp.int32, (8, 128), 1)
        sums = jnp.zeros((8, 128), F32)

        def put(sums, index, weight_sq, update_sq):
            sums = jnp.where((row == 0) & (lane == index), weight_sq, sums)
            return jnp.where((row == 1) & (lane == index), update_sq, sums)

        for k in range(3):
            gradient = chunk_sum(part_refs, (k * width, (k + 1) * width))
            fn, sn, update = lamb(gradient, m_ref[k], f_ref[k], s_ref[k])
            fn_ref[k], sn_ref[k], u_ref[k] = fn, sn, update
            sums = put(sums, k, whole_sum(m_ref[k]), whole_sum(update))
        gradient = chunk_sum(part_refs, (3 * width, 4 * width)).T
        fn, sn, update = lamb(gradient, mm_ref[...], mf_ref[...], ms_ref[...])
        mfn_ref[...], msn_ref[...], mu_ref[...] = fn, sn, update
        sums = put(sums, 3, whole_sum(mm_ref[...]), whole_sum(update))
        for index, ref in zip((4, 5), early_refs):
            sums = put(sums, index, ref[0:1, 0:1], ref[1:2, 0:1])
        pack[...] = jnp.zeros_like(pack)
        at = 0
        for group in range(4):
            count_rows, lanes_used = shapes[group]
            for which in range(3):
                pack[which, at : at + count_rows, 0:lanes_used] = small_refs[3 * group + which][...]
            at += count_rows
        fn, sn, update = lamb(small_total, pack[0], pack[1], pack[2])
        su_ref[...] = update
        at = 0
        for group in range(4):
            count_rows, lanes_used = shapes[group]
            small_out[2 * group][...] = fn[at : at + count_rows, 0:lanes_used]
            small_out[2 * group + 1][...] = sn[at : at + count_rows, 0:lanes_used]
            at += count_rows
        weight_rows = jnp.sum(pack[0] * pack[0], axis=1, keepdims=True)
        update_rows = jnp.sum(update * update, axis=1, keepdims=True)
        for index in range(9):
            part = 1.0 if index < 3 else share
            sums = put(
                sums, 6 + index, weight_rows[index : index + 1] * part, update_rows[index : index + 1] * part
            )
        sum_ref[...] = sums

    args = list(parts) + list(attn) + list(mix)
    args += [array for group in small for array in group] + list(early)
    if small_grad is not None:
        args.append(small_grad)
    outs = [out(attn[0].shape)] * 3 + [out(mix[0].shape)] * 3
    outs += [out(s) for s in shapes for _ in range(2)]
    outs += [out((16, 128)), out((8, 128))]
    return call(
        kernel, 1, [full(*a.shape) for a in args], [full(*o.shape) for o in outs], outs,
        [pltpu.VMEM((3, 16, 128), F32)], heavy=False,
    )(*args)


def finish(sums, matrices, updates, small, small_update):
    shapes = [a.shape for a in small]

    def kernel(*refs):
        sum_ref, refs = refs[0], refs[1:]
        m_refs, u_refs, v_refs, vu_ref = refs[:4], refs[4:8], refs[8:12], refs[12]
        m_outs, v_outs, norm_ref = refs[13:17], refs[17:21], refs[21]
        norms = jnp.sqrt(sum_ref[...])
        trust = 0.5 * (norms[0:1] / (norms[1:2] + 1e-06))
        norm_ref[...] = norms[0:2, 0:15]
        for k in range(3):
            m_outs[0][k] = m_refs[0][k] - trust[:, k : k + 1] * u_refs[0][k]
        for number in range(1, 4):
            at = 2 + number
            m_outs[number][...] = m_refs[number][...] - trust[:, at : at + 1] * u_refs[number][...]
        at = 0
        for group in range(4):
            count_rows, lanes_used = shapes[group]
            for r in range(count_rows):
                factor = trust[:, 6 + at : 7 + at]
                update = vu_ref[at : at + 1, 0:lanes_used]
                v_outs[group][r : r + 1] = v_refs[group][r : r + 1] - factor * update
                at += 1

    args = [sums] + list(matrices) + list(updates) + list(small) + [small_update]
    outs = [out(a.shape) for a in matrices] + [out(s) for s in shapes] + [out((2, 15))]
    return call(
        kernel, 1, [full(*a.shape) for a in args], [full(*o.shape) for o in outs], outs,
        heavy=False,
    )(*args)


def pack_rows(arrays):
    rows = [jnp.pad(a, ((0, 0), (0, 128 - a.shape[1]))) for a in arrays]
    total = sum(a.shape[0] for a in arrays)
    rows.append(jnp.zeros((16 - total, 128), F32))
    return jnp.concatenate(rows, axis=0)


def spread_vectors(qkv_sum, wide_grad, sums_one, sums_two, sizes):
    head_own, wide_own, gain_own, dp_size = sizes
    blocks, width = qkv_sum.shape[0], qkv_sum.shape[2] // 3

    def lanes128(array, own):
        array = array.reshape(array.shape[:-1] + (dp_size, own))
        return jnp.pad(array, ((0, 0),) * (array.ndim - 1) + ((0, 128 - own),))

    vectors = jnp.stack(
        [sums_one[0], sums_two[0], sums_one[2], sums_one[1], sums_two[2], sums_two[1]]
    )
    vectors = jnp.broadcast_to(
        lanes128(vectors, gain_own).transpose(1, 0, 2)[None], (blocks, dp_size, 6, 128)
    )
    return jnp.concatenate(
        [
            lanes128(qkv_sum[:, 0, :width], head_own)[:, :, None],
            lanes128(qkv_sum[:, 0, 2 * width :], head_own)[:, :, None],
            lanes128(wide_grad[:, 0], wide_own)[:, :, None],
            vectors,
            jnp.zeros((blocks, dp_size, 7, 128), F32),
        ],
        axis=2,
    )


def on_device(
    dp_size, tensor_size,
    tokens, cotangent, row_lengths, present, groups,
    attn_weight, attn_first, attn_second,
    mix_weight, mix_first, mix_second,
    up_weight, up_first, up_second,
    down_weight, down_first, down_second,
    head_bias, head_first, head_second,
    wide_bias, wide_first, wide_second,
    norm_gains, gain_first, gain_second,
    shift_bias, shift_first, shift_second,
):
    comm = GridComm() if (dp_size, tensor_size) == (8, 4) else GenericComm(dp_size, tensor_size)
    rank = lax.axis_index("tensor")
    row_count, n = groups.shape
    assert row_count == tensor_size
    d = tokens.shape[1]
    width, units = attn_weight.shape[2], up_weight.shape[1]
    head_own, wide_own, gain_own = head_bias.shape[1], wide_bias.shape[0], norm_gains.shape[1]
    small_arrays = [
        (head_bias, head_first, head_second),
        tuple(a.reshape(1, -1) for a in (wide_bias, wide_first, wide_second)),
        (norm_gains, gain_first, gain_second),
        (shift_bias, shift_first, shift_second),
    ]

    attn_shard = [attn_weight[0], attn_weight[1], attn_weight[2], mix_weight.T]
    small = pack_rows([group[0] for group in small_arrays])
    small_all = None
    if comm.small_inside:
        attn_shard.append(jnp.pad(small, ((0, attn_weight.shape[1] - 16), (0, 0))))
    else:
        small_all = comm.gather_small(small.astype(BF).astype(F32))
    attn_g = comm.gather(jnp.concatenate(attn_shard, axis=1).astype(BF))
    up_g = comm.gather(up_weight.astype(BF))
    down_g = comm.gather(down_weight.T.astype(BF))
    attn_z = attn_g.z([])
    attn_xy = attn_g.xy([])
    up_z = up_g.z(attn_z)
    attn_g.diagonal([])
    attn_w = attn_g.core()
    up_xy = up_g.xy(attn_xy)
    down_g.z(up_z)

    tok = lax.dynamic_slice_in_dim(tokens, rank * n, n, 0)
    cot = lax.dynamic_slice_in_dim(cotangent, rank * n, n, 0)
    group_row = lax.dynamic_index_in_dim(groups, rank, 0, keepdims=False)
    present_row = lax.dynamic_index_in_dim(present, rank, 0, keepdims=False)
    length = lax.dynamic_index_in_dim(row_lengths, rank, 0, keepdims=False)
    feature_ids = jnp.arange(present_row.shape[0])
    present_key = jnp.sum(
        (group_row[:, None] == feature_ids[None, :]) * present_row[None, :], axis=1
    )
    key_open = ((jnp.arange(n) < length) & (present_key == 1)).astype(jnp.int32)

    qkv, ctx, e, inv, n1, rstd, low, low_t, tok_t, rows, wide_low = attn_fwd(
        attn_w, width, ((head_own, wide_own, gain_own, dp_size), small_all), tok, group_row, key_open
    )
    deps = [qkv] if comm.small_inside else []
    up_g.diagonal(deps)
    up_w = up_g.core()
    down_g.xy(deps + up_xy)
    act, slope = ffn_up(up_w, low, wide_low)
    down_g.diagonal([act] if comm.small_inside else [])
    down_w = down_g.core()
    layer_out, ds2, df, df_t, sums_two = ffn_down(down_w, act, n1, cot, rows)
    layer_out_all = lax.all_gather(layer_out, "tensor", axis=0, tiled=True)

    down_red = comm.reduction([df_t], halves=True)
    df = tie(df, down_red.core([act]))
    dh, wide_grad, ds1, da, da_t, sums_one = ffn_bwd(up_w, down_w, df, slope, ds2, n1, rstd, rows)
    up_red = comm.reduction([low_t], halves=True)
    da = tie(da, down_red.split([act]) + up_red.core([dh]))
    attn_red = comm.reduction([tok_t, da_t], halves=True)
    sizes = (head_own, wide_own, gain_own, dp_size)
    small_sum = None
    if comm.small_inside:
        odd, odd_sum, back = attn_bwd(attn_w, width, (1, 3), da, qkv, ctx, e, inv, ds1, False)
        extra = pack_vectors((1, 3), odd_sum, wide_grad, sums_one, sums_two, sizes)
        rights = [[([1, 3], odd)], ctx]
        da = tie(
            da, down_red.neighbour() + up_red.split([dh]) + attn_red.core(rights, extra)
        )
        even, even_sum, back = attn_bwd(attn_w, width, (0, 2), da, qkv, ctx, e, inv, back, True)
        extra = pack_vectors((0, 2), even_sum, wide_grad, sums_one, sums_two, sizes)
        sent = attn_red.split([[([0, 2], even)], ctx], extra)
        up_red.neighbour()
        down_parts = down_red.last()
        sent = attn_red.neighbour()
        up_parts = up_red.last()
        attn_parts = attn_red.last()
        back = tie(back, sent)
    else:
        blocks = range(tensor_size)
        dqkv, dqkv_sum, back = attn_bwd(attn_w, width, blocks, da, qkv, ctx, e, inv, ds1, True)
        attn_red.core([dqkv, ctx])
        down_parts, up_parts, attn_parts = down_red.last(), up_red.last(), attn_red.last()
        small_sum = comm.scatter_small(
            spread_vectors(dqkv_sum, wide_grad, sums_one, sums_two, sizes)
        )
    tokens_grad_all = lax.all_gather(back, "tensor", axis=0, tiled=True)

    up_fn, up_sn, up_u, up_sums = lamb_matrix(up_parts, up_weight, up_first, up_second)
    down_rows = down_weight.T
    down_fn, down_sn, down_u, down_sums = lamb_matrix(
        down_parts, down_rows, down_first.T, down_second.T
    )
    last = lamb_last(
        attn_parts, (attn_weight, attn_first, attn_second), (mix_weight, mix_first, mix_second),
        small_sum, small_arrays, (up_sums, down_sums), 1.0 / tensor_size,
    )
    small_moments, small_u, sums = last[6:14], last[14], last[15]
    done = finish(
        comm.total(sums),
        (attn_weight, mix_weight, up_weight, down_rows),
        (last[2], last[5], up_u, down_u),
        [group[0] for group in small_arrays],
        small_u,
    )
    moments = [last[0:2], last[3:5], (up_fn, up_sn), (down_fn, down_sn)]
    moments += [small_moments[2 * k : 2 * k + 2] for k in range(4)]
    result = [layer_out_all, tokens_grad_all]
    for number, (first_new, second_new) in enumerate(moments):
        group = [done[number], first_new, second_new]
        if number == 3:
            group = [a.T for a in group]
        result += [a.reshape(-1) for a in group] if number == 5 else group
    return tuple(result) + (done[8],)


def solution(mesh):
    rows = P("dp", None)
    attn, mix, up = P(None, "dp", "tensor"), P("tensor", "dp"), P("dp", "tensor")
    head, wide, col = P(None, ("tensor", "dp")), P(("tensor", "dp")), P(None, "dp")
    params = tuple(spec for spec in (attn, mix, up, mix, head, wide, col, col) for _ in range(3))
    return jax.shard_map(
        functools.partial(on_device, mesh.shape["dp"], mesh.shape["tensor"]),
        mesh=mesh,
        in_specs=(rows, rows, P("dp"), rows, rows) + params,
        out_specs=(rows, rows) + params + (P(),),
        check_vma=False,
    )
```

```python
import functools

import jax
import jax.numpy as jnp
from jax import lax
from jax.experimental import pallas as pl
from jax.experimental.pallas import tpu as pltpu
from jax.sharding import PartitionSpec as P

HEAD = 64
BF = jnp.bfloat16
F32 = jnp.float32
NN = (((1,), (0,)), ((), ()))
NT = (((1,), (1,)), ((), ()))
TN = (((0,), (0,)), ((), ()))
VMEM_LIMIT = 58 << 20
EXTRA = 64
COST = 0.5e9


def mm(a, b, dims):
    return lax.dot_general(a, b, dims, preferred_element_type=F32)


def full(*shape):
    return pl.BlockSpec(shape, lambda i: (0,) * len(shape))


def per(*shape):
    return pl.BlockSpec((1,) + shape, lambda i: (i,) + (0,) * len(shape))


ANY = pl.BlockSpec(memory_space=pl.ANY)
SCALARS = pl.BlockSpec(memory_space=pltpu.SMEM)


def out(shape, dtype=F32):
    return jax.ShapeDtypeStruct(shape, dtype)


def call(kernel, grid, in_specs, out_specs, out_shape, scratch=(), us=2.0):
    return pl.pallas_call(
        kernel,
        grid=(grid,),
        in_specs=in_specs,
        out_specs=out_specs,
        out_shape=out_shape,
        scratch_shapes=list(scratch),
        compiler_params=pltpu.CompilerParams(vmem_limit_bytes=VMEM_LIMIT),
        cost_estimate=pl.CostEstimate(
            flops=int(us * COST), bytes_accessed=1000, transcendentals=0
        ),
    )


class Pieces:
    def __init__(self, arrays, plan, where, blocks, rows, lanes, group=None):
        self.arrays, self.plan, self.where, self.group = arrays, plan, where, group
        self.blocks, self.rows, self.lanes = blocks, rows, lanes

    def scratch(self):
        if self.group is not None:
            shape, count = (self.blocks, 8, self.rows // 8, self.lanes), 1
        elif self.plan is None:
            shape, count = (self.blocks, self.rows, self.lanes), 1
        else:
            shape, count = (self.blocks, 4, 2, self.rows // 8, self.lanes), 4
        return [pltpu.VMEM(shape, BF), pltpu.SemaphoreType.DMA((self.blocks, count))]

    def start(self, refs, where_ref, buffer, sems, ps=None):
        for p in range(self.blocks) if ps is None else ps:
            if self.group is not None:
                source = refs[0].at[:, where_ref[2] ^ p, self.group]
                pltpu.make_async_copy(source, buffer.at[p], sems.at[p, 0]).start()
                continue
            if self.plan is None:
                pltpu.make_async_copy(refs[0].at[p], buffer.at[p], sems.at[p, 0]).start()
                continue
            for number, (array, y_rel, pair_rel) in enumerate(self.plan[p]):
                pair = (where_ref[0] // 2) ^ pair_rel
                target = buffer.at[p, pl.ds(pair * 2, 2), where_ref[1] ^ y_rel]
                pltpu.make_async_copy(refs[array], target, sems.at[p, number]).start()

    def wait(self, refs, p, buffer, sems):
        if self.group is not None:
            source = refs[0].at[:, 0, self.group]
            pltpu.make_async_copy(source, buffer.at[p], sems.at[p, 0]).wait()
            return
        if self.plan is None:
            pltpu.make_async_copy(refs[0].at[0], buffer.at[p], sems.at[p, 0]).wait()
            return
        for number in range(4):
            target = buffer.at[p, pl.ds(0, 2), 0]
            pltpu.make_async_copy(refs[0], target, sems.at[p, number]).wait()

    def read(self, buffer, p, first, last):
        if self.group is not None:
            return buffer[p, :, :, first:last].reshape(self.rows, last - first)
        if self.plan is None:
            return buffer[p, :, first:last]
        return buffer[p, :, :, :, first:last].reshape(self.rows, last - first)


def tie(array, deps):
    return lax.optimization_barrier((array, tuple(deps)))[0] if deps else array


class GenericComm:
    small_inside = False

    def __init__(self, dp, tensor):
        self.dp, self.tensor = dp, tensor
        self.where = jnp.zeros((2,), jnp.int32)

    def gather(self, shard):
        return GenericGather(self, shard)

    def gather_stacked(self, shard):
        rows = shard.shape[0] // 2
        return [GenericGather(self, part).core() for part in (shard[:rows], shard[rows:])]

    def gather_small(self, vector):
        return lax.all_gather(lax.all_gather(vector, "dp", axis=0), "tensor", axis=0)

    def scatter_small(self, vectors):
        own = lax.psum_scatter(vectors, "tensor", scatter_dimension=0)
        return lax.psum_scatter(own, "dp", scatter_dimension=0)

    def total(self, values):
        return lax.psum(values, ("dp", "tensor"))

    def reduction(self, lefts):
        return GenericReduction(self, lefts)

    def block_sets(self):
        return [range(self.tensor)]


class GenericGather:
    def __init__(self, comm, shard):
        self.comm, self.shard = comm, shard

    def z(self, deps):
        return []

    def xy(self, deps):
        return []

    def diagonal(self, deps):
        pass

    def core(self):
        rows = lax.all_gather(self.shard, "dp", axis=0, tiled=True)
        blocks = lax.all_gather(rows, "tensor", axis=0)
        return Pieces([blocks], None, self.comm.where, *blocks.shape)


class GenericReduction:
    def __init__(self, comm, lefts):
        self.comm, self.lefts = comm, lefts

    def core(self, rights, extra=None):
        self.rights = rights
        return []


    def last(self):
        stacked = grads(list(zip(self.lefts, self.rights)), range(self.comm.tensor))
        own = lax.psum_scatter(stacked, "tensor", scatter_dimension=0)
        return [lax.psum_scatter(own, "dp", scatter_dimension=0, tiled=True).astype(F32)]


class GridComm:
    small_inside = True

    def __init__(self):
        self.z = lax.axis_index("dp") // 2
        self.y = lax.axis_index("dp") % 2
        rank = lax.axis_index("tensor")
        self.where = jnp.stack([self.z, self.y, rank]).astype(jnp.int32)

    @staticmethod
    def send(array, dp_xor, tensor_xor):
        pairs = [
            (d * 4 + t, (d ^ dp_xor) * 4 + (t ^ tensor_xor)) for d in range(8) for t in range(4)
        ]
        return lax.ppermute(array, ("dp", "tensor"), pairs)

    def send_core(self, array):
        return self.send(array, 0, 1)

    def send_x(self, array):
        return self.send(array, 0, 2)

    def send_y(self, array):
        return self.send(array, 1, 0)

    def send_z(self, array, k):
        return self.send(array, 2 * k, 0)

    def gather(self, shard):
        return GridGather(self, shard)

    def gather_stacked(self, shard):
        rows, lanes = shard.shape[0] // 2, shard.shape[1]
        everything = lax.all_gather(shard, ("dp", "tensor"), axis=0, tiled=True)
        everything = everything.reshape(8, 4, 2, rows, lanes)
        return [Pieces([everything], None, self.where, 4, 8 * rows, lanes, g) for g in range(2)]

    def total(self, values):
        values = values + self.send_core(values)
        sent = self.send_x(values), self.send_y(values), self.send(values, 1, 2)
        values = values + sent[0] + (sent[1] + sent[2])
        sent = [self.send_z(values, k) for k in (1, 2, 3)]
        return values + sent[0] + (sent[1] + sent[2])

    def reduction(self, lefts):
        return Reduction(self, lefts)

    def block_sets(self):
        return [(1, 3), (0, 2)]


class GridGather:
    def __init__(self, comm, shard):
        self.comm, self.shard = comm, shard

    def z(self, deps):
        shard = tie(self.shard, deps)
        self.by_z = [shard] + [self.comm.send_z(shard, k) for k in (1, 2, 3)]
        return self.by_z[1:]

    def xy(self, deps):
        low = pair(self.by_z[0], self.by_z[1], self.comm.where)
        high = pair(self.by_z[2], self.by_z[3], self.comm.where)
        low, high = tie(low, deps), tie(high, deps)
        x_low, y_low = self.comm.send_x(low), self.comm.send_y(low)
        x_high, y_high = self.comm.send_x(high), self.comm.send_y(high)
        self.near, self.far = [low, high, y_low, y_high], [x_low, x_high]
        return [x_high, y_high]

    def diagonal(self, deps):
        y_low, x_high = tie(self.near[2], deps), tie(self.far[1], deps)
        self.far += [self.comm.send_x(y_low), self.comm.send_y(x_high)]

    def core(self):
        near_core = [self.comm.send_core(a) for a in self.near]
        far_core = [self.comm.send_core(a) for a in self.far]
        arrays = self.near + near_core + self.far + far_core
        plan = [[(4 * p + c, c // 2, c % 2) for c in range(4)] for p in range(4)]
        rows, lanes = self.shard.shape
        return Pieces(arrays, plan, self.comm.where, 4, 8 * rows, lanes)


class Reduction:
    def __init__(self, comm, lefts):
        self.comm, self.lefts = comm, lefts

    def core(self, rights, extra=None):
        odd = grads(list(zip(self.lefts, rights)), (1, 3), extra)
        self.core_got = self.comm.send_core(odd)
        return [odd]

    def split(self, rights, extra=None, deps=()):
        terms = list(zip(self.lefts, rights))
        split = grads_split(terms, tie(self.core_got, deps), self.comm.where, extra)
        x_first, y_first, self.x_second, self.y_second, self.mine = split
        self.x_got, self.y_got = self.comm.send_x(x_first), self.comm.send_y(y_first)
        return [self.mine]

    def neighbour(self, deps=()):
        x_second, y_second = add_low(
            tie(self.x_second, deps), self.y_second, self.x_got, self.y_got
        )
        self.x_got2, self.y_got2 = self.comm.send_x(x_second), self.comm.send_y(y_second)
        return [x_second, y_second]

    def last(self, deps=(), us=2.8):
        mine = tie(self.mine, deps)[None]
        low = [(mine, 0), (self.x_got[None], 2), (self.y_got2[None], 0)]
        high = [(mine, 2), (self.y_got[None], 2), (self.x_got2[None], 0)]
        parts = combine([low, high], None, self.comm.where, us)
        self.done = [parts[0]]
        return [parts[0]] + [self.comm.send_z(parts[k], k) for k in (1, 2, 3)]


def pair(first, second, where):
    rows, lanes = first.shape

    def kernel(where_ref, first_ref, second_ref, out_ref):
        odd = where_ref[0] % 2
        out_ref[odd] = first_ref[...]
        out_ref[1 - odd] = second_ref[...]

    return call(
        kernel, 1, [SCALARS, full(rows, lanes), full(rows, lanes)], full(2, rows, lanes),
        out((2, rows, lanes), BF), us=1.8,
    )(where, first, second)


def add_low(x_second, y_second, x_got, y_got):
    half = x_second.shape

    def kernel(x_ref, y_ref, xg_ref, yg_ref, xo_ref, yo_ref):
        xo_ref[...] = (x_ref[...].astype(F32) + yg_ref[...].astype(F32)).astype(BF)
        yo_ref[...] = (y_ref[...].astype(F32) + xg_ref[...].astype(F32)).astype(BF)

    return call(
        kernel, 1, [full(*half)] * 4, [full(*half)] * 2, [out(half, BF), out(half, BF)],
        us=2.0,
    )(x_second, y_second, x_got, y_got)


def block_of(right, p):
    if not isinstance(right, list):
        return right, p
    for ps, array in right:
        if p in ps:
            return array, list(ps).index(p)
    raise KeyError(p)


def grads(terms, ps, extra=None):
    ps = list(ps)
    d, n = terms[0][0].shape
    firsts = [block_of(right, ps[0]) for _, right in terms]
    steps = [block_of(right, ps[1])[1] - first for (_, right), (_, first) in zip(terms, firsts)]
    lanes = [array.shape[2] for array, _ in firsts]

    def kernel(*refs):
        at = 0
        for number, width in enumerate(lanes):
            left, right = refs[2 * number], refs[2 * number + 1]
            refs[-1][0, :, at : at + width] = mm(left[...], right[0], NN).astype(BF)
            at += width
        if at < wide:
            refs[-1][0, :, at:] = jnp.zeros((d, wide - at), BF)
        if extra is not None:
            for c in range(8):
                refs[-1][0, c * (d // 8) : c * (d // 8) + 16, at:] = refs[-2][0, c]

    specs, args = [], []
    for (left, _), (array, first), step, wide in zip(terms, firsts, steps, lanes):
        specs.append(full(d, n))
        specs.append(
            pl.BlockSpec((1, n, wide), lambda i, first=first, step=step: (first + step * i, 0, 0))
        )
        args += [left, array]
    wide = sum(lanes)
    if extra is not None:
        specs.append(per(8, 16, EXTRA))
        args.append(extra)
    wide += -wide % 128
    return call(
        kernel, len(ps), specs, per(d, wide), out((len(ps), d, wide), BF),
        us=4.5,
    )(*args)


def split_call(terms, got, where, write, outs, extra=None):
    d, n = terms[0][0].shape
    rows = d // 8
    count = len(terms)
    evens = [[block_of(right, p) for p in (0, 2)] for _, right in terms]
    lanes = [pair[0][0].shape[2] for pair in evens]
    wide = got.shape[2]

    def kernel(where_ref, *refs):
        got_ref = refs[3 * count]
        y = where_ref[1]

        def part(p, y_at):
            at = 0
            columns = []
            for number, width in enumerate(lanes):
                left, right = refs[3 * number], refs[3 * number + 1 + p // 2]
                lhs = left[:, y_at].reshape(4 * rows, n)
                value = mm(lhs, right[0], NN).reshape(4, rows, width)
                value = value + got_ref[p // 2, :, y_at, :, at : at + width].astype(F32)
                columns.append((at, width, value.astype(BF)))
                at += width
            if extra is not None:
                value = got_ref[p // 2, :, y_at, :, at:].astype(F32)
                top = value[:, 0:16] + refs[3 * count + 1][p // 2, :, y_at].astype(F32)
                value = jnp.concatenate([top, value[:, 16:]], axis=1)
                columns.append((at, EXTRA, value.astype(BF)))
            elif at < wide:
                columns.append((at, wide - at, jnp.zeros((4, rows, wide - at), BF)))
            return columns

        write(part, y, refs[3 * count + 1 + (extra is not None) :])

    specs, args = [SCALARS], [where]
    for (left, _), pair, width in zip(terms, evens, lanes):
        specs.append(full(4, 2, rows, n))
        args.append(left.reshape(4, 2, rows, n))
        for array, index in pair:
            specs.append(pl.BlockSpec((1, n, width), lambda i, index=index: (index, 0, 0)))
            args.append(array)
    specs.append(full(2, 4, 2, rows, wide))
    args.append(got.reshape(2, 4, 2, rows, wide))
    if extra is not None:
        specs.append(full(2, 4, 2, 16, EXTRA))
        args.append(extra.reshape(2, 4, 2, 16, EXTRA))
    shapes = [shape + (rows, wide) for shape in outs]
    return call(
        kernel, 1, specs, [full(*shape) for shape in shapes], [out(shape, BF) for shape in shapes],
        us=5.0,
    )(*args)


def grads_split(terms, got, where, extra=None):
    def write(part, y, refs):
        x_first, y_first, x_second, y_second, mine = refs
        for at, width, value in part(2, 1 - y):
            x_first[0:2, :, at : at + width] = value[0:2]
            y_first[0:2, :, at : at + width] = value[2:4]
        for at, width, value in part(2, y):
            x_first[2:4, :, at : at + width] = value[0:2]
            x_second[:, :, at : at + width] = value[2:4]
        for at, width, value in part(0, 1 - y):
            y_first[2:4, :, at : at + width] = value[2:4]
            y_second[:, :, at : at + width] = value[0:2]
        for at, width, value in part(0, y):
            mine[:, :, at : at + width] = value

    return split_call(terms, got, where, write, [(4,), (4,), (2,), (2,), (4,)], extra)


def pack_vectors(ps, qkv_sum, wide_grad, sums_one, sums_two, sizes):
    head_own, wide_own, gain_own, dp_size = sizes
    width = qkv_sum.shape[2] // 3
    stride = ps[1] - ps[0]

    def kernel(qkv_ref, wide_ref, one_ref, two_ref, out_ref, rows_ref):
        rows_ref[...] = jnp.zeros_like(rows_ref)
        rows = [
            wide_ref[0], one_ref[0:1], two_ref[0:1], one_ref[2:3], one_ref[1:2], two_ref[2:3],
            two_ref[1:2],
        ]
        for c in range(dp_size):
            for number, first in enumerate((0, 2 * width)):
                first += c * head_own
                rows_ref[c, number : number + 1, 0:head_own] = qkv_ref[0, :, first : first + head_own]
            for number, row in enumerate(rows):
                own = gain_own if number else wide_own
                at, first = 2 + 2 * number, c * own
                rows_ref[c, at : at + 1, :] = row[:, first : first + EXTRA]
                rest = own - EXTRA
                rows_ref[c, at + 1 : at + 2, 0:rest] = row[:, first + EXTRA : first + own]
        out_ref[0] = rows_ref[...].astype(BF)

    return call(
        kernel, 2,
        [
            per(1, 3 * width), pl.BlockSpec((1, 1, wide_own * dp_size), lambda i: (ps[0] + stride * i, 0, 0)),
            full(*sums_one.shape), full(*sums_two.shape),
        ],
        per(dp_size, 16, EXTRA), out((2, dp_size, 16, EXTRA), BF),
        [pltpu.VMEM((dp_size, 16, EXTRA), F32)], us=1.7,
    )(qkv_sum, wide_grad, sums_one, sums_two)


def combine(halves, rows_of, where, us):
    arrays = []
    for array in [array for half in halves for array, _ in half]:
        if not any(array is other for other in arrays):
            arrays.append(array)
    index = lambda array: [array is other for other in arrays].index(True)
    plans = [
        [(index(array), rows_of[h][0] if rows_of else first) for array, first in half]
        for h, half in enumerate(halves)
    ]
    chunk = arrays[0].shape[2:]

    def kernel(where_ref, *refs):
        o0, o1, o2, o3, total = refs[len(arrays) :]
        for h, plan in enumerate(plans):
            for j in range(2):
                number, first = plan[0]
                value = refs[number][0, first + j].astype(F32)
                for number, first in plan[1:]:
                    value = value + refs[number][0, first + j].astype(F32)
                total[2 * h + j] = value
        z = where_ref[0]
        o0[...] = total[z]
        o1[...] = total[z ^ 1].astype(BF)
        o2[...] = total[z ^ 2].astype(BF)
        o3[...] = total[z ^ 3].astype(BF)

    return call(
        kernel, 1,
        [SCALARS] + [full(1, *a.shape[1:]) for a in arrays],
        [full(*chunk)] * 4,
        [out(chunk), out(chunk, BF), out(chunk, BF), out(chunk, BF)],
        [pltpu.VMEM((4,) + chunk, F32)],
        us=us,
    )(where, *arrays)


def norm(summed):
    center = summed - jnp.mean(summed, axis=-1, keepdims=True)
    spread = jnp.mean(center * center, axis=-1, keepdims=True)
    scaled = lax.rsqrt(spread + 1e-05)
    return (center * scaled, scaled)


def norm_back(upstream, normal, scaled):
    inner_sum = (
        upstream
        - jnp.mean(upstream, axis=-1, keepdims=True)
        - normal * jnp.mean(upstream * normal, axis=-1, keepdims=True)
    )
    return scaled * inner_sum


G1, G2, BO, B1, C2, B2 = range(6)


def attn_fwd(pieces, width, small, tok, groups, key_open):
    n, d = tok.shape
    blocks = pieces.blocks
    heads = width // HEAD
    count = len(pieces.arrays)
    (head_own, wide_own, gain_own, dp_size), given = small
    units = wide_own * dp_size

    def kernel(where_ref, tok_ref, gq_ref, gk_ref, open_ref, *refs):
        w_refs, refs = refs[:count], refs[count:]
        if given is not None:
            bias_in, rows_in, wide_in = refs[:3]
            refs = refs[3:]
        qkv_ref, ctx_ref, e_ref, inv_ref, n1_ref, rstd_ref, low_ref, low_t_ref, tok_t_ref = refs[:9]
        rows_ref, wide_ref, att_ref, mask_ref, w_ref, sems = refs[9:]
        step = pl.program_id(0)

        @pl.when(step == 0)
        def _():
            pieces.start(w_refs, where_ref, w_ref, sems)
            seen = (open_ref[...] == 1) | (gq_ref[...] == gk_ref[...])
            mask_ref[...] = jnp.where(seen, 0.0, -1e30)
            att_ref[...] = jnp.zeros_like(att_ref)
            tok_t_ref[...] = tok_ref[...].T

        pieces.wait(w_refs, step, w_ref, sems)
        if given is None:
            first = 4 * width
            vectors = [
                w_ref[step, c // 2, c % 2, 0:16, first : first + 128].astype(F32)
                for c in range(dp_size)
            ]

            def line(row, used):
                return jnp.concatenate([v[row : row + 1, :used] for v in vectors], axis=1)

            bias_q, bias_v = line(0, head_own), line(1, head_own)
            wide_ref[0] = line(2, wide_own)

            @pl.when(step == 0)
            def _():
                for row in range(6):
                    rows_ref[row : row + 1] = line(3 + row, gain_own)

        else:
            bias_q, bias_v = bias_in[0, 0:1], bias_in[0, 1:2]
            wide_ref[0] = wide_in[0]
            rows_ref[0:6] = rows_in[...]

        qkv = mm(tok_ref[...], pieces.read(w_ref, step, 0, 3 * width), NN)
        lane = lax.broadcasted_iota(jnp.int32, (n, 128), 1)
        q_all = (qkv[:, :width] + bias_q).astype(BF)
        k_all = qkv[:, width : 2 * width].astype(BF)
        v_all = (qkv[:, 2 * width :] + bias_v).astype(BF)
        qkv_ref[0] = jnp.concatenate([q_all, k_all, v_all], axis=1)
        contexts = []
        inv_all = jnp.zeros((n, 128), F32)
        for h in range(heads):
            q = q_all[:, h * HEAD : (h + 1) * HEAD] * jnp.asarray(HEAD**-0.5, BF)
            k = k_all[:, h * HEAD : (h + 1) * HEAD]
            v = v_all[:, h * HEAD : (h + 1) * HEAD]
            s = mm(q, k, NT) + mask_ref[...]
            e = jnp.exp(s - jnp.max(s, axis=-1, keepdims=True)).astype(BF)
            e_ref[0, h] = e
            v_one = jnp.concatenate([v, jnp.ones_like(v)], axis=1)
            r = mm(e, v_one, NN)
            inv = 1.0 / r[:, HEAD : HEAD + 1]
            contexts.append((r[:, :HEAD] * inv).astype(BF))
            inv_all = jnp.where(lane == h, inv, inv_all)
        ctx = jnp.concatenate(contexts, axis=1)
        ctx_ref[0] = ctx
        inv_ref[0] = inv_all
        att_ref[...] += mm(ctx, pieces.read(w_ref, step, 3 * width, 4 * width), NT)

        @pl.when(step == blocks - 1)
        def _():
            summed = tok_ref[...].astype(F32) + (att_ref[...] + rows_ref[BO : BO + 1])
            normal, scaled = norm(summed)
            n1_ref[...] = normal
            rstd_ref[...] = scaled
            normed = normal * rows_ref[G1 : G1 + 1] + rows_ref[B1 : B1 + 1]
            low = normed.astype(BF)
            low_ref[...] = low
            low_t_ref[...] = low.T

    specs = [SCALARS, full(n, d), full(n, 1), full(1, n), full(1, n)] + [ANY] * count
    args = [pieces.where, tok, groups.reshape(n, 1), groups.reshape(1, n), key_open.reshape(1, n)]
    args += pieces.arrays
    if given is not None:
        biases = given[:, :, 0:2, :head_own].transpose(0, 2, 1, 3).reshape(blocks, 2, width)
        wide_low = given[:, :, 2, :wide_own].reshape(blocks, 1, units)
        specs += [per(2, width), full(6, d), per(1, units)]
        args += [
            biases, given[0, :, 3:9, :gain_own].transpose(1, 0, 2).reshape(6, d), wide_low,
        ]
    return call(
        kernel, blocks, specs,
        [
            per(n, 3 * width), per(n, width), per(heads, n, n), per(n, 128),
            full(n, d), full(n, 1), full(n, d), full(d, n), full(d, n), full(8, d), per(1, units),
        ],
        [
            out((blocks, n, 3 * width), BF), out((blocks, n, width), BF),
            out((blocks, heads, n, n), BF), out((blocks, n, 128)),
            out((n, d)), out((n, 1)), out((n, d), BF), out((d, n), BF), out((d, n), BF),
            out((8, d)), out((blocks, 1, units)),
        ],
        [pltpu.VMEM((n, d), F32), pltpu.VMEM((n, n), F32)] + pieces.scratch(),
        us=17,
    )(*args)


def ffn_up(pieces, low, wide_bias):
    n, d = low.shape
    blocks, units, count = pieces.blocks, pieces.lanes, len(pieces.arrays)

    def kernel(where_ref, low_ref, bias_ref, *refs):
        w_refs, (act_ref, slope_ref, w_ref, sems) = refs[:count], refs[count:]
        step = pl.program_id(0)

        @pl.when(step == 0)
        def _():
            pieces.start(w_refs, where_ref, w_ref, sems)

        pieces.wait(w_refs, step, w_ref, sems)
        h = mm(low_ref[...], pieces.read(w_ref, step, 0, units), NN) + bias_ref[0]
        cdf = 0.5 * (1.0 + lax.erf(h * (0.5**0.5)))
        act_ref[0] = (h * cdf).astype(BF)
        density = jnp.exp(h * h * -0.5) * 0.3989422804014327
        slope_ref[0] = (cdf + h * density).astype(BF)

    return call(
        kernel, blocks,
        [SCALARS, full(n, d), per(1, units)] + [ANY] * count,
        [per(n, units), per(n, units)],
        [out((blocks, n, units), BF), out((blocks, n, units), BF)],
        pieces.scratch(),
        us=8.5,
    )(pieces.where, low, wide_bias, *pieces.arrays)


def ffn_down(pieces, act, n1, cot, rows):
    n, d = n1.shape
    blocks, units, count = pieces.blocks, pieces.lanes, len(pieces.arrays)

    def kernel(where_ref, act_ref, n1_ref, cot_ref, rows_ref, *refs):
        w_refs, refs = refs[:count], refs[count:]
        y_ref, ds_ref, df_ref, df_t_ref, sum_ref, acc_ref, w_ref, sems = refs
        step = pl.program_id(0)

        @pl.when(step == 0)
        def _():
            pieces.start(w_refs, where_ref, w_ref, sems)
            normed = n1_ref[...] * rows_ref[G1 : G1 + 1] + rows_ref[B1 : B1 + 1]
            acc_ref[...] = normed + rows_ref[C2 : C2 + 1]

        pieces.wait(w_refs, step, w_ref, sems)
        acc_ref[...] += mm(act_ref[0], pieces.read(w_ref, step, 0, units), NT)

        @pl.when(step == blocks - 1)
        def _():
            normal, scaled = norm(acc_ref[...])
            gain = rows_ref[G2 : G2 + 1]
            y_ref[...] = (normal * gain + rows_ref[B2 : B2 + 1]).astype(BF)
            upstream = cot_ref[...].astype(F32)
            ds = norm_back(upstream * gain, normal, scaled)
            ds_ref[...] = ds
            df = ds.astype(BF)
            df_ref[...] = df
            df_t_ref[...] = df.T
            sum_ref[...] = jnp.zeros_like(sum_ref)
            sum_ref[0:1] = jnp.sum(upstream * normal, axis=0, keepdims=True)
            sum_ref[1:2] = jnp.sum(upstream, axis=0, keepdims=True)
            sum_ref[2:3] = jnp.sum(ds, axis=0, keepdims=True)

    return call(
        kernel, blocks,
        [SCALARS, per(n, units), full(n, d), full(n, d), full(*rows.shape)] + [ANY] * count,
        [full(n, d), full(n, d), full(n, d), full(d, n), full(8, d)],
        [out((n, d), BF), out((n, d)), out((n, d), BF), out((d, n), BF), out((8, d))],
        [pltpu.VMEM((n, d), F32)] + pieces.scratch(),
        us=10.5,
    )(pieces.where, act, n1, cot, rows, *pieces.arrays)


def ffn_bwd(up, down, df, slope, ds2, n1, rstd, rows):
    n, d = n1.shape
    blocks, units = up.blocks, up.lanes
    up_count, down_count = len(up.arrays), len(down.arrays)

    def kernel(where_ref, df_ref, slope_ref, ds2_ref, n1_ref, rstd_ref, rows_ref, *refs):
        up_refs, down_refs = refs[:up_count], refs[up_count : up_count + down_count]
        refs = refs[up_count + down_count :]
        dh_ref, dc_ref, ds_ref, da_ref, da_t_ref, sum_ref = refs[:6]
        acc_ref, wu_ref, sems_u, wd_ref, sems_d = refs[6:]
        step = pl.program_id(0)

        @pl.when(step == 0)
        def _():
            down.start(down_refs, where_ref, wd_ref, sems_d)
            up.start(up_refs, where_ref, wu_ref, sems_u)
            acc_ref[...] = ds2_ref[...]

        down.wait(down_refs, step, wd_ref, sems_d)
        up.wait(up_refs, step, wu_ref, sems_u)
        dact = mm(df_ref[...], down.read(wd_ref, step, 0, units), NN)
        dh = (dact * slope_ref[0].astype(F32)).astype(BF)
        dh_ref[0] = dh
        dc_ref[0] = jnp.sum(dh.astype(F32), axis=0, keepdims=True)
        acc_ref[...] += mm(dh, up.read(wu_ref, step, 0, units), NT)

        @pl.when(step == blocks - 1)
        def _():
            dnormed = acc_ref[...]
            normal = n1_ref[...]
            ds = norm_back(dnormed * rows_ref[G1 : G1 + 1], normal, rstd_ref[...])
            ds_ref[...] = ds
            da = ds.astype(BF)
            da_ref[...] = da
            da_t_ref[...] = da.T
            sum_ref[...] = jnp.zeros_like(sum_ref)
            sum_ref[0:1] = jnp.sum(dnormed * normal, axis=0, keepdims=True)
            sum_ref[1:2] = jnp.sum(dnormed, axis=0, keepdims=True)
            sum_ref[2:3] = jnp.sum(ds, axis=0, keepdims=True)

    return call(
        kernel, blocks,
        [SCALARS, full(n, d), per(n, units), full(n, d), full(n, d), full(n, 1), full(*rows.shape)]
        + [ANY] * (up_count + down_count),
        [per(n, units), per(1, units), full(n, d), full(n, d), full(d, n), full(8, d)],
        [
            out((blocks, n, units), BF), out((blocks, 1, units)), out((n, d)),
            out((n, d), BF), out((d, n), BF), out((8, d)),
        ],
        [pltpu.VMEM((n, d), F32)] + up.scratch() + down.scratch(),
        us=13.5,
    )(up.where, df, slope, ds2, n1, rstd, rows, *up.arrays, *down.arrays)


def attn_bwd(pieces, width, ps, da, qkv, ctx, e, inv, back, last):
    n, d = back.shape
    ps = list(ps)
    count = len(pieces.arrays)
    heads = width // HEAD
    stride = ps[1] - ps[0]
    at = lambda i: ps[0] + stride * i

    def kernel(where_ref, da_ref, qkv_ref, ctx_ref, e_ref, inv_ref, back_ref, *refs):
        w_refs, (dqkv_ref, sum_ref, tg_ref, acc_ref, w_ref, sems) = refs[:count], refs[count:]
        step = pl.program_id(0)

        @pl.when(step == 0)
        def _():
            pieces.start(w_refs, where_ref, w_ref, sems, ps)
            acc_ref[...] = back_ref[...]

        pieces.wait(w_refs, at(step), w_ref, sems)
        dctx = mm(da_ref[...], pieces.read(w_ref, at(step), 3 * width, 4 * width), NN)
        dctx = dctx.astype(BF).astype(F32)
        scale = HEAD**-0.5
        dqs, dks, dvs = [], [], []
        for h in range(heads):
            q = qkv_ref[0, :, h * HEAD : (h + 1) * HEAD]
            k = qkv_ref[0, :, width + h * HEAD : width + (h + 1) * HEAD]
            v = qkv_ref[0, :, 2 * width + h * HEAD : 2 * width + (h + 1) * HEAD]
            e = e_ref[0, h]
            do = dctx[:, h * HEAD : (h + 1) * HEAD] * inv_ref[0, :, h : h + 1]
            ctx = ctx_ref[0, :, h * HEAD : (h + 1) * HEAD].astype(F32)
            delta = jnp.sum(do * ctx, axis=-1, keepdims=True)
            do_low = do.astype(BF)
            dp = mm(do_low, v, NT)
            ds = (e.astype(F32) * (dp - delta)).astype(BF)
            dvs.append(mm(e, do_low, TN))
            dqs.append(mm(ds, k, NN) * scale)
            dks.append(mm(ds, q, TN) * scale)
        dqkv = jnp.concatenate(dqs + dks + dvs, axis=1).astype(BF)
        dqkv_ref[0] = dqkv
        sum_ref[0] = jnp.sum(dqkv.astype(F32), axis=0, keepdims=True)
        acc_ref[...] += mm(dqkv, pieces.read(w_ref, at(step), 0, 3 * width), NT)

        @pl.when(step == len(ps) - 1)
        def _():
            tg_ref[...] = acc_ref[...].astype(tg_ref.dtype)

    def of(*shape):
        return pl.BlockSpec((1,) + shape, lambda i: (at(i),) + (0,) * len(shape))

    return call(
        kernel, len(ps),
        [SCALARS, full(n, d), of(n, 3 * width), of(n, width), of(heads, n, n), of(n, 128), full(n, d)]
        + [ANY] * count,
        [per(n, 3 * width), per(1, 3 * width), full(n, d)],
        [
            out((len(ps), n, 3 * width), BF), out((len(ps), 1, 3 * width)),
            out((n, d), BF if last else F32),
        ],
        [pltpu.VMEM((n, d), F32)] + pieces.scratch(),
        us=14.3,
    )(pieces.where, da, qkv, ctx, e, inv, back, *pieces.arrays)


def lamb(gradient, master, first, second):
    first_new = 0.5 * first + 0.5 * gradient
    second_new = 0.5 * second + 0.5 * gradient * gradient
    update = first_new / (jnp.sqrt(second_new) + 1e-06) + 0.01 * master
    return first_new, second_new, update


def whole_sum(array):
    return jnp.sum(jnp.sum(array * array, axis=1, keepdims=True), axis=0, keepdims=True)


def chunk_sum(refs, lanes):
    total = refs[0][:, lanes[0] : lanes[1]]
    for ref in refs[1:]:
        total = total + ref[:, lanes[0] : lanes[1]].astype(F32)
    return total


def moved(source, target, buffer, sems):
    into = pltpu.make_async_copy(source, buffer, sems.at[0])
    back = pltpu.make_async_copy(buffer, target, sems.at[1])
    into.start()

    def turn():
        into.wait()
        back.start()

    return turn, back.wait


def lamb_matrices(parts, entries, carried=None):
    count = len(parts)
    extra = [] if carried is None else [carried]

    def kernel(*refs):
        part_refs = refs[:count]
        ins, refs = refs[count : count + 3 * len(entries)], refs[count + 3 * len(entries) :]
        if extra:
            turn, end = moved(refs[0], refs[1 + 3 * len(entries) + 1], refs[-2], refs[-1])
            refs = refs[1:]
        sum_ref = refs[3 * len(entries)]
        for number, (lane, turned, master, _, _) in enumerate(entries):
            m_ref, f_ref, s_ref = ins[3 * number : 3 * number + 3]
            fn_ref, sn_ref, u_ref = refs[3 * number : 3 * number + 3]
            gradient = chunk_sum(part_refs, (lane, lane + master.shape[0 if turned else 1]))
            if turned:
                gradient = gradient.T
            fn_ref[...], sn_ref[...], update = lamb(gradient, m_ref[...], f_ref[...], s_ref[...])
            u_ref[...] = update
            at = 2 * number
            sum_ref[at : at + 1] = jnp.broadcast_to(whole_sum(m_ref[...]), (1, 128))
            sum_ref[at + 1 : at + 2] = jnp.broadcast_to(whole_sum(update), (1, 128))
        if extra:
            turn()
            end()

    shapes = [entry[2].shape for entry in entries for _ in range(3)]
    args = list(parts) + [array for entry in entries for array in entry[2:]]
    specs = [full(*a.shape) for a in args] + [ANY] * len(extra)
    outs = [out(shape) for shape in shapes] + [out((8, 128))]
    out_specs = [full(*o.shape) for o in outs] + [ANY] * len(extra)
    outs += [out(a.shape, a.dtype) for a in extra]
    scratch = []
    for a in extra:
        scratch = [pltpu.VMEM(a.shape, a.dtype), pltpu.SemaphoreType.DMA((2,))]
    return call(kernel, 1, specs, out_specs, outs, scratch, us=2.6)(*args, *extra)


def lamb_last(parts, attn, small_grad, small, early, share):
    count = len(parts)
    width = attn[0].shape[2]
    shapes = [group[0].shape for group in small]

    def kernel(*refs):
        part_refs, refs = refs[:count], refs[count:]
        m_ref, f_ref, s_ref = refs[:3]
        small_refs, early_refs, refs = refs[3:15], refs[15:17], refs[17:]
        if small_grad is not None:
            small_ref, refs = refs[0], refs[1:]
        fn_ref, sn_ref, u_ref = refs[:3]
        small_out, su_ref, sum_ref, pack = refs[3:11], refs[11], refs[12], refs[13]
        row = lax.broadcasted_iota(jnp.int32, (8, 128), 0)
        lane = lax.broadcasted_iota(jnp.int32, (8, 128), 1)
        sums = jnp.zeros((8, 128), F32)

        def put(sums, index, weight_sq, update_sq):
            sums = jnp.where((row == 0) & (lane == index), weight_sq, sums)
            return jnp.where((row == 1) & (lane == index), update_sq, sums)

        for k in range(3):
            gradient = chunk_sum(part_refs, (k * width, (k + 1) * width))
            fn, sn, update = lamb(gradient, m_ref[k], f_ref[k], s_ref[k])
            fn_ref[k], sn_ref[k], u_ref[k] = fn, sn, update
            sums = put(sums, k, whole_sum(m_ref[k]), whole_sum(update))
        for index, call_index, at in ((3, 0, 2), (4, 0, 0), (5, 1, 0)):
            ref = early_refs[call_index]
            sums = put(sums, index, ref[at : at + 1, 0:1], ref[at + 1 : at + 2, 0:1])
        pack[...] = jnp.zeros_like(pack)
        at = 0
        for group in range(4):
            count_rows, lanes_used = shapes[group]
            for which in range(3):
                pack[which, at : at + count_rows, 0:lanes_used] = small_refs[3 * group + which][...]
            at += count_rows
        if small_grad is not None:
            pack[3] = small_ref[...]
        else:
            total = chunk_sum([ref.at[0:16] for ref in part_refs], (3 * width, 3 * width + EXTRA))
            pack[3, 0:2, 0:EXTRA] = total[0:2]
            for number in range(7):
                at = 2 + 2 * number
                pack[3, 2 + number : 3 + number, 0:EXTRA] = total[at : at + 1]
                pack[3, 2 + number : 3 + number, EXTRA : 2 * EXTRA] = total[at + 1 : at + 2]
        fn, sn, update = lamb(pack[3], pack[0], pack[1], pack[2])
        su_ref[...] = update
        at = 0
        for group in range(4):
            count_rows, lanes_used = shapes[group]
            small_out[2 * group][...] = fn[at : at + count_rows, 0:lanes_used]
            small_out[2 * group + 1][...] = sn[at : at + count_rows, 0:lanes_used]
            at += count_rows
        weight_rows = jnp.sum(pack[0] * pack[0], axis=1, keepdims=True)
        update_rows = jnp.sum(update * update, axis=1, keepdims=True)
        for index in range(9):
            part = 1.0 if index < 3 else share
            sums = put(
                sums, 6 + index, weight_rows[index : index + 1] * part, update_rows[index : index + 1] * part
            )
        sum_ref[...] = sums

    args = list(parts) + list(attn)
    args += [array for group in small for array in group] + list(early)
    if small_grad is not None:
        args.append(small_grad)
    outs = [out(attn[0].shape)] * 3
    outs += [out(s) for s in shapes for _ in range(2)]
    outs += [out((16, 128)), out((8, 128))]
    return call(
        kernel, 1, [full(*a.shape) for a in args], [full(*o.shape) for o in outs], outs,
        [pltpu.VMEM((4, 16, 128), F32)], us=3.1,
    )(*args)


def finish(sums, matrices, updates, small, small_update, carried):
    shapes = [a.shape for a in small]

    def kernel(*refs):
        sum_ref, refs = refs[0], refs[1:]
        m_refs, u_refs, v_refs, vu_ref = refs[:4], refs[4:8], refs[8:12], refs[12]
        turn, end = moved(refs[13], refs[23], refs[24], refs[25])
        m_outs, v_outs, norm_ref = refs[14:18], refs[18:22], refs[22]
        norms = jnp.sqrt(sum_ref[...])
        trust = 0.5 * (norms[0:1] / (norms[1:2] + 1e-06))
        norm_ref[...] = norms[0:2, 0:15]
        for k in range(3):
            m_outs[0][k] = m_refs[0][k] - trust[:, k : k + 1] * u_refs[0][k]
        for number in range(1, 4):
            at = 2 + number
            m_outs[number][...] = m_refs[number][...] - trust[:, at : at + 1] * u_refs[number][...]
        at = 0
        for group in range(4):
            count_rows, lanes_used = shapes[group]
            for r in range(count_rows):
                factor = trust[:, 6 + at : 7 + at]
                update = vu_ref[at : at + 1, 0:lanes_used]
                v_outs[group][r : r + 1] = v_refs[group][r : r + 1] - factor * update
                at += 1
        turn()
        end()

    args = [sums] + list(matrices) + list(updates) + list(small) + [small_update]
    outs = [out(a.shape) for a in matrices] + [out(s) for s in shapes] + [out((2, 15))]
    return call(
        kernel, 1,
        [full(*a.shape) for a in args] + [ANY],
        [full(*o.shape) for o in outs] + [ANY],
        outs + [out(carried.shape, carried.dtype)],
        [pltpu.VMEM(carried.shape, carried.dtype), pltpu.SemaphoreType.DMA((2,))],
        us=2.6,
    )(*args, carried)


def prepare(attn, mix, up, down_rows, small, inside):
    rows, width = attn.shape[1:]
    units = up.shape[1]
    lanes = 4 * width + (128 if inside else 0)

    def kernel(attn_ref, mix_ref, up_ref, down_ref, *refs):
        attn_out, ffn_out = refs[len(small)], refs[len(small) + 1]
        for k in range(3):
            attn_out[:, k * width : (k + 1) * width] = attn_ref[k].astype(BF)
        attn_out[:, 3 * width : 4 * width] = mix_ref[...].T.astype(BF)
        ffn_out[0:rows] = up_ref[...].astype(BF)
        ffn_out[rows : 2 * rows] = down_ref[...].astype(BF)
        if inside:
            pack = refs[len(small) + 2]
            pack[...] = jnp.zeros_like(pack)
            at = 0
            for ref in refs[: len(small)]:
                pack[at : at + ref.shape[0], 0 : ref.shape[1]] = ref[...]
                at += ref.shape[0]
            attn_out[:, 4 * width :] = pack[...].astype(BF)

    args = [attn, mix, up, down_rows] + list(small)
    outs = [out((rows, lanes), BF), out((2 * rows, units), BF)]
    return call(
        kernel, 1, [full(*a.shape) for a in args], [full(*o.shape) for o in outs], outs,
        [pltpu.VMEM((rows, 128), F32)], us=2.1,
    )(*args)


def pack_rows(arrays):
    rows = [jnp.pad(a, ((0, 0), (0, 128 - a.shape[1]))) for a in arrays]
    total = sum(a.shape[0] for a in arrays)
    rows.append(jnp.zeros((16 - total, 128), F32))
    return jnp.concatenate(rows, axis=0)


def spread_vectors(qkv_sum, wide_grad, sums_one, sums_two, sizes):
    head_own, wide_own, gain_own, dp_size = sizes
    blocks, width = qkv_sum.shape[0], qkv_sum.shape[2] // 3

    def lanes128(array, own):
        array = array.reshape(array.shape[:-1] + (dp_size, own))
        return jnp.pad(array, ((0, 0),) * (array.ndim - 1) + ((0, 128 - own),))

    vectors = jnp.stack(
        [sums_one[0], sums_two[0], sums_one[2], sums_one[1], sums_two[2], sums_two[1]]
    )
    vectors = jnp.broadcast_to(
        lanes128(vectors, gain_own).transpose(1, 0, 2)[None], (blocks, dp_size, 6, 128)
    )
    return jnp.concatenate(
        [
            lanes128(qkv_sum[:, 0, :width], head_own)[:, :, None],
            lanes128(qkv_sum[:, 0, 2 * width :], head_own)[:, :, None],
            lanes128(wide_grad[:, 0], wide_own)[:, :, None],
            vectors,
            jnp.zeros((blocks, dp_size, 7, 128), F32),
        ],
        axis=2,
    )


def on_device(
    dp_size, tensor_size,
    tokens, cotangent, row_lengths, present, groups,
    attn_weight, attn_first, attn_second,
    mix_weight, mix_first, mix_second,
    up_weight, up_first, up_second,
    down_weight, down_first, down_second,
    head_bias, head_first, head_second,
    wide_bias, wide_first, wide_second,
    norm_gains, gain_first, gain_second,
    shift_bias, shift_first, shift_second,
):
    comm = GridComm() if (dp_size, tensor_size) == (8, 4) else GenericComm(dp_size, tensor_size)
    rank = lax.axis_index("tensor")
    row_count, n = groups.shape
    assert row_count == tensor_size
    d = tokens.shape[1]
    width, units = attn_weight.shape[2], up_weight.shape[1]
    head_own, wide_own, gain_own = head_bias.shape[1], wide_bias.shape[0], norm_gains.shape[1]
    small_arrays = [
        (head_bias, head_first, head_second),
        tuple(a.reshape(1, -1) for a in (wide_bias, wide_first, wide_second)),
        (norm_gains, gain_first, gain_second),
        (shift_bias, shift_first, shift_second),
    ]

    down_rows = down_weight.T
    small_masters = [group[0] for group in small_arrays]
    small_all = None
    if not comm.small_inside:
        small_all = comm.gather_small(pack_rows(small_masters).astype(BF).astype(F32))
    attn_shard, ffn_shard = prepare(
        attn_weight, mix_weight, up_weight, down_rows, small_masters, comm.small_inside
    )
    attn_g = comm.gather(attn_shard)
    attn_g.z([])
    attn_g.xy([])
    attn_g.diagonal([])
    attn_w = attn_g.core()
    up_w, down_w = comm.gather_stacked(ffn_shard)

    tok = lax.dynamic_slice_in_dim(tokens, rank * n, n, 0)
    cot = lax.dynamic_slice_in_dim(cotangent, rank * n, n, 0)
    group_row = lax.dynamic_index_in_dim(groups, rank, 0, keepdims=False)
    present_row = lax.dynamic_index_in_dim(present, rank, 0, keepdims=False)
    length = lax.dynamic_index_in_dim(row_lengths, rank, 0, keepdims=False)
    feature_ids = jnp.arange(present_row.shape[0])
    present_key = jnp.sum(
        (group_row[:, None] == feature_ids[None, :]) * present_row[None, :], axis=1
    )
    key_open = ((jnp.arange(n) < length) & (present_key == 1)).astype(jnp.int32)

    qkv, ctx, e, inv, n1, rstd, low, low_t, tok_t, rows, wide_low = attn_fwd(
        attn_w, width, ((head_own, wide_own, gain_own, dp_size), small_all), tok, group_row, key_open
    )
    act, slope = ffn_up(up_w, low, wide_low)
    layer_out, ds2, df, df_t, sums_two = ffn_down(down_w, act, n1, cot, rows)
    layer_out_all = lax.all_gather(layer_out, "tensor", axis=0, tiled=True)

    down_red = comm.reduction([df_t])
    df = tie(df, down_red.core([act]))
    dh, wide_grad, ds1, da, da_t, sums_one = ffn_bwd(up_w, down_w, df, slope, ds2, n1, rstd, rows)
    up_red = comm.reduction([low_t, da_t])
    attn_red = comm.reduction([tok_t])
    sizes = (head_own, wide_own, gain_own, dp_size)
    small_sum = None
    down_lamb = lambda parts: lamb_matrices(
        parts, [(0, False, down_rows, down_first.T, down_second.T)], layer_out_all
    )
    up_lamb = lambda parts: lamb_matrices(
        parts,
        [
            (0, False, up_weight, up_first, up_second),
            (units, True, mix_weight, mix_first, mix_second),
        ],
    )
    if comm.small_inside:
        done = down_red.split([act], deps=[da])
        done = up_red.core([tie(dh, done), ctx])
        da = tie(da, done)
        odd, odd_sum, back = attn_bwd(attn_w, width, (1, 3), da, qkv, ctx, e, inv, ds1, False)
        done = down_red.neighbour([odd])
        done = up_red.split([dh, ctx], deps=done)
        extra = pack_vectors((1, 3), odd_sum, wide_grad, sums_one, sums_two, sizes)
        done = attn_red.core([[([1, 3], odd)]], tie(extra, done))
        da = tie(da, done)
        even, even_sum, back = attn_bwd(attn_w, width, (0, 2), da, qkv, ctx, e, inv, back, True)
        extra = pack_vectors((0, 2), even_sum, wide_grad, sums_one, sums_two, sizes)
        done = attn_red.split([[([0, 2], even)]], extra)
        done = up_red.neighbour(done)
        down_parts = down_red.last(done)
        done = attn_red.neighbour(down_red.done)
        tokens_grad_all = lax.all_gather(tie(back, done), "tensor", axis=0, tiled=True)
        up_parts = up_red.last(done)
        down_parts[1] = tie(down_parts[1], up_red.done)
        down_done = down_lamb(down_parts)
        attn_parts = attn_red.last([down_done[3]])
        up_parts[1] = tie(up_parts[1], attn_red.done)
        up_done = up_lamb(up_parts)
        attn_parts[1] = tie(attn_parts[1], [tokens_grad_all])
    else:
        blocks = range(tensor_size)
        dqkv, dqkv_sum, back = attn_bwd(attn_w, width, blocks, da, qkv, ctx, e, inv, ds1, True)
        tokens_grad_all = lax.all_gather(back, "tensor", axis=0, tiled=True)
        up_red.core([dh, ctx])
        attn_red.core([dqkv])
        down_done, up_done = down_lamb(down_red.last()), up_lamb(up_red.last())
        attn_parts = attn_red.last()
        small_sum = comm.scatter_small(
            spread_vectors(dqkv_sum, wide_grad, sums_one, sums_two, sizes)
        )

    last = lamb_last(
        attn_parts, (attn_weight, attn_first, attn_second), small_sum, small_arrays,
        (up_done[6], down_done[3]), 1.0 / tensor_size,
    )
    small_moments, small_u, sums = last[3:11], last[11], last[12]
    done = finish(
        comm.total(sums),
        (attn_weight, mix_weight, up_weight, down_rows),
        (last[2], up_done[5], up_done[2], down_done[2]),
        small_masters,
        small_u,
        tokens_grad_all,
    )
    moments = [last[0:2], up_done[3:5], up_done[0:2], down_done[0:2]]
    moments += [small_moments[2 * k : 2 * k + 2] for k in range(4)]
    result = [down_done[4], done[9]]
    for number, (first_new, second_new) in enumerate(moments):
        group = [done[number], first_new, second_new]
        if number == 3:
            group = [a.T for a in group]
        result += [a.reshape(-1) for a in group] if number == 5 else group
    return tuple(result) + (done[8],)


def solution(mesh):
    rows = P("dp", None)
    attn, mix, up = P(None, "dp", "tensor"), P("tensor", "dp"), P("dp", "tensor")
    head, wide, col = P(None, ("tensor", "dp")), P(("tensor", "dp")), P(None, "dp")
    params = tuple(spec for spec in (attn, mix, up, mix, head, wide, col, col) for _ in range(3))
    return jax.shard_map(
        functools.partial(on_device, mesh.shape["dp"], mesh.shape["tensor"]),
        mesh=mesh,
        in_specs=(rows, rows, P("dp"), rows, rows) + params,
        out_specs=(rows, rows) + params + (P(),),
        check_vma=False,
    )
```

```python
import functools

import jax
import jax.numpy as jnp
from jax import lax
from jax.experimental import pallas as pl
from jax.experimental.pallas import tpu as pltpu
from jax.sharding import PartitionSpec as P

HEAD = 64
BF = jnp.bfloat16
F32 = jnp.float32
NN = (((1,), (0,)), ((), ()))
NT = (((1,), (1,)), ((), ()))
TN = (((0,), (0,)), ((), ()))
VMEM_LIMIT = 58 << 20
EXTRA = 64
COST = 0.5e9


def mm(a, b, dims):
    return lax.dot_general(a, b, dims, preferred_element_type=F32)


def full(*shape):
    return pl.BlockSpec(shape, lambda i: (0,) * len(shape))


def per(*shape):
    return pl.BlockSpec((1,) + shape, lambda i: (i,) + (0,) * len(shape))


ANY = pl.BlockSpec(memory_space=pl.ANY)
SCALARS = pl.BlockSpec(memory_space=pltpu.SMEM)


def out(shape, dtype=F32):
    return jax.ShapeDtypeStruct(shape, dtype)


def call(kernel, grid, in_specs, out_specs, out_shape, scratch=(), us=2.0):
    return pl.pallas_call(
        kernel,
        grid=(grid,),
        in_specs=in_specs,
        out_specs=out_specs,
        out_shape=out_shape,
        scratch_shapes=list(scratch),
        compiler_params=pltpu.CompilerParams(vmem_limit_bytes=VMEM_LIMIT),
        cost_estimate=pl.CostEstimate(
            flops=int(us * COST), bytes_accessed=1000, transcendentals=0
        ),
    )


class Pieces:
    def __init__(self, arrays, plan, where, blocks, rows, lanes, group=None):
        self.arrays, self.plan, self.where, self.group = arrays, plan, where, group
        self.blocks, self.rows, self.lanes = blocks, rows, lanes

    def scratch(self):
        if self.group is not None:
            shape, count = (self.blocks, 8, self.rows // 8, self.lanes), 1
        elif self.plan is None:
            shape, count = (self.blocks, self.rows, self.lanes), 1
        else:
            shape, count = (self.blocks, 4, 2, self.rows // 8, self.lanes), 4
        return [pltpu.VMEM(shape, BF), pltpu.SemaphoreType.DMA((self.blocks, count))]

    def start(self, refs, where_ref, buffer, sems, ps=None):
        for p in range(self.blocks) if ps is None else ps:
            if self.group is not None:
                source = refs[0].at[:, where_ref[2] ^ p, self.group]
                pltpu.make_async_copy(source, buffer.at[p], sems.at[p, 0]).start()
                continue
            if self.plan is None:
                pltpu.make_async_copy(refs[0].at[p], buffer.at[p], sems.at[p, 0]).start()
                continue
            for number, (array, y_rel, pair_rel) in enumerate(self.plan[p]):
                pair = (where_ref[0] // 2) ^ pair_rel
                target = buffer.at[p, pl.ds(pair * 2, 2), where_ref[1] ^ y_rel]
                pltpu.make_async_copy(refs[array], target, sems.at[p, number]).start()

    def wait(self, refs, p, buffer, sems):
        if self.group is not None:
            source = refs[0].at[:, 0, self.group]
            pltpu.make_async_copy(source, buffer.at[p], sems.at[p, 0]).wait()
            return
        if self.plan is None:
            pltpu.make_async_copy(refs[0].at[0], buffer.at[p], sems.at[p, 0]).wait()
            return
        for number in range(4):
            target = buffer.at[p, pl.ds(0, 2), 0]
            pltpu.make_async_copy(refs[0], target, sems.at[p, number]).wait()

    def read(self, buffer, p, first, last):
        if self.group is not None:
            return buffer[p, :, :, first:last].reshape(self.rows, last - first)
        if self.plan is None:
            return buffer[p, :, first:last]
        return buffer[p, :, :, :, first:last].reshape(self.rows, last - first)


def tie(array, deps):
    return lax.optimization_barrier((array, tuple(deps)))[0] if deps else array


class GenericComm:
    small_inside = False

    def __init__(self, dp, tensor):
        self.dp, self.tensor = dp, tensor
        self.where = jnp.zeros((2,), jnp.int32)

    def gather(self, shard):
        return GenericGather(self, shard)

    def gather_stacked(self, shard):
        rows = shard.shape[0] // 2
        return [GenericGather(self, part).core() for part in (shard[:rows], shard[rows:])]

    def gather_small(self, vector):
        return lax.all_gather(lax.all_gather(vector, "dp", axis=0), "tensor", axis=0)

    def scatter_small(self, vectors):
        own = lax.psum_scatter(vectors, "tensor", scatter_dimension=0)
        return lax.psum_scatter(own, "dp", scatter_dimension=0)

    def total(self, values):
        return lax.psum(values, ("dp", "tensor"))

    def reduction(self, lefts):
        return GenericReduction(self, lefts)

    def block_sets(self):
        return [range(self.tensor)]


class GenericGather:
    def __init__(self, comm, shard):
        self.comm, self.shard = comm, shard

    def z(self, deps):
        return []

    def xy(self, deps):
        return []

    def diagonal(self, deps):
        pass

    def core(self):
        rows = lax.all_gather(self.shard, "dp", axis=0, tiled=True)
        blocks = lax.all_gather(rows, "tensor", axis=0)
        return Pieces([blocks], None, self.comm.where, *blocks.shape)


class GenericReduction:
    def __init__(self, comm, lefts):
        self.comm, self.lefts = comm, lefts

    def core(self, rights):
        self.rights = rights
        return []


    def last(self):
        stacked = grads(list(zip(self.lefts, self.rights)), range(self.comm.tensor))
        own = lax.psum_scatter(stacked, "tensor", scatter_dimension=0)
        return [lax.psum_scatter(own, "dp", scatter_dimension=0, tiled=True).astype(F32)]


class GridComm:
    small_inside = True

    def __init__(self):
        self.z = lax.axis_index("dp") // 2
        self.y = lax.axis_index("dp") % 2
        rank = lax.axis_index("tensor")
        self.where = jnp.stack([self.z, self.y, rank]).astype(jnp.int32)

    @staticmethod
    def send(array, dp_xor, tensor_xor):
        pairs = [
            (d * 4 + t, (d ^ dp_xor) * 4 + (t ^ tensor_xor)) for d in range(8) for t in range(4)
        ]
        return lax.ppermute(array, ("dp", "tensor"), pairs)

    def send_core(self, array):
        return self.send(array, 0, 1)

    def send_x(self, array):
        return self.send(array, 0, 2)

    def send_y(self, array):
        return self.send(array, 1, 0)

    def send_z(self, array, k):
        return self.send(array, 2 * k, 0)

    def gather(self, shard):
        return GridGather(self, shard)

    def gather_stacked(self, shard):
        rows, lanes = shard.shape[0] // 2, shard.shape[1]
        everything = lax.all_gather(shard, ("dp", "tensor"), axis=0, tiled=True)
        everything = everything.reshape(8, 4, 2, rows, lanes)
        return [Pieces([everything], None, self.where, 4, 8 * rows, lanes, g) for g in range(2)]

    def total(self, values):
        values = values + self.send_core(values)
        sent = self.send_x(values), self.send_y(values), self.send(values, 1, 2)
        values = values + sent[0] + (sent[1] + sent[2])
        sent = [self.send_z(values, k) for k in (1, 2, 3)]
        return values + sent[0] + (sent[1] + sent[2])

    def reduction(self, lefts):
        return Reduction(self, lefts)

    def block_sets(self):
        return [(1, 3), (0, 2)]


class GridGather:
    def __init__(self, comm, shard):
        self.comm, self.shard = comm, shard

    def z(self, deps):
        shard = tie(self.shard, deps)
        self.by_z = [shard] + [self.comm.send_z(shard, k) for k in (1, 2, 3)]
        return self.by_z[1:]

    def xy(self, deps):
        low = pair(self.by_z[0], self.by_z[1], self.comm.where)
        high = pair(self.by_z[2], self.by_z[3], self.comm.where)
        low, high = tie(low, deps), tie(high, deps)
        x_low, y_low = self.comm.send_x(low), self.comm.send_y(low)
        x_high, y_high = self.comm.send_x(high), self.comm.send_y(high)
        self.near, self.far = [low, high, y_low, y_high], [x_low, x_high]
        return [x_high, y_high]

    def diagonal(self, deps):
        y_low, x_high = tie(self.near[2], deps), tie(self.far[1], deps)
        self.far += [self.comm.send_x(y_low), self.comm.send_y(x_high)]

    def core(self):
        near_core = [self.comm.send_core(a) for a in self.near]
        far_core = [self.comm.send_core(a) for a in self.far]
        arrays = self.near + near_core + self.far + far_core
        plan = [[(4 * p + c, c // 2, c % 2) for c in range(4)] for p in range(4)]
        rows, lanes = self.shard.shape
        return Pieces(arrays, plan, self.comm.where, 4, 8 * rows, lanes)


class Reduction:
    def __init__(self, comm, lefts):
        self.comm, self.lefts = comm, lefts

    def core(self, rights):
        return self.send_odd(grads(list(zip(self.lefts, rights)), (1, 3)))

    def send_odd(self, odd):
        self.core_got = self.comm.send_core(odd)
        return [odd]

    def split(self, rights, extra=None, deps=()):
        terms = list(zip(self.lefts, rights))
        split = grads_split(terms, tie(self.core_got, deps), self.comm.where, extra)
        x_first, y_first, self.x_second, self.y_second, self.mine = split
        self.x_got, self.y_got = self.comm.send_x(x_first), self.comm.send_y(y_first)
        return [self.mine]

    def neighbour(self, deps=(), us=0.01):
        x_second, y_second = add_low(
            tie(self.x_second, deps), self.y_second, self.x_got, self.y_got, us
        )
        self.x_got2, self.y_got2 = self.comm.send_x(x_second), self.comm.send_y(y_second)
        return [x_second, y_second]

    def last(self, deps=(), us=0.01):
        mine = tie(self.mine, deps)[None]
        low = [(mine, 0), (self.x_got[None], 2), (self.y_got2[None], 0)]
        high = [(mine, 2), (self.y_got[None], 2), (self.x_got2[None], 0)]
        parts = combine([low, high], None, self.comm.where, us)
        self.done = [parts[0]]
        return [parts[0]] + [self.comm.send_z(parts[k], k) for k in (1, 2, 3)]


def pair(first, second, where):
    rows, lanes = first.shape

    def kernel(where_ref, first_ref, second_ref, out_ref):
        odd = where_ref[0] % 2
        out_ref[odd] = first_ref[...]
        out_ref[1 - odd] = second_ref[...]

    return call(
        kernel, 1, [SCALARS, full(rows, lanes), full(rows, lanes)], full(2, rows, lanes),
        out((2, rows, lanes), BF), us=1.8,
    )(where, first, second)


def add_low(x_second, y_second, x_got, y_got, us):
    half = x_second.shape

    def kernel(x_ref, y_ref, xg_ref, yg_ref, xo_ref, yo_ref):
        xo_ref[...] = (x_ref[...].astype(F32) + yg_ref[...].astype(F32)).astype(BF)
        yo_ref[...] = (y_ref[...].astype(F32) + xg_ref[...].astype(F32)).astype(BF)

    return call(
        kernel, 1, [full(*half)] * 4, [full(*half)] * 2, [out(half, BF), out(half, BF)],
        us=us,
    )(x_second, y_second, x_got, y_got)


def block_of(right, p):
    if not isinstance(right, list):
        return right, p
    for ps, array in right:
        if p in ps:
            return array, list(ps).index(p)
    raise KeyError(p)


def grads(terms, ps):
    ps = list(ps)
    d, n = terms[0][0].shape
    firsts = [block_of(right, ps[0]) for _, right in terms]
    steps = [block_of(right, ps[1])[1] - first for (_, right), (_, first) in zip(terms, firsts)]
    lanes = [array.shape[2] for array, _ in firsts]

    def kernel(*refs):
        at = 0
        for number, width in enumerate(lanes):
            left, right = refs[2 * number], refs[2 * number + 1]
            refs[-1][0, :, at : at + width] = mm(left[...], right[0], NN).astype(BF)
            at += width
        if at < wide:
            refs[-1][0, :, at:] = jnp.zeros((d, wide - at), BF)

    specs, args = [], []
    for (left, _), (array, first), step, wide in zip(terms, firsts, steps, lanes):
        specs.append(full(d, n))
        specs.append(
            pl.BlockSpec((1, n, wide), lambda i, first=first, step=step: (first + step * i, 0, 0))
        )
        args += [left, array]
    wide = sum(lanes)
    wide += -wide % 128
    return call(
        kernel, len(ps), specs, per(d, wide), out((len(ps), d, wide), BF),
        us=0.01,
    )(*args)


def split_call(terms, got, where, write, outs, extra=None):
    d, n = terms[0][0].shape
    rows = d // 8
    count = len(terms)
    evens = [[block_of(right, p) for p in (0, 2)] for _, right in terms]
    lanes = [pair[0][0].shape[2] for pair in evens]
    wide = got.shape[2]

    def kernel(where_ref, *refs):
        got_ref = refs[3 * count]
        y = where_ref[1]

        def part(p, y_at):
            at = 0
            columns = []
            for number, width in enumerate(lanes):
                left, right = refs[3 * number], refs[3 * number + 1 + p // 2]
                lhs = left[:, y_at].reshape(4 * rows, n)
                value = mm(lhs, right[0], NN).reshape(4, rows, width)
                value = value + got_ref[p // 2, :, y_at, :, at : at + width].astype(F32)
                columns.append((at, width, value.astype(BF)))
                at += width
            if extra is not None:
                value = got_ref[p // 2, :, y_at, :, at:].astype(F32)
                top = value[:, 0:16] + refs[3 * count + 1][p // 2, :, y_at].astype(F32)
                value = jnp.concatenate([top, value[:, 16:]], axis=1)
                columns.append((at, EXTRA, value.astype(BF)))
            elif at < wide:
                columns.append((at, wide - at, jnp.zeros((4, rows, wide - at), BF)))
            return columns

        write(part, y, refs[3 * count + 1 + (extra is not None) :])

    specs, args = [SCALARS], [where]
    for (left, _), pair, width in zip(terms, evens, lanes):
        specs.append(full(4, 2, rows, n))
        args.append(left.reshape(4, 2, rows, n))
        for array, index in pair:
            specs.append(pl.BlockSpec((1, n, width), lambda i, index=index: (index, 0, 0)))
            args.append(array)
    specs.append(full(2, 4, 2, rows, wide))
    args.append(got.reshape(2, 4, 2, rows, wide))
    if extra is not None:
        specs.append(full(2, 4, 2, 16, EXTRA))
        args.append(extra.reshape(2, 4, 2, 16, EXTRA))
    shapes = [shape + (rows, wide) for shape in outs]
    return call(
        kernel, 1, specs, [full(*shape) for shape in shapes], [out(shape, BF) for shape in shapes],
        us=0.01,
    )(*args)


def grads_split(terms, got, where, extra=None):
    def write(part, y, refs):
        x_first, y_first, x_second, y_second, mine = refs
        for at, width, value in part(2, 1 - y):
            x_first[0:2, :, at : at + width] = value[0:2]
            y_first[0:2, :, at : at + width] = value[2:4]
        for at, width, value in part(2, y):
            x_first[2:4, :, at : at + width] = value[0:2]
            x_second[:, :, at : at + width] = value[2:4]
        for at, width, value in part(0, 1 - y):
            y_first[2:4, :, at : at + width] = value[2:4]
            y_second[:, :, at : at + width] = value[0:2]
        for at, width, value in part(0, y):
            mine[:, :, at : at + width] = value

    return split_call(terms, got, where, write, [(4,), (4,), (2,), (2,), (4,)], extra)


def combine(halves, rows_of, where, us):
    arrays = []
    for array in [array for half in halves for array, _ in half]:
        if not any(array is other for other in arrays):
            arrays.append(array)
    index = lambda array: [array is other for other in arrays].index(True)
    plans = [
        [(index(array), rows_of[h][0] if rows_of else first) for array, first in half]
        for h, half in enumerate(halves)
    ]
    chunk = arrays[0].shape[2:]

    def kernel(where_ref, *refs):
        o0, o1, o2, o3, total = refs[len(arrays) :]
        for h, plan in enumerate(plans):
            for j in range(2):
                number, first = plan[0]
                value = refs[number][0, first + j].astype(F32)
                for number, first in plan[1:]:
                    value = value + refs[number][0, first + j].astype(F32)
                total[2 * h + j] = value
        z = where_ref[0]
        o0[...] = total[z]
        o1[...] = total[z ^ 1].astype(BF)
        o2[...] = total[z ^ 2].astype(BF)
        o3[...] = total[z ^ 3].astype(BF)

    return call(
        kernel, 1,
        [SCALARS] + [full(1, *a.shape[1:]) for a in arrays],
        [full(*chunk)] * 4,
        [out(chunk), out(chunk, BF), out(chunk, BF), out(chunk, BF)],
        [pltpu.VMEM((4,) + chunk, F32)],
        us=us,
    )(where, *arrays)


def norm(summed):
    center = summed - jnp.mean(summed, axis=-1, keepdims=True)
    spread = jnp.mean(center * center, axis=-1, keepdims=True)
    scaled = lax.rsqrt(spread + 1e-05)
    return (center * scaled, scaled)


def norm_back(upstream, normal, scaled):
    inner_sum = (
        upstream
        - jnp.mean(upstream, axis=-1, keepdims=True)
        - normal * jnp.mean(upstream * normal, axis=-1, keepdims=True)
    )
    return scaled * inner_sum


G1, G2, BO, B1, C2, B2 = range(6)


def attn_fwd(pieces, width, small, tok, groups, key_open):
    n, d = tok.shape
    blocks = pieces.blocks
    heads = width // HEAD
    count = len(pieces.arrays)
    (head_own, wide_own, gain_own, dp_size), given = small
    units = wide_own * dp_size

    def kernel(where_ref, tok_ref, gq_ref, gk_ref, open_ref, *refs):
        w_refs, refs = refs[:count], refs[count:]
        if given is not None:
            bias_in, rows_in, wide_in = refs[:3]
            refs = refs[3:]
        qkv_ref, ctx_ref, e_ref, inv_ref, n1_ref, rstd_ref, low_ref, low_t_ref, tok_t_ref = refs[:9]
        rows_ref, wide_ref, att_ref, mask_ref, w_ref, sems = refs[9:]
        step = pl.program_id(0)

        @pl.when(step == 0)
        def _():
            pieces.start(w_refs, where_ref, w_ref, sems)
            seen = (open_ref[...] == 1) | (gq_ref[...] == gk_ref[...])
            mask_ref[...] = jnp.where(seen, 0.0, -1e30)
            att_ref[...] = jnp.zeros_like(att_ref)
            tok_t_ref[...] = tok_ref[...].T

        pieces.wait(w_refs, step, w_ref, sems)
        if given is None:
            first = 4 * width
            vectors = [
                w_ref[step, c // 2, c % 2, 0:16, first : first + 128].astype(F32)
                for c in range(dp_size)
            ]

            def line(row, used):
                return jnp.concatenate([v[row : row + 1, :used] for v in vectors], axis=1)

            bias_q, bias_v = line(0, head_own), line(1, head_own)
            wide_ref[0] = line(2, wide_own)

            @pl.when(step == 0)
            def _():
                for row in range(6):
                    rows_ref[row : row + 1] = line(3 + row, gain_own)

        else:
            bias_q, bias_v = bias_in[0, 0:1], bias_in[0, 1:2]
            wide_ref[0] = wide_in[0]
            rows_ref[0:6] = rows_in[...]

        qkv = mm(tok_ref[...], pieces.read(w_ref, step, 0, 3 * width), NN)
        lane = lax.broadcasted_iota(jnp.int32, (n, 128), 1)
        q_all = (qkv[:, :width] + bias_q).astype(BF)
        k_all = qkv[:, width : 2 * width].astype(BF)
        v_all = (qkv[:, 2 * width :] + bias_v).astype(BF)
        qkv_ref[0] = jnp.concatenate([q_all, k_all, v_all], axis=1)
        contexts = []
        inv_all = jnp.zeros((n, 128), F32)
        for h in range(heads):
            q = q_all[:, h * HEAD : (h + 1) * HEAD] * jnp.asarray(HEAD**-0.5, BF)
            k = k_all[:, h * HEAD : (h + 1) * HEAD]
            v = v_all[:, h * HEAD : (h + 1) * HEAD]
            s = mm(q, k, NT) + mask_ref[...]
            e = jnp.exp(s - jnp.max(s, axis=-1, keepdims=True)).astype(BF)
            e_ref[0, h] = e
            v_one = jnp.concatenate([v, jnp.ones_like(v)], axis=1)
            r = mm(e, v_one, NN)
            inv = 1.0 / r[:, HEAD : HEAD + 1]
            contexts.append((r[:, :HEAD] * inv).astype(BF))
            inv_all = jnp.where(lane == h, inv, inv_all)
        ctx = jnp.concatenate(contexts, axis=1)
        ctx_ref[0] = ctx
        inv_ref[0] = inv_all
        att_ref[...] += mm(ctx, pieces.read(w_ref, step, 3 * width, 4 * width), NT)

        @pl.when(step == blocks - 1)
        def _():
            summed = tok_ref[...].astype(F32) + (att_ref[...] + rows_ref[BO : BO + 1])
            normal, scaled = norm(summed)
            n1_ref[...] = normal
            rstd_ref[...] = scaled
            normed = normal * rows_ref[G1 : G1 + 1] + rows_ref[B1 : B1 + 1]
            low = normed.astype(BF)
            low_ref[...] = low
            low_t_ref[...] = low.T

    specs = [SCALARS, full(n, d), full(n, 1), full(1, n), full(1, n)] + [ANY] * count
    args = [pieces.where, tok, groups.reshape(n, 1), groups.reshape(1, n), key_open.reshape(1, n)]
    args += pieces.arrays
    if given is not None:
        biases = given[:, :, 0:2, :head_own].transpose(0, 2, 1, 3).reshape(blocks, 2, width)
        wide_low = given[:, :, 2, :wide_own].reshape(blocks, 1, units)
        specs += [per(2, width), full(6, d), per(1, units)]
        args += [
            biases, given[0, :, 3:9, :gain_own].transpose(1, 0, 2).reshape(6, d), wide_low,
        ]
    return call(
        kernel, blocks, specs,
        [
            per(n, 3 * width), per(n, width), per(heads, n, n), per(n, 128),
            full(n, d), full(n, 1), full(n, d), full(d, n), full(d, n), full(8, d), per(1, units),
        ],
        [
            out((blocks, n, 3 * width), BF), out((blocks, n, width), BF),
            out((blocks, heads, n, n), BF), out((blocks, n, 128)),
            out((n, d)), out((n, 1)), out((n, d), BF), out((d, n), BF), out((d, n), BF),
            out((8, d)), out((blocks, 1, units)),
        ],
        [pltpu.VMEM((n, d), F32), pltpu.VMEM((n, n), F32)] + pieces.scratch(),
        us=17,
    )(*args)


def ffn_up(pieces, low, wide_bias):
    n, d = low.shape
    blocks, units, count = pieces.blocks, pieces.lanes, len(pieces.arrays)

    def kernel(where_ref, low_ref, bias_ref, *refs):
        w_refs, (act_ref, slope_ref, w_ref, sems) = refs[:count], refs[count:]
        step = pl.program_id(0)

        @pl.when(step == 0)
        def _():
            pieces.start(w_refs, where_ref, w_ref, sems)

        pieces.wait(w_refs, step, w_ref, sems)
        h = mm(low_ref[...], pieces.read(w_ref, step, 0, units), NN) + bias_ref[0]
        cdf = 0.5 * (1.0 + lax.erf(h * (0.5**0.5)))
        act_ref[0] = (h * cdf).astype(BF)
        density = jnp.exp(h * h * -0.5) * 0.3989422804014327
        slope_ref[0] = (cdf + h * density).astype(BF)

    return call(
        kernel, blocks,
        [SCALARS, full(n, d), per(1, units)] + [ANY] * count,
        [per(n, units), per(n, units)],
        [out((blocks, n, units), BF), out((blocks, n, units), BF)],
        pieces.scratch(),
        us=8.5,
    )(pieces.where, low, wide_bias, *pieces.arrays)


def ffn_down(pieces, act, n1, cot, rows):
    n, d = n1.shape
    blocks, units, count = pieces.blocks, pieces.lanes, len(pieces.arrays)

    def kernel(where_ref, act_ref, n1_ref, cot_ref, rows_ref, *refs):
        w_refs, refs = refs[:count], refs[count:]
        y_ref, ds_ref, df_ref, df_t_ref, sum_ref, acc_ref, w_ref, sems = refs
        step = pl.program_id(0)

        @pl.when(step == 0)
        def _():
            pieces.start(w_refs, where_ref, w_ref, sems)
            normed = n1_ref[...] * rows_ref[G1 : G1 + 1] + rows_ref[B1 : B1 + 1]
            acc_ref[...] = normed + rows_ref[C2 : C2 + 1]

        pieces.wait(w_refs, step, w_ref, sems)
        acc_ref[...] += mm(act_ref[0], pieces.read(w_ref, step, 0, units), NT)

        @pl.when(step == blocks - 1)
        def _():
            normal, scaled = norm(acc_ref[...])
            gain = rows_ref[G2 : G2 + 1]
            y_ref[...] = (normal * gain + rows_ref[B2 : B2 + 1]).astype(BF)
            upstream = cot_ref[...].astype(F32)
            ds = norm_back(upstream * gain, normal, scaled)
            ds_ref[...] = ds
            df = ds.astype(BF)
            df_ref[...] = df
            df_t_ref[...] = df.T
            sum_ref[...] = jnp.zeros_like(sum_ref)
            sum_ref[0:1] = jnp.sum(upstream * normal, axis=0, keepdims=True)
            sum_ref[1:2] = jnp.sum(upstream, axis=0, keepdims=True)
            sum_ref[2:3] = jnp.sum(ds, axis=0, keepdims=True)

    return call(
        kernel, blocks,
        [SCALARS, per(n, units), full(n, d), full(n, d), full(*rows.shape)] + [ANY] * count,
        [full(n, d), full(n, d), full(n, d), full(d, n), full(8, d)],
        [out((n, d), BF), out((n, d)), out((n, d), BF), out((d, n), BF), out((8, d))],
        [pltpu.VMEM((n, d), F32)] + pieces.scratch(),
        us=10.5,
    )(pieces.where, act, n1, cot, rows, *pieces.arrays)


def ffn_bwd(up, down, df, slope, ds2, n1, rstd, rows, odd=None):
    n, d = n1.shape
    blocks, units = up.blocks, up.lanes
    up_count, down_count = len(up.arrays), len(down.arrays)
    wide = 0
    if odd is not None:
        width = odd[1].shape[2]
        wide = units + width + -(units + width) % 128

    def kernel(where_ref, df_ref, slope_ref, ds2_ref, n1_ref, rstd_ref, rows_ref, *refs):
        if odd is not None:
            low_t_ref, ctx_ref, refs = refs[0], refs[1], refs[2:]
        up_refs, down_refs = refs[:up_count], refs[up_count : up_count + down_count]
        refs = refs[up_count + down_count :]
        if odd is not None:
            odd_ref, refs = refs[0], refs[1:]
        dh_ref, dc_ref, ds_ref, da_ref, da_t_ref, sum_ref = refs[:6]
        acc_ref, wu_ref, sems_u, wd_ref, sems_d = refs[6:]
        step = pl.program_id(0)

        @pl.when(step == 0)
        def _():
            down.start(down_refs, where_ref, wd_ref, sems_d)
            up.start(up_refs, where_ref, wu_ref, sems_u)
            acc_ref[...] = ds2_ref[...]

        down.wait(down_refs, step, wd_ref, sems_d)
        dact = mm(df_ref[...], down.read(wd_ref, step, 0, units), NN)
        dh = (dact * slope_ref[0].astype(F32)).astype(BF)
        dh_ref[0] = dh
        dc_ref[0] = jnp.sum(dh.astype(F32), axis=0, keepdims=True)
        up.wait(up_refs, step, wu_ref, sems_u)
        acc_ref[...] += mm(dh, up.read(wu_ref, step, 0, units), NT)
        if odd is not None:

            @pl.when(step % 2 == 1)
            def _():
                odd_ref[step // 2, :, 0:units] = mm(low_t_ref[...], dh, NN).astype(BF)

        @pl.when(step == blocks - 1)
        def _():
            dnormed = acc_ref[...]
            normal = n1_ref[...]
            ds = norm_back(dnormed * rows_ref[G1 : G1 + 1], normal, rstd_ref[...])
            ds_ref[...] = ds
            da = ds.astype(BF)
            da_ref[...] = da
            da_t = da.T
            da_t_ref[...] = da_t
            sum_ref[...] = jnp.zeros_like(sum_ref)
            sum_ref[0:1] = jnp.sum(dnormed * normal, axis=0, keepdims=True)
            sum_ref[1:2] = jnp.sum(dnormed, axis=0, keepdims=True)
            sum_ref[2:3] = jnp.sum(ds, axis=0, keepdims=True)
            if odd is not None:
                for k in range(2):
                    part = mm(da_t, ctx_ref[2 * k + 1], NN).astype(BF)
                    odd_ref[k, :, units : units + width] = part
                    odd_ref[k, :, units + width :] = jnp.zeros((d, wide - units - width), BF)

    specs = [SCALARS, full(n, d), per(n, units), full(n, d), full(n, d), full(n, 1), full(*rows.shape)]
    args = [up.where, df, slope, ds2, n1, rstd, rows]
    outs = [
        out((blocks, n, units), BF), out((blocks, 1, units)), out((n, d)),
        out((n, d), BF), out((d, n), BF), out((8, d)),
    ]
    out_specs = [per(n, units), per(1, units), full(n, d), full(n, d), full(d, n), full(8, d)]
    if odd is not None:
        specs += [full(*a.shape) for a in odd]
        args += list(odd)
        outs = [out((2, d, wide), BF)] + outs
        out_specs = [full(2, d, wide)] + out_specs
    return call(
        kernel, blocks, specs + [ANY] * (up_count + down_count), out_specs, outs,
        [pltpu.VMEM((n, d), F32)] + up.scratch() + down.scratch(),
        us=100,
    )(*args, *up.arrays, *down.arrays)


def fill_rows(rows_ref, qkv_sum, wide_row, one_ref, two_ref, sizes):
    head_own, wide_own, gain_own, dp_size = sizes
    width = qkv_sum.shape[1] // 3
    rows_ref[...] = jnp.zeros_like(rows_ref)
    rows = [
        wide_row, one_ref[0:1], two_ref[0:1], one_ref[2:3], one_ref[1:2], two_ref[2:3], two_ref[1:2],
    ]
    for c in range(dp_size):
        for number, first in enumerate((0, 2 * width)):
            first += c * head_own
            rows_ref[c, number : number + 1, 0:head_own] = qkv_sum[:, first : first + head_own]
        for number, row in enumerate(rows):
            own = gain_own if number else wide_own
            at, first = 2 + 2 * number, c * own
            rows_ref[c, at : at + 1, :] = row[:, first : first + EXTRA]
            rest = own - EXTRA
            rows_ref[c, at + 1 : at + 2, 0:rest] = row[:, first + EXTRA : first + own]


def attn_bwd(pieces, width, ps, da, qkv, ctx, e, inv, back, last, vectors=None, tok_t=None):
    n, d = back.shape
    ps = list(ps)
    count = len(pieces.arrays)
    heads = width // HEAD
    stride = ps[1] - ps[0]
    at = lambda i: ps[0] + stride * i

    def kernel(where_ref, da_ref, qkv_ref, ctx_ref, e_ref, inv_ref, back_ref, *refs):
        if vectors is not None:
            wide_ref, one_ref, two_ref, refs = refs[0], refs[1], refs[2], refs[3:]
        if tok_t is not None:
            tok_t_ref, refs = refs[0], refs[1:]
        w_refs, refs = refs[:count], refs[count:]
        if vectors is not None:
            first_ref, rows_ref, refs = refs[0], refs[-1], refs[1:-1]
        dqkv_ref, sum_ref, tg_ref, acc_ref, w_ref, sems = refs
        step = pl.program_id(0)

        @pl.when(step == 0)
        def _():
            pieces.start(w_refs, where_ref, w_ref, sems, ps)
            acc_ref[...] = back_ref[...]

        pieces.wait(w_refs, at(step), w_ref, sems)
        dctx = mm(da_ref[...], pieces.read(w_ref, at(step), 3 * width, 4 * width), NN)
        dctx = dctx.astype(BF).astype(F32)
        scale = HEAD**-0.5
        dos, deltas = [], []
        for h in range(heads):
            do = dctx[:, h * HEAD : (h + 1) * HEAD] * inv_ref[0, :, h : h + 1]
            ctx = ctx_ref[0, :, h * HEAD : (h + 1) * HEAD].astype(F32)
            deltas.append(jnp.sum(do * ctx, axis=-1, keepdims=True))
            dos.append(do.astype(BF))
        do_t = jnp.concatenate(dos, axis=1).T
        q_t = qkv_ref[0, :, 0:width].T
        dqs, dks, dvs = [], [], []
        for h in range(heads):
            k = qkv_ref[0, :, width + h * HEAD : width + (h + 1) * HEAD]
            v = qkv_ref[0, :, 2 * width + h * HEAD : 2 * width + (h + 1) * HEAD]
            e = e_ref[0, h]
            dp = mm(dos[h], v, NT)
            ds = (e.astype(F32) * (dp - deltas[h])).astype(BF)
            dvs.append(mm(do_t[h * HEAD : (h + 1) * HEAD], e, NN))
            dqs.append(mm(ds, k, NN) * scale)
            dks.append(mm(q_t[h * HEAD : (h + 1) * HEAD], ds, NN) * scale)
        dk = jnp.concatenate(dks, axis=0).astype(BF).T
        dv = jnp.concatenate(dvs, axis=0).astype(BF).T
        dqkv = jnp.concatenate([jnp.concatenate(dqs, axis=1).astype(BF), dk, dv], axis=1)
        dqkv_ref[0] = dqkv
        sums = jnp.sum(dqkv.astype(F32), axis=0, keepdims=True)
        sum_ref[0] = sums
        acc_ref[...] += mm(dqkv, pieces.read(w_ref, at(step), 0, 3 * width), NT)
        if vectors is not None:
            fill_rows(rows_ref, sums, wide_ref[0], one_ref, two_ref, vectors[3])
            rows = rows_ref[...].astype(BF)
            if tok_t is None:
                first_ref[0] = rows
            else:
                first_ref[0, :, 0 : 3 * width] = mm(tok_t_ref[...], dqkv, NN).astype(BF)
                first_ref[0, :, 3 * width :] = jnp.zeros((d, EXTRA), BF)
                for c in range(8):
                    first = c * (d // 8)
                    first_ref[0, first : first + 16, 3 * width :] = rows[c]

        @pl.when(step == len(ps) - 1)
        def _():
            tg_ref[...] = acc_ref[...].astype(tg_ref.dtype)

    def of(*shape):
        return pl.BlockSpec((1,) + shape, lambda i: (at(i),) + (0,) * len(shape))

    specs = [SCALARS, full(n, d), of(n, 3 * width), of(n, width), of(heads, n, n), of(n, 128), full(n, d)]
    args = [pieces.where, da, qkv, ctx, e, inv, back]
    out_specs = [per(n, 3 * width), per(1, 3 * width), full(n, d)]
    outs = [
        out((len(ps), n, 3 * width), BF), out((len(ps), 1, 3 * width)), out((n, d), BF if last else F32),
    ]
    scratch = [pltpu.VMEM((n, d), F32)] + pieces.scratch()
    if vectors is not None:
        specs += [of(1, vectors[0].shape[2]), full(*vectors[1].shape), full(*vectors[2].shape)]
        args += list(vectors[:3])
        scratch.append(pltpu.VMEM((8, 16, EXTRA), F32))
        first = (8, 16, EXTRA)
        if tok_t is not None:
            specs.append(full(d, n))
            args.append(tok_t)
            first = (d, 3 * width + EXTRA)
        out_specs = [per(*first)] + out_specs
        outs = [out((len(ps),) + first, BF)] + outs
    return call(
        kernel, len(ps), specs + [ANY] * count, out_specs, outs, scratch, us=100,
    )(*args, *pieces.arrays)


def lamb(gradient, master, first, second):
    first_new = 0.5 * first + 0.5 * gradient
    second_new = 0.5 * second + 0.5 * gradient * gradient
    update = first_new / (jnp.sqrt(second_new) + 1e-06) + 0.01 * master
    return first_new, second_new, update


def whole_sum(array):
    return jnp.sum(jnp.sum(array * array, axis=1, keepdims=True), axis=0, keepdims=True)


def chunk_sum(refs, lanes):
    total = refs[0][:, lanes[0] : lanes[1]]
    for ref in refs[1:]:
        total = total + ref[:, lanes[0] : lanes[1]].astype(F32)
    return total


def moved(source, target, buffer, sems):
    into = pltpu.make_async_copy(source, buffer, sems.at[0])
    back = pltpu.make_async_copy(buffer, target, sems.at[1])
    into.start()

    def turn():
        into.wait()
        back.start()

    return turn, back.wait


def lamb_matrices(parts, entries, carried=None):
    count = len(parts)
    extra = [] if carried is None else [carried]

    def kernel(*refs):
        part_refs = refs[:count]
        ins, refs = refs[count : count + 3 * len(entries)], refs[count + 3 * len(entries) :]
        if extra:
            turn, end = moved(refs[0], refs[1 + 3 * len(entries) + 1], refs[-2], refs[-1])
            refs = refs[1:]
        sum_ref = refs[3 * len(entries)]
        for number, (lane, turned, master, _, _) in enumerate(entries):
            m_ref, f_ref, s_ref = ins[3 * number : 3 * number + 3]
            fn_ref, sn_ref, u_ref = refs[3 * number : 3 * number + 3]
            gradient = chunk_sum(part_refs, (lane, lane + master.shape[0 if turned else 1]))
            if turned:
                gradient = gradient.T
            fn_ref[...], sn_ref[...], update = lamb(gradient, m_ref[...], f_ref[...], s_ref[...])
            u_ref[...] = update
            at = 2 * number
            sum_ref[at : at + 1] = jnp.broadcast_to(whole_sum(m_ref[...]), (1, 128))
            sum_ref[at + 1 : at + 2] = jnp.broadcast_to(whole_sum(update), (1, 128))
        if extra:
            turn()
            end()

    shapes = [entry[2].shape for entry in entries for _ in range(3)]
    args = list(parts) + [array for entry in entries for array in entry[2:]]
    specs = [full(*a.shape) for a in args] + [ANY] * len(extra)
    outs = [out(shape) for shape in shapes] + [out((8, 128))]
    out_specs = [full(*o.shape) for o in outs] + [ANY] * len(extra)
    outs += [out(a.shape, a.dtype) for a in extra]
    scratch = []
    for a in extra:
        scratch = [pltpu.VMEM(a.shape, a.dtype), pltpu.SemaphoreType.DMA((2,))]
    return call(kernel, 1, specs, out_specs, outs, scratch, us=0.01)(*args, *extra)


def lamb_last(parts, attn, small_grad, small, early, share):
    count = len(parts)
    width = attn[0].shape[2]
    shapes = [group[0].shape for group in small]

    def kernel(*refs):
        part_refs, refs = refs[:count], refs[count:]
        m_ref, f_ref, s_ref = refs[:3]
        small_refs, early_refs, refs = refs[3:15], refs[15:17], refs[17:]
        if small_grad is not None:
            small_ref, refs = refs[0], refs[1:]
        fn_ref, sn_ref, u_ref = refs[:3]
        small_out, su_ref, sum_ref, pack = refs[3:11], refs[11], refs[12], refs[13]
        row = lax.broadcasted_iota(jnp.int32, (8, 128), 0)
        lane = lax.broadcasted_iota(jnp.int32, (8, 128), 1)
        sums = jnp.zeros((8, 128), F32)

        def put(sums, index, weight_sq, update_sq):
            sums = jnp.where((row == 0) & (lane == index), weight_sq, sums)
            return jnp.where((row == 1) & (lane == index), update_sq, sums)

        for k in range(3):
            gradient = chunk_sum(part_refs, (k * width, (k + 1) * width))
            fn, sn, update = lamb(gradient, m_ref[k], f_ref[k], s_ref[k])
            fn_ref[k], sn_ref[k], u_ref[k] = fn, sn, update
            sums = put(sums, k, whole_sum(m_ref[k]), whole_sum(update))
        for index, call_index, at in ((3, 0, 2), (4, 0, 0), (5, 1, 0)):
            ref = early_refs[call_index]
            sums = put(sums, index, ref[at : at + 1, 0:1], ref[at + 1 : at + 2, 0:1])
        pack[...] = jnp.zeros_like(pack)
        at = 0
        for group in range(4):
            count_rows, lanes_used = shapes[group]
            for which in range(3):
                pack[which, at : at + count_rows, 0:lanes_used] = small_refs[3 * group + which][...]
            at += count_rows
        if small_grad is not None:
            pack[3] = small_ref[...]
        else:
            total = chunk_sum([ref.at[0:16] for ref in part_refs], (3 * width, 3 * width + EXTRA))
            pack[3, 0:2, 0:EXTRA] = total[0:2]
            for number in range(7):
                at = 2 + 2 * number
                pack[3, 2 + number : 3 + number, 0:EXTRA] = total[at : at + 1]
                pack[3, 2 + number : 3 + number, EXTRA : 2 * EXTRA] = total[at + 1 : at + 2]
        fn, sn, update = lamb(pack[3], pack[0], pack[1], pack[2])
        su_ref[...] = update
        at = 0
        for group in range(4):
            count_rows, lanes_used = shapes[group]
            small_out[2 * group][...] = fn[at : at + count_rows, 0:lanes_used]
            small_out[2 * group + 1][...] = sn[at : at + count_rows, 0:lanes_used]
            at += count_rows
        weight_rows = jnp.sum(pack[0] * pack[0], axis=1, keepdims=True)
        update_rows = jnp.sum(update * update, axis=1, keepdims=True)
        for index in range(9):
            part = 1.0 if index < 3 else share
            sums = put(
                sums, 6 + index, weight_rows[index : index + 1] * part, update_rows[index : index + 1] * part
            )
        sum_ref[...] = sums

    args = list(parts) + list(attn)
    args += [array for group in small for array in group] + list(early)
    if small_grad is not None:
        args.append(small_grad)
    outs = [out(attn[0].shape)] * 3
    outs += [out(s) for s in shapes for _ in range(2)]
    outs += [out((16, 128)), out((8, 128))]
    return call(
        kernel, 1, [full(*a.shape) for a in args], [full(*o.shape) for o in outs], outs,
        [pltpu.VMEM((4, 16, 128), F32)], us=3.1,
    )(*args)


def finish(sums, matrices, updates, small, small_update):
    shapes = [a.shape for a in small]

    def kernel(*refs):
        sum_ref, refs = refs[0], refs[1:]
        m_refs, u_refs, v_refs, vu_ref = refs[:4], refs[4:8], refs[8:12], refs[12]
        m_outs, v_outs, norm_ref = refs[13:17], refs[17:21], refs[21]
        norms = jnp.sqrt(sum_ref[...])
        trust = 0.5 * (norms[0:1] / (norms[1:2] + 1e-06))
        norm_ref[...] = norms[0:2, 0:15]
        for k in range(3):
            m_outs[0][k] = m_refs[0][k] - trust[:, k : k + 1] * u_refs[0][k]
        for number in range(1, 4):
            at = 2 + number
            m_outs[number][...] = m_refs[number][...] - trust[:, at : at + 1] * u_refs[number][...]
        at = 0
        for group in range(4):
            count_rows, lanes_used = shapes[group]
            for r in range(count_rows):
                factor = trust[:, 6 + at : 7 + at]
                update = vu_ref[at : at + 1, 0:lanes_used]
                v_outs[group][r : r + 1] = v_refs[group][r : r + 1] - factor * update
                at += 1

    args = [sums] + list(matrices) + list(updates) + list(small) + [small_update]
    outs = [out(a.shape) for a in matrices] + [out(s) for s in shapes] + [out((2, 15))]
    return call(
        kernel, 1,
        [full(*a.shape) for a in args], [full(*o.shape) for o in outs], outs,
        us=0.01,
    )(*args)


def prepare(attn, mix, up, down_rows, small, inside):
    rows, width = attn.shape[1:]
    units = up.shape[1]
    lanes = 4 * width + (128 if inside else 0)

    def kernel(attn_ref, mix_ref, up_ref, down_ref, *refs):
        attn_out, ffn_out = refs[len(small)], refs[len(small) + 1]
        for k in range(3):
            attn_out[:, k * width : (k + 1) * width] = attn_ref[k].astype(BF)
        attn_out[:, 3 * width : 4 * width] = mix_ref[...].T.astype(BF)
        ffn_out[0:rows] = up_ref[...].astype(BF)
        ffn_out[rows : 2 * rows] = down_ref[...].astype(BF)
        if inside:
            pack = refs[len(small) + 2]
            pack[...] = jnp.zeros_like(pack)
            at = 0
            for ref in refs[: len(small)]:
                pack[at : at + ref.shape[0], 0 : ref.shape[1]] = ref[...]
                at += ref.shape[0]
            attn_out[:, 4 * width :] = pack[...].astype(BF)

    args = [attn, mix, up, down_rows] + list(small)
    outs = [out((rows, lanes), BF), out((2 * rows, units), BF)]
    return call(
        kernel, 1, [full(*a.shape) for a in args], [full(*o.shape) for o in outs], outs,
        [pltpu.VMEM((rows, 128), F32)], us=2.1,
    )(*args)


def pack_rows(arrays):
    rows = [jnp.pad(a, ((0, 0), (0, 128 - a.shape[1]))) for a in arrays]
    total = sum(a.shape[0] for a in arrays)
    rows.append(jnp.zeros((16 - total, 128), F32))
    return jnp.concatenate(rows, axis=0)


def spread_vectors(qkv_sum, wide_grad, sums_one, sums_two, sizes):
    head_own, wide_own, gain_own, dp_size = sizes
    blocks, width = qkv_sum.shape[0], qkv_sum.shape[2] // 3

    def lanes128(array, own):
        array = array.reshape(array.shape[:-1] + (dp_size, own))
        return jnp.pad(array, ((0, 0),) * (array.ndim - 1) + ((0, 128 - own),))

    vectors = jnp.stack(
        [sums_one[0], sums_two[0], sums_one[2], sums_one[1], sums_two[2], sums_two[1]]
    )
    vectors = jnp.broadcast_to(
        lanes128(vectors, gain_own).transpose(1, 0, 2)[None], (blocks, dp_size, 6, 128)
    )
    return jnp.concatenate(
        [
            lanes128(qkv_sum[:, 0, :width], head_own)[:, :, None],
            lanes128(qkv_sum[:, 0, 2 * width :], head_own)[:, :, None],
            lanes128(wide_grad[:, 0], wide_own)[:, :, None],
            vectors,
            jnp.zeros((blocks, dp_size, 7, 128), F32),
        ],
        axis=2,
    )


def on_device(
    dp_size, tensor_size,
    tokens, cotangent, row_lengths, present, groups,
    attn_weight, attn_first, attn_second,
    mix_weight, mix_first, mix_second,
    up_weight, up_first, up_second,
    down_weight, down_first, down_second,
    head_bias, head_first, head_second,
    wide_bias, wide_first, wide_second,
    norm_gains, gain_first, gain_second,
    shift_bias, shift_first, shift_second,
):
    comm = GridComm() if (dp_size, tensor_size) == (8, 4) else GenericComm(dp_size, tensor_size)
    rank = lax.axis_index("tensor")
    row_count, n = groups.shape
    assert row_count == tensor_size
    d = tokens.shape[1]
    width, units = attn_weight.shape[2], up_weight.shape[1]
    head_own, wide_own, gain_own = head_bias.shape[1], wide_bias.shape[0], norm_gains.shape[1]
    small_arrays = [
        (head_bias, head_first, head_second),
        tuple(a.reshape(1, -1) for a in (wide_bias, wide_first, wide_second)),
        (norm_gains, gain_first, gain_second),
        (shift_bias, shift_first, shift_second),
    ]

    down_rows = down_weight.T
    small_masters = [group[0] for group in small_arrays]
    small_all = None
    if not comm.small_inside:
        small_all = comm.gather_small(pack_rows(small_masters).astype(BF).astype(F32))
    attn_shard, ffn_shard = prepare(
        attn_weight, mix_weight, up_weight, down_rows, small_masters, comm.small_inside
    )
    attn_g = comm.gather(attn_shard)
    attn_g.z([])
    attn_g.xy([])
    attn_g.diagonal([])
    attn_w = attn_g.core()
    up_w, down_w = comm.gather_stacked(ffn_shard)

    tok = lax.dynamic_slice_in_dim(tokens, rank * n, n, 0)
    cot = lax.dynamic_slice_in_dim(cotangent, rank * n, n, 0)
    group_row = lax.dynamic_index_in_dim(groups, rank, 0, keepdims=False)
    present_row = lax.dynamic_index_in_dim(present, rank, 0, keepdims=False)
    length = lax.dynamic_index_in_dim(row_lengths, rank, 0, keepdims=False)
    feature_ids = jnp.arange(present_row.shape[0])
    present_key = jnp.sum(
        (group_row[:, None] == feature_ids[None, :]) * present_row[None, :], axis=1
    )
    key_open = ((jnp.arange(n) < length) & (present_key == 1)).astype(jnp.int32)

    qkv, ctx, e, inv, n1, rstd, low, low_t, tok_t, rows, wide_low = attn_fwd(
        attn_w, width, ((head_own, wide_own, gain_own, dp_size), small_all), tok, group_row, key_open
    )
    act, slope = ffn_up(up_w, low, wide_low)
    layer_out, ds2, df, df_t, sums_two = ffn_down(down_w, act, n1, cot, rows)
    layer_out_all = lax.all_gather(layer_out, "tensor", axis=0, tiled=True)

    down_red = comm.reduction([df_t])
    df = tie(df, down_red.core([act]))
    up_red = comm.reduction([low_t, None])
    attn_red = comm.reduction([tok_t])
    sizes = (head_own, wide_own, gain_own, dp_size)
    small_sum = None
    ffn_args = (up_w, down_w, df, slope, ds2, n1, rstd, rows)
    down_entries = [(0, False, down_rows, down_first.T, down_second.T)]
    up_entries = [
        (0, False, up_weight, up_first, up_second),
        (units, True, mix_weight, mix_first, mix_second),
    ]
    if comm.small_inside:
        odd, dh, wide_grad, ds1, da, da_t, sums_one = ffn_bwd(*ffn_args, (low_t, ctx))
        up_red.lefts[1] = da_t
        up_red.send_odd(odd)
        done = down_red.split([act], deps=[da])
        vectors = (wide_grad, sums_one, sums_two, sizes)
        odd, dqkv_odd, _, back = attn_bwd(
            attn_w, width, (1, 3), tie(da, done), qkv, ctx, e, inv, ds1, False, vectors, tok_t
        )
        attn_red.send_odd(odd)
        done = down_red.neighbour([odd, layer_out_all], us=100)
        done = up_red.split([dh, ctx], deps=done + [attn_red.core_got])
        down_parts = down_red.last(done)
        extra, dqkv, _, back = attn_bwd(
            attn_w, width, (0, 2), tie(da, down_red.done), qkv, ctx, e, inv, back, True, vectors
        )
        done = attn_red.split([[([0, 2], dqkv)]], extra)
        down_parts[1] = tie(down_parts[1], done)
        down_done = lamb_matrices(down_parts, down_entries, layer_out_all)
        done = up_red.neighbour(down_done[3:4], us=100)
        done = attn_red.neighbour(done)
        tokens_grad_all = lax.all_gather(tie(back, done), "tensor", axis=0, tiled=True)
        up_parts = up_red.last(done)
        attn_parts = attn_red.last(up_red.done)
        up_parts[1] = tie(up_parts[1], attn_red.done)
        up_done = lamb_matrices(up_parts, up_entries, tokens_grad_all)
    else:
        blocks = range(tensor_size)
        dh, wide_grad, ds1, da, da_t, sums_one = ffn_bwd(*ffn_args)
        up_red.lefts[1] = da_t
        dqkv, dqkv_sum, back = attn_bwd(attn_w, width, blocks, da, qkv, ctx, e, inv, ds1, True)
        tokens_grad_all = lax.all_gather(back, "tensor", axis=0, tiled=True)
        up_red.core([dh, ctx])
        attn_red.core([dqkv])
        down_done = lamb_matrices(down_red.last(), down_entries, layer_out_all)
        up_done = lamb_matrices(up_red.last(), up_entries, tokens_grad_all)
        attn_parts = attn_red.last()
        small_sum = comm.scatter_small(
            spread_vectors(dqkv_sum, wide_grad, sums_one, sums_two, sizes)
        )

    last = lamb_last(
        attn_parts, (attn_weight, attn_first, attn_second), small_sum, small_arrays,
        (up_done[6], down_done[3]), 1.0 / tensor_size,
    )
    small_moments, small_u, sums = last[3:11], last[11], last[12]
    done = finish(
        comm.total(sums),
        (attn_weight, mix_weight, up_weight, down_rows),
        (last[2], up_done[5], up_done[2], down_done[2]),
        small_masters,
        small_u,
    )
    moments = [last[0:2], up_done[3:5], up_done[0:2], down_done[0:2]]
    moments += [small_moments[2 * k : 2 * k + 2] for k in range(4)]
    result = [down_done[4], up_done[7]]
    for number, (first_new, second_new) in enumerate(moments):
        group = [done[number], first_new, second_new]
        if number == 3:
            group = [a.T for a in group]
        result += [a.reshape(-1) for a in group] if number == 5 else group
    return tuple(result) + (done[8],)


def solution(mesh):
    rows = P("dp", None)
    attn, mix, up = P(None, "dp", "tensor"), P("tensor", "dp"), P("dp", "tensor")
    head, wide, col = P(None, ("tensor", "dp")), P(("tensor", "dp")), P(None, "dp")
    params = tuple(spec for spec in (attn, mix, up, mix, head, wide, col, col) for _ in range(3))
    return jax.shard_map(
        functools.partial(on_device, mesh.shape["dp"], mesh.shape["tensor"]),
        mesh=mesh,
        in_specs=(rows, rows, P("dp"), rows, rows) + params,
        out_specs=(rows, rows) + params + (P(),),
        check_vma=False,
    )
```

```python
import functools

import jax
import jax.numpy as jnp
from jax import lax
from jax.experimental import pallas as pl
from jax.experimental.pallas import tpu as pltpu
from jax.sharding import PartitionSpec as P

HEAD = 64
BF = jnp.bfloat16
F32 = jnp.float32
NN = (((1,), (0,)), ((), ()))
NT = (((1,), (1,)), ((), ()))
TN = (((0,), (0,)), ((), ()))
VMEM_LIMIT = 58 << 20
EXTRA = 64
COST = 0.5e9


def mm(a, b, dims):
    return lax.dot_general(a, b, dims, preferred_element_type=F32)


def full(*shape):
    return pl.BlockSpec(shape, lambda i: (0,) * len(shape))


def per(*shape):
    return pl.BlockSpec((1,) + shape, lambda i: (i,) + (0,) * len(shape))


ANY = pl.BlockSpec(memory_space=pl.ANY)
SCALARS = pl.BlockSpec(memory_space=pltpu.SMEM)


def out(shape, dtype=F32):
    return jax.ShapeDtypeStruct(shape, dtype)


def call(kernel, grid, in_specs, out_specs, out_shape, scratch=(), us=2.0):
    return pl.pallas_call(
        kernel,
        grid=(grid,),
        in_specs=in_specs,
        out_specs=out_specs,
        out_shape=out_shape,
        scratch_shapes=list(scratch),
        compiler_params=pltpu.CompilerParams(vmem_limit_bytes=VMEM_LIMIT),
        cost_estimate=pl.CostEstimate(
            flops=int(us * COST), bytes_accessed=1000, transcendentals=0
        ),
    )


class Pieces:
    def __init__(self, arrays, plan, where, blocks, rows, lanes, group=None):
        self.arrays, self.plan, self.where, self.group = arrays, plan, where, group
        self.blocks, self.rows, self.lanes = blocks, rows, lanes

    def scratch(self):
        if self.group is not None:
            shape, count = (self.blocks, 8, self.rows // 8, self.lanes), 1
        elif self.plan is None:
            shape, count = (self.blocks, self.rows, self.lanes), 1
        else:
            shape, count = (self.blocks, 4, 2, self.rows // 8, self.lanes), 4
        return [pltpu.VMEM(shape, BF), pltpu.SemaphoreType.DMA((self.blocks, count))]

    def start(self, refs, where_ref, buffer, sems, ps=None):
        for p in range(self.blocks) if ps is None else ps:
            if self.group is not None:
                source = refs[0].at[:, where_ref[2] ^ p, self.group]
                pltpu.make_async_copy(source, buffer.at[p], sems.at[p, 0]).start()
                continue
            if self.plan is None:
                pltpu.make_async_copy(refs[0].at[p], buffer.at[p], sems.at[p, 0]).start()
                continue
            for number, (array, y_rel, pair_rel) in enumerate(self.plan[p]):
                pair = (where_ref[0] // 2) ^ pair_rel
                target = buffer.at[p, pl.ds(pair * 2, 2), where_ref[1] ^ y_rel]
                pltpu.make_async_copy(refs[array], target, sems.at[p, number]).start()

    def wait(self, refs, p, buffer, sems):
        if self.group is not None:
            source = refs[0].at[:, 0, self.group]
            pltpu.make_async_copy(source, buffer.at[p], sems.at[p, 0]).wait()
            return
        if self.plan is None:
            pltpu.make_async_copy(refs[0].at[0], buffer.at[p], sems.at[p, 0]).wait()
            return
        for number in range(4):
            target = buffer.at[p, pl.ds(0, 2), 0]
            pltpu.make_async_copy(refs[0], target, sems.at[p, number]).wait()

    def read(self, buffer, p, first, last):
        if self.group is not None:
            return buffer[p, :, :, first:last].reshape(self.rows, last - first)
        if self.plan is None:
            return buffer[p, :, first:last]
        return buffer[p, :, :, :, first:last].reshape(self.rows, last - first)


def tie(array, deps):
    return lax.optimization_barrier((array, tuple(deps)))[0] if deps else array


class GenericComm:
    small_inside = False

    def __init__(self, dp, tensor):
        self.dp, self.tensor = dp, tensor
        self.where = jnp.zeros((2,), jnp.int32)

    def gather(self, shard):
        return GenericGather(self, shard)

    def gather_stacked(self, shard):
        rows = shard.shape[0] // 2
        return [GenericGather(self, part).core() for part in (shard[:rows], shard[rows:])]

    def gather_small(self, vector):
        return lax.all_gather(lax.all_gather(vector, "dp", axis=0), "tensor", axis=0)

    def scatter_small(self, vectors):
        own = lax.psum_scatter(vectors, "tensor", scatter_dimension=0)
        return lax.psum_scatter(own, "dp", scatter_dimension=0)

    def total(self, values):
        return lax.psum(values, ("dp", "tensor"))

    def reduction(self, lefts, library=False):
        return GenericReduction(self, lefts)

    def block_sets(self):
        return [range(self.tensor)]


class GenericGather:
    def __init__(self, comm, shard):
        self.comm, self.shard = comm, shard

    def z(self, deps):
        return []

    def xy(self, deps):
        return []

    def diagonal(self, deps):
        pass

    def core(self):
        rows = lax.all_gather(self.shard, "dp", axis=0, tiled=True)
        blocks = lax.all_gather(rows, "tensor", axis=0)
        return Pieces([blocks], None, self.comm.where, *blocks.shape)


class GenericReduction:
    def __init__(self, comm, lefts):
        self.comm, self.lefts = comm, lefts

    def core(self, rights):
        self.rights = rights
        return []


    def last(self):
        stacked = grads(list(zip(self.lefts, self.rights)), range(self.comm.tensor))
        own = lax.psum_scatter(stacked, "tensor", scatter_dimension=0)
        return [lax.psum_scatter(own, "dp", scatter_dimension=0, tiled=True).astype(F32)]


class GridComm:
    small_inside = True

    def __init__(self):
        self.z = lax.axis_index("dp") // 2
        self.y = lax.axis_index("dp") % 2
        rank = lax.axis_index("tensor")
        self.where = jnp.stack([self.z, self.y, rank]).astype(jnp.int32)

    @staticmethod
    def send(array, dp_xor, tensor_xor):
        pairs = [
            (d * 4 + t, (d ^ dp_xor) * 4 + (t ^ tensor_xor)) for d in range(8) for t in range(4)
        ]
        return lax.ppermute(array, ("dp", "tensor"), pairs)

    def send_core(self, array):
        return self.send(array, 0, 1)

    def send_x(self, array):
        return self.send(array, 0, 2)

    def send_y(self, array):
        return self.send(array, 1, 0)

    def send_z(self, array, k):
        return self.send(array, 2 * k, 0)

    def gather(self, shard):
        return GridGather(self, shard)

    @staticmethod
    def sum_z(chunks):
        rows = chunks.reshape((-1, chunks.shape[2]))
        groups = [[2 * z + y for z in range(4)] for y in range(2)]
        return lax.psum_scatter(
            rows, "dp", scatter_dimension=0, axis_index_groups=groups, tiled=True
        )

    def gather_stacked(self, shard):
        rows, lanes = shard.shape[0] // 2, shard.shape[1]
        everything = lax.all_gather(shard, ("dp", "tensor"), axis=0, tiled=True)
        everything = everything.reshape(8, 4, 2, rows, lanes)
        return [Pieces([everything], None, self.where, 4, 8 * rows, lanes, g) for g in range(2)]

    def total(self, values):
        values = values + self.send_core(values)
        sent = self.send_x(values), self.send_y(values), self.send(values, 1, 2)
        values = values + sent[0] + (sent[1] + sent[2])
        sent = [self.send_z(values, k) for k in (1, 2, 3)]
        return values + sent[0] + (sent[1] + sent[2])

    def reduction(self, lefts, library=False):
        return Reduction(self, lefts, library)

    def block_sets(self):
        return [(1, 3), (0, 2)]


class GridGather:
    def __init__(self, comm, shard):
        self.comm, self.shard = comm, shard

    def z(self, deps):
        shard = tie(self.shard, deps)
        self.by_z = [shard] + [self.comm.send_z(shard, k) for k in (1, 2, 3)]
        return self.by_z[1:]

    def xy(self, deps):
        low = pair(self.by_z[0], self.by_z[1], self.comm.where)
        high = pair(self.by_z[2], self.by_z[3], self.comm.where)
        low, high = tie(low, deps), tie(high, deps)
        x_low, y_low = self.comm.send_x(low), self.comm.send_y(low)
        x_high, y_high = self.comm.send_x(high), self.comm.send_y(high)
        self.near, self.far = [low, high, y_low, y_high], [x_low, x_high]
        return [x_high, y_high]

    def diagonal(self, deps):
        y_low, x_high = tie(self.near[2], deps), tie(self.far[1], deps)
        self.far += [self.comm.send_x(y_low), self.comm.send_y(x_high)]

    def core(self):
        near_core = [self.comm.send_core(a) for a in self.near]
        far_core = [self.comm.send_core(a) for a in self.far]
        arrays = self.near + near_core + self.far + far_core
        plan = [[(4 * p + c, c // 2, c % 2) for c in range(4)] for p in range(4)]
        rows, lanes = self.shard.shape
        return Pieces(arrays, plan, self.comm.where, 4, 8 * rows, lanes)


class Reduction:
    def __init__(self, comm, lefts, library):
        self.comm, self.lefts, self.library = comm, lefts, library

    def core(self, rights):
        return self.send_odd(grads(list(zip(self.lefts, rights)), (1, 3)))

    def send_odd(self, odd):
        self.core_got = self.comm.send_core(odd)
        return [odd]

    def split(self, rights, extra=None, deps=()):
        terms = list(zip(self.lefts, rights))
        split = grads_split(terms, tie(self.core_got, deps), self.comm.where, extra)
        x_first, y_first, self.x_second, self.y_second, self.mine = split
        self.x_got, self.y_got = self.comm.send_x(x_first), self.comm.send_y(y_first)
        return [self.mine]

    def neighbour(self, deps=(), us=0.01):
        x_second, y_second = add_low(
            tie(self.x_second, deps), self.y_second, self.x_got, self.y_got, us
        )
        self.x_got2, self.y_got2 = self.comm.send_x(x_second), self.comm.send_y(y_second)
        return [x_second, y_second]

    def last(self, deps=(), us=0.01):
        mine = tie(self.mine, deps)[None]
        low = [(mine, 0), (self.x_got[None], 2), (self.y_got2[None], 0)]
        high = [(mine, 2), (self.y_got[None], 2), (self.x_got2[None], 0)]
        parts = combine([low, high], self.comm.where, us, self.library)
        self.done = [parts[0]]
        if self.library:
            return [self.comm.sum_z(parts[0])]
        return [parts[0]] + [self.comm.send_z(parts[k], k) for k in (1, 2, 3)]


def pair(first, second, where):
    rows, lanes = first.shape

    def kernel(where_ref, first_ref, second_ref, out_ref):
        odd = where_ref[0] % 2
        out_ref[odd] = first_ref[...]
        out_ref[1 - odd] = second_ref[...]

    return call(
        kernel, 1, [SCALARS, full(rows, lanes), full(rows, lanes)], full(2, rows, lanes),
        out((2, rows, lanes), BF), us=1.8,
    )(where, first, second)


def add_low(x_second, y_second, x_got, y_got, us):
    half = x_second.shape

    def kernel(x_ref, y_ref, xg_ref, yg_ref, xo_ref, yo_ref):
        xo_ref[...] = (x_ref[...].astype(F32) + yg_ref[...].astype(F32)).astype(BF)
        yo_ref[...] = (y_ref[...].astype(F32) + xg_ref[...].astype(F32)).astype(BF)

    return call(
        kernel, 1, [full(*half)] * 4, [full(*half)] * 2, [out(half, BF), out(half, BF)],
        us=us,
    )(x_second, y_second, x_got, y_got)


def block_of(right, p):
    if not isinstance(right, list):
        return right, p
    for ps, array in right:
        if p in ps:
            return array, list(ps).index(p)
    raise KeyError(p)


def grads(terms, ps):
    ps = list(ps)
    d, n = terms[0][0].shape
    firsts = [block_of(right, ps[0]) for _, right in terms]
    steps = [block_of(right, ps[1])[1] - first for (_, right), (_, first) in zip(terms, firsts)]
    lanes = [array.shape[2] for array, _ in firsts]

    def kernel(*refs):
        at = 0
        for number, width in enumerate(lanes):
            left, right = refs[2 * number], refs[2 * number + 1]
            refs[-1][0, :, at : at + width] = mm(left[...], right[0], NN).astype(BF)
            at += width
        if at < wide:
            refs[-1][0, :, at:] = jnp.zeros((d, wide - at), BF)

    specs, args = [], []
    for (left, _), (array, first), step, wide in zip(terms, firsts, steps, lanes):
        specs.append(full(d, n))
        specs.append(
            pl.BlockSpec((1, n, wide), lambda i, first=first, step=step: (first + step * i, 0, 0))
        )
        args += [left, array]
    wide = sum(lanes)
    wide += -wide % 128
    return call(
        kernel, len(ps), specs, per(d, wide), out((len(ps), d, wide), BF),
        us=0.01,
    )(*args)


def split_call(terms, got, where, write, outs, extra=None):
    d, n = terms[0][0].shape
    rows = d // 8
    count = len(terms)
    evens = [[block_of(right, p) for p in (0, 2)] for _, right in terms]
    lanes = [pair[0][0].shape[2] for pair in evens]
    wide = got.shape[2]

    def kernel(where_ref, *refs):
        got_ref = refs[3 * count]
        y = where_ref[1]

        def part(p, y_at):
            at = 0
            columns = []
            for number, width in enumerate(lanes):
                left, right = refs[3 * number], refs[3 * number + 1 + p // 2]
                lhs = left[:, y_at].reshape(4 * rows, n)
                value = mm(lhs, right[0], NN).reshape(4, rows, width)
                value = value + got_ref[p // 2, :, y_at, :, at : at + width].astype(F32)
                columns.append((at, width, value.astype(BF)))
                at += width
            if extra is not None:
                value = got_ref[p // 2, :, y_at, :, at:].astype(F32)
                top = value[:, 0:16] + refs[3 * count + 1][p // 2, :, y_at].astype(F32)
                value = jnp.concatenate([top, value[:, 16:]], axis=1)
                columns.append((at, EXTRA, value.astype(BF)))
            elif at < wide:
                columns.append((at, wide - at, jnp.zeros((4, rows, wide - at), BF)))
            return columns

        write(part, y, refs[3 * count + 1 + (extra is not None) :])

    specs, args = [SCALARS], [where]
    for (left, _), pair, width in zip(terms, evens, lanes):
        specs.append(full(4, 2, rows, n))
        args.append(left.reshape(4, 2, rows, n))
        for array, index in pair:
            specs.append(pl.BlockSpec((1, n, width), lambda i, index=index: (index, 0, 0)))
            args.append(array)
    specs.append(full(2, 4, 2, rows, wide))
    args.append(got.reshape(2, 4, 2, rows, wide))
    if extra is not None:
        specs.append(full(2, 4, 2, 16, EXTRA))
        args.append(extra.reshape(2, 4, 2, 16, EXTRA))
    shapes = [shape + (rows, wide) for shape in outs]
    return call(
        kernel, 1, specs, [full(*shape) for shape in shapes], [out(shape, BF) for shape in shapes],
        us=0.01,
    )(*args)


def grads_split(terms, got, where, extra=None):
    def write(part, y, refs):
        x_first, y_first, x_second, y_second, mine = refs
        for at, width, value in part(2, 1 - y):
            x_first[0:2, :, at : at + width] = value[0:2]
            y_first[0:2, :, at : at + width] = value[2:4]
        for at, width, value in part(2, y):
            x_first[2:4, :, at : at + width] = value[0:2]
            x_second[:, :, at : at + width] = value[2:4]
        for at, width, value in part(0, 1 - y):
            y_first[2:4, :, at : at + width] = value[2:4]
            y_second[:, :, at : at + width] = value[0:2]
        for at, width, value in part(0, y):
            mine[:, :, at : at + width] = value

    return split_call(terms, got, where, write, [(4,), (4,), (2,), (2,), (4,)], extra)


def combine(halves, where, us, whole):
    arrays = []
    for array in [array for half in halves for array, _ in half]:
        if not any(array is other for other in arrays):
            arrays.append(array)
    index = lambda array: [array is other for other in arrays].index(True)
    plans = [[(index(array), first) for array, first in half] for half in halves]
    chunk = arrays[0].shape[2:]

    def kernel(where_ref, *refs):
        outs, total = refs[len(arrays) :], refs[-1]
        for h, plan in enumerate(plans):
            for j in range(2):
                number, first = plan[0]
                value = refs[number][0, first + j].astype(F32)
                for number, first in plan[1:]:
                    value = value + refs[number][0, first + j].astype(F32)
                total[2 * h + j] = value.astype(total.dtype)
        if not whole:
            z = where_ref[0]
            outs[0][...] = total[z]
            for k in (1, 2, 3):
                outs[k][...] = total[z ^ k].astype(BF)

    outs = [out((4,) + chunk, BF)] if whole else [out(chunk)] + [out(chunk, BF)] * 3
    return call(
        kernel, 1,
        [SCALARS] + [full(*a.shape) for a in arrays],
        [full(*o.shape) for o in outs], outs,
        [] if whole else [pltpu.VMEM((4,) + chunk, F32)],
        us=us,
    )(where, *arrays)


def norm(summed):
    center = summed - jnp.mean(summed, axis=-1, keepdims=True)
    spread = jnp.mean(center * center, axis=-1, keepdims=True)
    scaled = lax.rsqrt(spread + 1e-05)
    return (center * scaled, scaled)


def norm_back(upstream, normal, scaled):
    inner_sum = (
        upstream
        - jnp.mean(upstream, axis=-1, keepdims=True)
        - normal * jnp.mean(upstream * normal, axis=-1, keepdims=True)
    )
    return scaled * inner_sum


G1, G2, BO, B1, C2, B2 = range(6)


def attn_fwd(pieces, width, small, tok, groups, key_open):
    n, d = tok.shape
    blocks = pieces.blocks
    heads = width // HEAD
    count = len(pieces.arrays)
    (head_own, wide_own, gain_own, dp_size), given = small
    units = wide_own * dp_size

    def kernel(where_ref, tok_ref, gq_ref, gk_ref, open_ref, *refs):
        w_refs, refs = refs[:count], refs[count:]
        if given is not None:
            bias_in, rows_in, wide_in = refs[:3]
            refs = refs[3:]
        qkv_ref, ctx_ref, e_ref, inv_ref, n1_ref, rstd_ref, low_ref, low_t_ref, tok_t_ref = refs[:9]
        rows_ref, wide_ref, att_ref, mask_ref, w_ref, sems = refs[9:]
        step = pl.program_id(0)

        @pl.when(step == 0)
        def _():
            pieces.start(w_refs, where_ref, w_ref, sems)
            seen = (open_ref[...] == 1) | (gq_ref[...] == gk_ref[...])
            mask_ref[...] = jnp.where(seen, 0.0, -1e30)
            att_ref[...] = jnp.zeros_like(att_ref)
            tok_t_ref[...] = tok_ref[...].T

        pieces.wait(w_refs, step, w_ref, sems)
        if given is None:
            first = 4 * width
            vectors = [
                w_ref[step, c // 2, c % 2, 0:16, first : first + 128].astype(F32)
                for c in range(dp_size)
            ]

            def line(row, used):
                return jnp.concatenate([v[row : row + 1, :used] for v in vectors], axis=1)

            bias_q, bias_v = line(0, head_own), line(1, head_own)
            wide_ref[0] = line(2, wide_own)

            @pl.when(step == 0)
            def _():
                for row in range(6):
                    rows_ref[row : row + 1] = line(3 + row, gain_own)

        else:
            bias_q, bias_v = bias_in[0, 0:1], bias_in[0, 1:2]
            wide_ref[0] = wide_in[0]
            rows_ref[0:6] = rows_in[...]

        qkv = mm(tok_ref[...], pieces.read(w_ref, step, 0, 3 * width), NN)
        lane = lax.broadcasted_iota(jnp.int32, (n, 128), 1)
        q_all = (qkv[:, :width] + bias_q).astype(BF)
        k_all = qkv[:, width : 2 * width].astype(BF)
        v_all = (qkv[:, 2 * width :] + bias_v).astype(BF)
        qkv_ref[0] = jnp.concatenate([q_all, k_all, v_all], axis=1)
        contexts = []
        inv_all = jnp.zeros((n, 128), F32)
        for h in range(heads):
            q = q_all[:, h * HEAD : (h + 1) * HEAD] * jnp.asarray(HEAD**-0.5, BF)
            k = k_all[:, h * HEAD : (h + 1) * HEAD]
            v = v_all[:, h * HEAD : (h + 1) * HEAD]
            s = mm(q, k, NT) + mask_ref[...]
            e = jnp.exp(s - jnp.max(s, axis=-1, keepdims=True)).astype(BF)
            e_ref[0, h] = e
            v_one = jnp.concatenate([v, jnp.ones_like(v)], axis=1)
            r = mm(e, v_one, NN)
            inv = 1.0 / r[:, HEAD : HEAD + 1]
            contexts.append((r[:, :HEAD] * inv).astype(BF))
            inv_all = jnp.where(lane == h, inv, inv_all)
        ctx = jnp.concatenate(contexts, axis=1)
        ctx_ref[0] = ctx
        inv_ref[0] = inv_all
        att_ref[...] += mm(ctx, pieces.read(w_ref, step, 3 * width, 4 * width), NT)

        @pl.when(step == blocks - 1)
        def _():
            summed = tok_ref[...].astype(F32) + (att_ref[...] + rows_ref[BO : BO + 1])
            normal, scaled = norm(summed)
            n1_ref[...] = normal
            rstd_ref[...] = scaled
            normed = normal * rows_ref[G1 : G1 + 1] + rows_ref[B1 : B1 + 1]
            low = normed.astype(BF)
            low_ref[...] = low
            low_t_ref[...] = low.T

    specs = [SCALARS, full(n, d), full(n, 1), full(1, n), full(1, n)] + [ANY] * count
    args = [pieces.where, tok, groups.reshape(n, 1), groups.reshape(1, n), key_open.reshape(1, n)]
    args += pieces.arrays
    if given is not None:
        biases = given[:, :, 0:2, :head_own].transpose(0, 2, 1, 3).reshape(blocks, 2, width)
        wide_low = given[:, :, 2, :wide_own].reshape(blocks, 1, units)
        specs += [per(2, width), full(6, d), per(1, units)]
        args += [
            biases, given[0, :, 3:9, :gain_own].transpose(1, 0, 2).reshape(6, d), wide_low,
        ]
    return call(
        kernel, blocks, specs,
        [
            per(n, 3 * width), per(n, width), per(heads, n, n), per(n, 128),
            full(n, d), full(n, 1), full(n, d), full(d, n), full(d, n), full(8, d), per(1, units),
        ],
        [
            out((blocks, n, 3 * width), BF), out((blocks, n, width), BF),
            out((blocks, heads, n, n), BF), out((blocks, n, 128)),
            out((n, d)), out((n, 1)), out((n, d), BF), out((d, n), BF), out((d, n), BF),
            out((8, d)), out((blocks, 1, units)),
        ],
        [pltpu.VMEM((n, d), F32), pltpu.VMEM((n, n), F32)] + pieces.scratch(),
        us=17,
    )(*args)


def ffn_fwd(up, down, low, wide_bias, n1, cot, rows, with_odd):
    n, d = low.shape
    blocks, units = up.blocks, up.lanes
    up_count, down_count = len(up.arrays), len(down.arrays)

    def kernel(where_ref, low_ref, bias_ref, n1_ref, cot_ref, rows_ref, *refs):
        up_refs, down_refs = refs[:up_count], refs[up_count : up_count + down_count]
        refs = refs[up_count + down_count :]
        if with_odd:
            odd_ref, kept_ref, refs = refs[0], refs[-1], refs[1:-1]
        act_ref, slope_ref, y_ref, ds_ref, df_ref, df_t_ref, sum_ref = refs[:7]
        acc_ref, wu_ref, sems_u, wd_ref, sems_d = refs[7:]
        step = pl.program_id(0)

        @pl.when(step == 0)
        def _():
            up.start(up_refs, where_ref, wu_ref, sems_u)
            down.start(down_refs, where_ref, wd_ref, sems_d)
            normed = n1_ref[...] * rows_ref[G1 : G1 + 1] + rows_ref[B1 : B1 + 1]
            acc_ref[...] = normed + rows_ref[C2 : C2 + 1]

        up.wait(up_refs, step, wu_ref, sems_u)
        h = mm(low_ref[...], up.read(wu_ref, step, 0, units), NN) + bias_ref[0]
        cdf = 0.5 * (1.0 + lax.erf(h * (0.5**0.5)))
        act = (h * cdf).astype(BF)
        act_ref[0] = act
        density = jnp.exp(h * h * -0.5) * 0.3989422804014327
        slope_ref[0] = (cdf + h * density).astype(BF)
        if with_odd:

            @pl.when(step % 2 == 1)
            def _():
                kept_ref[step // 2] = act

        down.wait(down_refs, step, wd_ref, sems_d)
        acc_ref[...] += mm(act, down.read(wd_ref, step, 0, units), NT)

        @pl.when(step == blocks - 1)
        def _():
            normal, scaled = norm(acc_ref[...])
            gain = rows_ref[G2 : G2 + 1]
            y_ref[...] = (normal * gain + rows_ref[B2 : B2 + 1]).astype(BF)
            upstream = cot_ref[...].astype(F32)
            ds = norm_back(upstream * gain, normal, scaled)
            ds_ref[...] = ds
            df = ds.astype(BF)
            df_ref[...] = df
            df_t = df.T
            df_t_ref[...] = df_t
            sum_ref[...] = jnp.zeros_like(sum_ref)
            sum_ref[0:1] = jnp.sum(upstream * normal, axis=0, keepdims=True)
            sum_ref[1:2] = jnp.sum(upstream, axis=0, keepdims=True)
            sum_ref[2:3] = jnp.sum(ds, axis=0, keepdims=True)
            if with_odd:
                for k in range(2):
                    odd_ref[k] = mm(df_t, kept_ref[k], NN).astype(BF)

    outs = [
        out((blocks, n, units), BF), out((blocks, n, units), BF), out((n, d), BF), out((n, d)),
        out((n, d), BF), out((d, n), BF), out((8, d)),
    ]
    out_specs = [
        per(n, units), per(n, units), full(n, d), full(n, d), full(n, d), full(d, n), full(8, d),
    ]
    scratch = [pltpu.VMEM((n, d), F32)] + up.scratch() + down.scratch()
    if with_odd:
        outs = [out((2, d, units), BF)] + outs
        out_specs = [full(2, d, units)] + out_specs
        scratch.append(pltpu.VMEM((2, n, units), BF))
    return call(
        kernel, blocks,
        [SCALARS, full(n, d), per(1, units), full(n, d), full(n, d), full(*rows.shape)]
        + [ANY] * (up_count + down_count),
        out_specs, outs, scratch, us=20,
    )(up.where, low, wide_bias, n1, cot, rows, *up.arrays, *down.arrays)


def ffn_bwd(up, down, df, slope, ds2, n1, rstd, rows, odd=None):
    n, d = n1.shape
    blocks, units = up.blocks, up.lanes
    up_count, down_count = len(up.arrays), len(down.arrays)
    wide = 0
    if odd is not None:
        width = odd[1].shape[2]
        wide = units + width + -(units + width) % 128

    def kernel(where_ref, df_ref, slope_ref, ds2_ref, n1_ref, rstd_ref, rows_ref, *refs):
        if odd is not None:
            low_t_ref, ctx_ref, refs = refs[0], refs[1], refs[2:]
        up_refs, down_refs = refs[:up_count], refs[up_count : up_count + down_count]
        refs = refs[up_count + down_count :]
        if odd is not None:
            odd_ref, refs = refs[0], refs[1:]
        dh_ref, dc_ref, ds_ref, da_ref, da_t_ref, sum_ref = refs[:6]
        acc_ref, wu_ref, sems_u, wd_ref, sems_d = refs[6:]
        step = pl.program_id(0)

        @pl.when(step == 0)
        def _():
            down.start(down_refs, where_ref, wd_ref, sems_d)
            up.start(up_refs, where_ref, wu_ref, sems_u)
            acc_ref[...] = ds2_ref[...]

        down.wait(down_refs, step, wd_ref, sems_d)
        dact = mm(df_ref[...], down.read(wd_ref, step, 0, units), NN)
        dh = (dact * slope_ref[0].astype(F32)).astype(BF)
        dh_ref[0] = dh
        dc_ref[0] = jnp.sum(dh.astype(F32), axis=0, keepdims=True)
        up.wait(up_refs, step, wu_ref, sems_u)
        acc_ref[...] += mm(dh, up.read(wu_ref, step, 0, units), NT)
        if odd is not None:

            @pl.when(step % 2 == 1)
            def _():
                odd_ref[step // 2, :, 0:units] = mm(low_t_ref[...], dh, NN).astype(BF)

        @pl.when(step == blocks - 1)
        def _():
            dnormed = acc_ref[...]
            normal = n1_ref[...]
            ds = norm_back(dnormed * rows_ref[G1 : G1 + 1], normal, rstd_ref[...])
            ds_ref[...] = ds
            da = ds.astype(BF)
            da_ref[...] = da
            da_t = da.T
            da_t_ref[...] = da_t
            sum_ref[...] = jnp.zeros_like(sum_ref)
            sum_ref[0:1] = jnp.sum(dnormed * normal, axis=0, keepdims=True)
            sum_ref[1:2] = jnp.sum(dnormed, axis=0, keepdims=True)
            sum_ref[2:3] = jnp.sum(ds, axis=0, keepdims=True)
            if odd is not None:
                for k in range(2):
                    part = mm(da_t, ctx_ref[2 * k + 1], NN).astype(BF)
                    odd_ref[k, :, units : units + width] = part
                    odd_ref[k, :, units + width :] = jnp.zeros((d, wide - units - width), BF)

    specs = [SCALARS, full(n, d), per(n, units), full(n, d), full(n, d), full(n, 1), full(*rows.shape)]
    args = [up.where, df, slope, ds2, n1, rstd, rows]
    outs = [
        out((blocks, n, units), BF), out((blocks, 1, units)), out((n, d)),
        out((n, d), BF), out((d, n), BF), out((8, d)),
    ]
    out_specs = [per(n, units), per(1, units), full(n, d), full(n, d), full(d, n), full(8, d)]
    if odd is not None:
        specs += [full(*a.shape) for a in odd]
        args += list(odd)
        outs = [out((2, d, wide), BF)] + outs
        out_specs = [full(2, d, wide)] + out_specs
    return call(
        kernel, blocks, specs + [ANY] * (up_count + down_count), out_specs, outs,
        [pltpu.VMEM((n, d), F32)] + up.scratch() + down.scratch(),
        us=100,
    )(*args, *up.arrays, *down.arrays)


def fill_rows(rows_ref, qkv_sum, wide_row, one_ref, two_ref, sizes):
    head_own, wide_own, gain_own, dp_size = sizes
    width = qkv_sum.shape[1] // 3
    rows_ref[...] = jnp.zeros_like(rows_ref)
    rows = [
        wide_row, one_ref[0:1], two_ref[0:1], one_ref[2:3], one_ref[1:2], two_ref[2:3], two_ref[1:2],
    ]
    for c in range(dp_size):
        for number, first in enumerate((0, 2 * width)):
            first += c * head_own
            rows_ref[c, number : number + 1, 0:head_own] = qkv_sum[:, first : first + head_own]
        for number, row in enumerate(rows):
            own = gain_own if number else wide_own
            at, first = 2 + 2 * number, c * own
            rows_ref[c, at : at + 1, :] = row[:, first : first + EXTRA]
            rest = own - EXTRA
            rows_ref[c, at + 1 : at + 2, 0:rest] = row[:, first + EXTRA : first + own]


def attn_bwd(pieces, width, ps, da, qkv, ctx, e, inv, back, last, vectors=None, tok_t=None, carried=None):
    n, d = back.shape
    ps = list(ps)
    count = len(pieces.arrays)
    heads = width // HEAD
    stride = ps[1] - ps[0]
    at = lambda i: ps[0] + stride * i

    def kernel(where_ref, da_ref, qkv_ref, ctx_ref, e_ref, inv_ref, back_ref, *refs):
        if vectors is not None:
            wide_ref, one_ref, two_ref, refs = refs[0], refs[1], refs[2], refs[3:]
        if tok_t is not None:
            tok_t_ref, refs = refs[0], refs[1:]
        w_refs, refs = refs[:count], refs[count:]
        if carried is not None:
            source_ref, target_ref, buffer_ref, copy_sems = refs[0], refs[5], refs[-2], refs[-1]
            refs = refs[1:5] + refs[6:-2]
        if vectors is not None:
            first_ref, rows_ref, refs = refs[0], refs[-1], refs[1:-1]
        dqkv_ref, sum_ref, tg_ref, acc_ref, w_ref, sems = refs
        step = pl.program_id(0)

        @pl.when(step == 0)
        def _():
            pieces.start(w_refs, where_ref, w_ref, sems, ps)
            acc_ref[...] = back_ref[...]
            if carried is not None:
                pltpu.make_async_copy(source_ref, buffer_ref, copy_sems.at[0]).start()

        if carried is not None:

            @pl.when(step == len(ps) - 1)
            def _():
                pltpu.make_async_copy(source_ref, buffer_ref, copy_sems.at[0]).wait()
                pltpu.make_async_copy(buffer_ref, target_ref, copy_sems.at[1]).start()

        pieces.wait(w_refs, at(step), w_ref, sems)
        dctx = mm(da_ref[...], pieces.read(w_ref, at(step), 3 * width, 4 * width), NN)
        dctx = dctx.astype(BF).astype(F32)
        scale = HEAD**-0.5
        dos, deltas = [], []
        for h in range(heads):
            do = dctx[:, h * HEAD : (h + 1) * HEAD] * inv_ref[0, :, h : h + 1]
            ctx = ctx_ref[0, :, h * HEAD : (h + 1) * HEAD].astype(F32)
            deltas.append(jnp.sum(do * ctx, axis=-1, keepdims=True))
            dos.append(do.astype(BF))
        do_t = jnp.concatenate(dos, axis=1).T
        q_t = qkv_ref[0, :, 0:width].T
        dqs, dks, dvs = [], [], []
        for h in range(heads):
            k = qkv_ref[0, :, width + h * HEAD : width + (h + 1) * HEAD]
            v = qkv_ref[0, :, 2 * width + h * HEAD : 2 * width + (h + 1) * HEAD]
            e = e_ref[0, h]
            dp = mm(dos[h], v, NT)
            ds = (e.astype(F32) * (dp - deltas[h])).astype(BF)
            dvs.append(mm(do_t[h * HEAD : (h + 1) * HEAD], e, NN))
            dqs.append(mm(ds, k, NN) * scale)
            dks.append(mm(q_t[h * HEAD : (h + 1) * HEAD], ds, NN) * scale)
        dk = jnp.concatenate(dks, axis=0).astype(BF).T
        dv = jnp.concatenate(dvs, axis=0).astype(BF).T
        dqkv = jnp.concatenate([jnp.concatenate(dqs, axis=1).astype(BF), dk, dv], axis=1)
        dqkv_ref[0] = dqkv
        sums = jnp.sum(dqkv.astype(F32), axis=0, keepdims=True)
        sum_ref[0] = sums
        acc_ref[...] += mm(dqkv, pieces.read(w_ref, at(step), 0, 3 * width), NT)
        if vectors is not None:
            fill_rows(rows_ref, sums, wide_ref[0], one_ref, two_ref, vectors[3])
            rows = rows_ref[...].astype(BF)
            if tok_t is None:
                first_ref[0] = rows
            else:
                first_ref[0, :, 0 : 3 * width] = mm(tok_t_ref[...], dqkv, NN).astype(BF)
                first_ref[0, :, 3 * width :] = jnp.zeros((d, EXTRA), BF)
                for c in range(8):
                    first = c * (d // 8)
                    first_ref[0, first : first + 16, 3 * width :] = rows[c]

        @pl.when(step == len(ps) - 1)
        def _():
            tg_ref[...] = acc_ref[...].astype(tg_ref.dtype)
            if carried is not None:
                pltpu.make_async_copy(buffer_ref, target_ref, copy_sems.at[1]).wait()

    def of(*shape):
        return pl.BlockSpec((1,) + shape, lambda i: (at(i),) + (0,) * len(shape))

    specs = [SCALARS, full(n, d), of(n, 3 * width), of(n, width), of(heads, n, n), of(n, 128), full(n, d)]
    args = [pieces.where, da, qkv, ctx, e, inv, back]
    out_specs = [per(n, 3 * width), per(1, 3 * width), full(n, d)]
    outs = [
        out((len(ps), n, 3 * width), BF), out((len(ps), 1, 3 * width)), out((n, d), BF if last else F32),
    ]
    scratch = [pltpu.VMEM((n, d), F32)] + pieces.scratch()
    if vectors is not None:
        specs += [of(1, vectors[0].shape[2]), full(*vectors[1].shape), full(*vectors[2].shape)]
        args += list(vectors[:3])
        scratch.append(pltpu.VMEM((8, 16, EXTRA), F32))
        first = (8, 16, EXTRA)
        if tok_t is not None:
            specs.append(full(d, n))
            args.append(tok_t)
            first = (d, 3 * width + EXTRA)
        out_specs = [per(*first)] + out_specs
        outs = [out((len(ps),) + first, BF)] + outs
    specs += [ANY] * count
    args += pieces.arrays
    if carried is not None:
        specs.append(ANY)
        args.append(carried)
        out_specs.append(ANY)
        outs.append(out(carried.shape, carried.dtype))
        scratch += [pltpu.VMEM(carried.shape, carried.dtype), pltpu.SemaphoreType.DMA((2,))]
    return call(kernel, len(ps), specs, out_specs, outs, scratch, us=100)(*args)


def lamb(gradient, master, first, second):
    first_new = 0.5 * first + 0.5 * gradient
    second_new = 0.5 * second + 0.5 * gradient * gradient
    update = first_new / (jnp.sqrt(second_new) + 1e-06) + 0.01 * master
    return first_new, second_new, update


def whole_sum(array):
    return jnp.sum(jnp.sum(array * array, axis=1, keepdims=True), axis=0, keepdims=True)


def chunk_sum(refs, lanes):
    total = refs[0][:, lanes[0] : lanes[1]].astype(F32)
    for ref in refs[1:]:
        total = total + ref[:, lanes[0] : lanes[1]].astype(F32)
    return total


def moved(source, target, buffer, sems):
    into = pltpu.make_async_copy(source, buffer, sems.at[0])
    back = pltpu.make_async_copy(buffer, target, sems.at[1])
    into.start()

    def turn():
        into.wait()
        back.start()

    return turn, back.wait


def lamb_matrices(parts, entries, carried=None):
    count = len(parts)
    extra = [] if carried is None else [carried]

    def kernel(*refs):
        part_refs = refs[:count]
        ins, refs = refs[count : count + 3 * len(entries)], refs[count + 3 * len(entries) :]
        if extra:
            turn, end = moved(refs[0], refs[1 + 3 * len(entries) + 1], refs[-2], refs[-1])
            refs = refs[1:]
        sum_ref = refs[3 * len(entries)]
        for number, (lane, turned, master, _, _) in enumerate(entries):
            m_ref, f_ref, s_ref = ins[3 * number : 3 * number + 3]
            fn_ref, sn_ref, u_ref = refs[3 * number : 3 * number + 3]
            gradient = chunk_sum(part_refs, (lane, lane + master.shape[0 if turned else 1]))
            if turned:
                gradient = gradient.T
            fn_ref[...], sn_ref[...], update = lamb(gradient, m_ref[...], f_ref[...], s_ref[...])
            u_ref[...] = update
            at = 2 * number
            sum_ref[at : at + 1] = jnp.broadcast_to(whole_sum(m_ref[...]), (1, 128))
            sum_ref[at + 1 : at + 2] = jnp.broadcast_to(whole_sum(update), (1, 128))
            if extra and number == 0:
                turn()
        if extra:
            end()

    shapes = [entry[2].shape for entry in entries for _ in range(3)]
    args = list(parts) + [array for entry in entries for array in entry[2:]]
    specs = [full(*a.shape) for a in args] + [ANY] * len(extra)
    outs = [out(shape) for shape in shapes] + [out((8, 128))]
    out_specs = [full(*o.shape) for o in outs] + [ANY] * len(extra)
    outs += [out(a.shape, a.dtype) for a in extra]
    scratch = []
    for a in extra:
        scratch = [pltpu.VMEM(a.shape, a.dtype), pltpu.SemaphoreType.DMA((2,))]
    return call(kernel, 1, specs, out_specs, outs, scratch, us=0.01)(*args, *extra)


def lamb_last(parts, attn, small_grad, small, early, share):
    count = len(parts)
    width = attn[0].shape[2]
    shapes = [group[0].shape for group in small]

    def kernel(*refs):
        part_refs, refs = refs[:count], refs[count:]
        m_ref, f_ref, s_ref = refs[:3]
        small_refs, early_refs, refs = refs[3:15], refs[15:17], refs[17:]
        if small_grad is not None:
            small_ref, refs = refs[0], refs[1:]
        fn_ref, sn_ref, u_ref = refs[:3]
        small_out, su_ref, sum_ref, pack = refs[3:11], refs[11], refs[12], refs[13]
        row = lax.broadcasted_iota(jnp.int32, (8, 128), 0)
        lane = lax.broadcasted_iota(jnp.int32, (8, 128), 1)
        sums = jnp.zeros((8, 128), F32)

        def put(sums, index, weight_sq, update_sq):
            sums = jnp.where((row == 0) & (lane == index), weight_sq, sums)
            return jnp.where((row == 1) & (lane == index), update_sq, sums)

        for k in range(3):
            gradient = chunk_sum(part_refs, (k * width, (k + 1) * width))
            fn, sn, update = lamb(gradient, m_ref[k], f_ref[k], s_ref[k])
            fn_ref[k], sn_ref[k], u_ref[k] = fn, sn, update
            sums = put(sums, k, whole_sum(m_ref[k]), whole_sum(update))
        for index, call_index, at in ((3, 0, 2), (4, 0, 0), (5, 1, 0)):
            ref = early_refs[call_index]
            sums = put(sums, index, ref[at : at + 1, 0:1], ref[at + 1 : at + 2, 0:1])
        pack[...] = jnp.zeros_like(pack)
        at = 0
        for group in range(4):
            count_rows, lanes_used = shapes[group]
            for which in range(3):
                pack[which, at : at + count_rows, 0:lanes_used] = small_refs[3 * group + which][...]
            at += count_rows
        if small_grad is not None:
            pack[3] = small_ref[...]
        else:
            total = chunk_sum([ref.at[0:16] for ref in part_refs], (3 * width, 3 * width + EXTRA))
            pack[3, 0:2, 0:EXTRA] = total[0:2]
            for number in range(7):
                at = 2 + 2 * number
                pack[3, 2 + number : 3 + number, 0:EXTRA] = total[at : at + 1]
                pack[3, 2 + number : 3 + number, EXTRA : 2 * EXTRA] = total[at + 1 : at + 2]
        fn, sn, update = lamb(pack[3], pack[0], pack[1], pack[2])
        su_ref[...] = update
        at = 0
        for group in range(4):
            count_rows, lanes_used = shapes[group]
            small_out[2 * group][...] = fn[at : at + count_rows, 0:lanes_used]
            small_out[2 * group + 1][...] = sn[at : at + count_rows, 0:lanes_used]
            at += count_rows
        weight_rows = jnp.sum(pack[0] * pack[0], axis=1, keepdims=True)
        update_rows = jnp.sum(update * update, axis=1, keepdims=True)
        for index in range(9):
            part = 1.0 if index < 3 else share
            sums = put(
                sums, 6 + index, weight_rows[index : index + 1] * part, update_rows[index : index + 1] * part
            )
        sum_ref[...] = sums

    args = list(parts) + list(attn)
    args += [array for group in small for array in group] + list(early)
    if small_grad is not None:
        args.append(small_grad)
    outs = [out(attn[0].shape)] * 3
    outs += [out(s) for s in shapes for _ in range(2)]
    outs += [out((16, 128)), out((8, 128))]
    return call(
        kernel, 1, [full(*a.shape) for a in args], [full(*o.shape) for o in outs], outs,
        [pltpu.VMEM((4, 16, 128), F32)], us=3.1,
    )(*args)


def finish(sums, matrices, updates, small, small_update):
    shapes = [a.shape for a in small]

    def kernel(*refs):
        sum_ref, refs = refs[0], refs[1:]
        m_refs, u_refs, v_refs, vu_ref = refs[:4], refs[4:8], refs[8:12], refs[12]
        m_outs, v_outs, norm_ref = refs[13:17], refs[17:21], refs[21]
        norms = jnp.sqrt(sum_ref[...])
        trust = 0.5 * (norms[0:1] / (norms[1:2] + 1e-06))
        norm_ref[...] = norms[0:2, 0:15]
        for k in range(3):
            m_outs[0][k] = m_refs[0][k] - trust[:, k : k + 1] * u_refs[0][k]
        for number in range(1, 4):
            at = 2 + number
            m_outs[number][...] = m_refs[number][...] - trust[:, at : at + 1] * u_refs[number][...]
        at = 0
        for group in range(4):
            count_rows, lanes_used = shapes[group]
            for r in range(count_rows):
                factor = trust[:, 6 + at : 7 + at]
                update = vu_ref[at : at + 1, 0:lanes_used]
                v_outs[group][r : r + 1] = v_refs[group][r : r + 1] - factor * update
                at += 1

    args = [sums] + list(matrices) + list(updates) + list(small) + [small_update]
    outs = [out(a.shape) for a in matrices] + [out(s) for s in shapes] + [out((2, 15))]
    return call(
        kernel, 1,
        [full(*a.shape) for a in args], [full(*o.shape) for o in outs], outs,
        us=0.01,
    )(*args)


def prepare(attn, mix, up, down_rows, small, inside):
    rows, width = attn.shape[1:]
    units = up.shape[1]
    lanes = 4 * width + (128 if inside else 0)

    def kernel(attn_ref, mix_ref, up_ref, down_ref, *refs):
        attn_out, ffn_out = refs[len(small)], refs[len(small) + 1]
        for k in range(3):
            attn_out[:, k * width : (k + 1) * width] = attn_ref[k].astype(BF)
        attn_out[:, 3 * width : 4 * width] = mix_ref[...].T.astype(BF)
        ffn_out[0:rows] = up_ref[...].astype(BF)
        ffn_out[rows : 2 * rows] = down_ref[...].astype(BF)
        if inside:
            pack = refs[len(small) + 2]
            pack[...] = jnp.zeros_like(pack)
            at = 0
            for ref in refs[: len(small)]:
                pack[at : at + ref.shape[0], 0 : ref.shape[1]] = ref[...]
                at += ref.shape[0]
            attn_out[:, 4 * width :] = pack[...].astype(BF)

    args = [attn, mix, up, down_rows] + list(small)
    outs = [out((rows, lanes), BF), out((2 * rows, units), BF)]
    return call(
        kernel, 1, [full(*a.shape) for a in args], [full(*o.shape) for o in outs], outs,
        [pltpu.VMEM((rows, 128), F32)], us=2.1,
    )(*args)


def pack_rows(arrays):
    rows = [jnp.pad(a, ((0, 0), (0, 128 - a.shape[1]))) for a in arrays]
    total = sum(a.shape[0] for a in arrays)
    rows.append(jnp.zeros((16 - total, 128), F32))
    return jnp.concatenate(rows, axis=0)


def spread_vectors(qkv_sum, wide_grad, sums_one, sums_two, sizes):
    head_own, wide_own, gain_own, dp_size = sizes
    blocks, width = qkv_sum.shape[0], qkv_sum.shape[2] // 3

    def lanes128(array, own):
        array = array.reshape(array.shape[:-1] + (dp_size, own))
        return jnp.pad(array, ((0, 0),) * (array.ndim - 1) + ((0, 128 - own),))

    vectors = jnp.stack(
        [sums_one[0], sums_two[0], sums_one[2], sums_one[1], sums_two[2], sums_two[1]]
    )
    vectors = jnp.broadcast_to(
        lanes128(vectors, gain_own).transpose(1, 0, 2)[None], (blocks, dp_size, 6, 128)
    )
    return jnp.concatenate(
        [
            lanes128(qkv_sum[:, 0, :width], head_own)[:, :, None],
            lanes128(qkv_sum[:, 0, 2 * width :], head_own)[:, :, None],
            lanes128(wide_grad[:, 0], wide_own)[:, :, None],
            vectors,
            jnp.zeros((blocks, dp_size, 7, 128), F32),
        ],
        axis=2,
    )


def on_device(
    dp_size, tensor_size,
    tokens, cotangent, row_lengths, present, groups,
    attn_weight, attn_first, attn_second,
    mix_weight, mix_first, mix_second,
    up_weight, up_first, up_second,
    down_weight, down_first, down_second,
    head_bias, head_first, head_second,
    wide_bias, wide_first, wide_second,
    norm_gains, gain_first, gain_second,
    shift_bias, shift_first, shift_second,
):
    comm = GridComm() if (dp_size, tensor_size) == (8, 4) else GenericComm(dp_size, tensor_size)
    rank = lax.axis_index("tensor")
    row_count, n = groups.shape
    assert row_count == tensor_size
    d = tokens.shape[1]
    width, units = attn_weight.shape[2], up_weight.shape[1]
    head_own, wide_own, gain_own = head_bias.shape[1], wide_bias.shape[0], norm_gains.shape[1]
    small_arrays = [
        (head_bias, head_first, head_second),
        tuple(a.reshape(1, -1) for a in (wide_bias, wide_first, wide_second)),
        (norm_gains, gain_first, gain_second),
        (shift_bias, shift_first, shift_second),
    ]

    down_rows = down_weight.T
    small_masters = [group[0] for group in small_arrays]
    small_all = None
    if not comm.small_inside:
        small_all = comm.gather_small(pack_rows(small_masters).astype(BF).astype(F32))
    attn_shard, ffn_shard = prepare(
        attn_weight, mix_weight, up_weight, down_rows, small_masters, comm.small_inside
    )
    attn_g = comm.gather(attn_shard)
    attn_g.z([])
    attn_g.xy([])
    attn_g.diagonal([])
    attn_w = attn_g.core()
    up_w, down_w = comm.gather_stacked(ffn_shard)

    tok = lax.dynamic_slice_in_dim(tokens, rank * n, n, 0)
    cot = lax.dynamic_slice_in_dim(cotangent, rank * n, n, 0)
    group_row = lax.dynamic_index_in_dim(groups, rank, 0, keepdims=False)
    present_row = lax.dynamic_index_in_dim(present, rank, 0, keepdims=False)
    length = lax.dynamic_index_in_dim(row_lengths, rank, 0, keepdims=False)
    feature_ids = jnp.arange(present_row.shape[0])
    present_key = jnp.sum(
        (group_row[:, None] == feature_ids[None, :]) * present_row[None, :], axis=1
    )
    key_open = ((jnp.arange(n) < length) & (present_key == 1)).astype(jnp.int32)

    qkv, ctx, e, inv, n1, rstd, low, low_t, tok_t, rows, wide_low = attn_fwd(
        attn_w, width, ((head_own, wide_own, gain_own, dp_size), small_all), tok, group_row, key_open
    )
    act, slope, layer_out, ds2, df, df_t, sums_two = (
        ffn := ffn_fwd(up_w, down_w, low, wide_low, n1, cot, rows, comm.small_inside)
    )[-7:]
    layer_out_all = lax.all_gather(layer_out, "tensor", axis=0, tiled=True)

    down_red = comm.reduction([df_t], library=True)
    if comm.small_inside:
        down_red.send_odd(ffn[0])
    else:
        down_red.core([act])
    up_red = comm.reduction([low_t, None])
    attn_red = comm.reduction([tok_t])
    sizes = (head_own, wide_own, gain_own, dp_size)
    small_sum = None
    ffn_args = (up_w, down_w, df, slope, ds2, n1, rstd, rows)
    down_entries = [(0, False, down_rows, down_first.T, down_second.T)]
    up_entries = [
        (0, False, up_weight, up_first, up_second),
        (units, True, mix_weight, mix_first, mix_second),
    ]
    if comm.small_inside:
        odd, dh, wide_grad, ds1, da, da_t, sums_one = ffn_bwd(*ffn_args, (low_t, ctx))
        up_red.lefts[1] = da_t
        up_red.send_odd(odd)
        done = down_red.split([act], deps=[da])
        vectors = (wide_grad, sums_one, sums_two, sizes)
        odd, dqkv_odd, _, back = attn_bwd(
            attn_w, width, (1, 3), tie(da, done), qkv, ctx, e, inv, ds1, False, vectors, tok_t
        )
        attn_red.send_odd(odd)
        done = down_red.neighbour([odd, layer_out_all], us=100)
        done = up_red.split([dh, ctx], deps=done + [attn_red.core_got])
        down_parts = down_red.last(done)
        extra, dqkv, _, back, layer_out_done = attn_bwd(
            attn_w, width, (0, 2), tie(da, down_red.done), qkv, ctx, e, inv, back, True, vectors,
            carried=layer_out_all,
        )
        done = attn_red.split([[([0, 2], dqkv)]], extra)
        down_parts[0] = tie(down_parts[0], done)
        down_done = lamb_matrices(down_parts, down_entries)
        done = up_red.neighbour(down_done[3:4], us=100)
        tokens_grad_all = lax.all_gather(tie(back, done), "tensor", axis=0, tiled=True)
        done = attn_red.neighbour(done, us=100)
        up_parts = up_red.last(done)
        attn_parts = attn_red.last(up_red.done)
        up_parts[1] = tie(up_parts[1], attn_red.done)
        up_done = lamb_matrices(up_parts, up_entries, tokens_grad_all)
    else:
        blocks = range(tensor_size)
        dh, wide_grad, ds1, da, da_t, sums_one = ffn_bwd(*ffn_args)
        up_red.lefts[1] = da_t
        dqkv, dqkv_sum, back = attn_bwd(attn_w, width, blocks, da, qkv, ctx, e, inv, ds1, True)
        tokens_grad_all = lax.all_gather(back, "tensor", axis=0, tiled=True)
        up_red.core([dh, ctx])
        attn_red.core([dqkv])
        layer_out_done = layer_out_all
        down_done = lamb_matrices(down_red.last(), down_entries)
        up_done = lamb_matrices(up_red.last(), up_entries, tokens_grad_all)
        attn_parts = attn_red.last()
        small_sum = comm.scatter_small(
            spread_vectors(dqkv_sum, wide_grad, sums_one, sums_two, sizes)
        )

    last = lamb_last(
        attn_parts, (attn_weight, attn_first, attn_second), small_sum, small_arrays,
        (up_done[6], down_done[3]), 1.0 / tensor_size,
    )
    small_moments, small_u, sums = last[3:11], last[11], last[12]
    done = finish(
        comm.total(sums),
        (attn_weight, mix_weight, up_weight, down_rows),
        (last[2], up_done[5], up_done[2], down_done[2]),
        small_masters,
        small_u,
    )
    moments = [last[0:2], up_done[3:5], up_done[0:2], down_done[0:2]]
    moments += [small_moments[2 * k : 2 * k + 2] for k in range(4)]
    result = [layer_out_done, up_done[7]]
    for number, (first_new, second_new) in enumerate(moments):
        group = [done[number], first_new, second_new]
        if number == 3:
            group = [a.T for a in group]
        result += [a.reshape(-1) for a in group] if number == 5 else group
    return tuple(result) + (done[8],)


def solution(mesh):
    rows = P("dp", None)
    attn, mix, up = P(None, "dp", "tensor"), P("tensor", "dp"), P("dp", "tensor")
    head, wide, col = P(None, ("tensor", "dp")), P(("tensor", "dp")), P(None, "dp")
    params = tuple(spec for spec in (attn, mix, up, mix, head, wide, col, col) for _ in range(3))
    return jax.shard_map(
        functools.partial(on_device, mesh.shape["dp"], mesh.shape["tensor"]),
        mesh=mesh,
        in_specs=(rows, rows, P("dp"), rows, rows) + params,
        out_specs=(rows, rows) + params + (P(),),
        check_vma=False,
    )
```

```python
import functools

import jax
import jax.numpy as jnp
from jax import lax
from jax.experimental import pallas as pl
from jax.experimental.pallas import tpu as pltpu
from jax.sharding import PartitionSpec as P

HEAD = 64
BF = jnp.bfloat16
F32 = jnp.float32
NN = (((1,), (0,)), ((), ()))
NT = (((1,), (1,)), ((), ()))
TN = (((0,), (0,)), ((), ()))
VMEM_LIMIT = 58 << 20
EXTRA = 64
CHUNK = 256
COST = 0.5e9


def mm(a, b, dims):
    return lax.dot_general(a, b, dims, preferred_element_type=F32)


def full(*shape):
    return pl.BlockSpec(shape, lambda i: (0,) * len(shape))


def per(*shape):
    return pl.BlockSpec((1,) + shape, lambda i: (i,) + (0,) * len(shape))


ANY = pl.BlockSpec(memory_space=pl.ANY)
SCALARS = pl.BlockSpec(memory_space=pltpu.SMEM)


def out(shape, dtype=F32):
    return jax.ShapeDtypeStruct(shape, dtype)


def call(kernel, grid, in_specs, out_specs, out_shape, scratch=(), us=2.0):
    return pl.pallas_call(
        kernel,
        grid=(grid,),
        in_specs=in_specs,
        out_specs=out_specs,
        out_shape=out_shape,
        scratch_shapes=list(scratch),
        compiler_params=pltpu.CompilerParams(vmem_limit_bytes=VMEM_LIMIT),
        cost_estimate=pl.CostEstimate(
            flops=int(us * COST), bytes_accessed=1000, transcendentals=0
        ),
    )


class Pieces:
    def __init__(self, arrays, plan, where, blocks, rows, lanes, group=None):
        self.arrays, self.plan, self.where, self.group = arrays, plan, where, group
        self.blocks, self.rows, self.lanes = blocks, rows, lanes

    def scratch(self):
        if self.group is not None:
            shape, count = (self.blocks, 8, self.rows // 8, self.lanes), 1
        elif self.plan is None:
            shape, count = (self.blocks, self.rows, self.lanes), 1
        else:
            shape, count = (self.blocks, 4, 2, self.rows // 8, self.lanes), 4
        return [pltpu.VMEM(shape, BF), pltpu.SemaphoreType.DMA((self.blocks, count))]

    def start(self, refs, where_ref, buffer, sems, ps=None):
        for p in range(self.blocks) if ps is None else ps:
            if self.group is not None:
                source = refs[0].at[:, where_ref[2] ^ p, self.group]
                pltpu.make_async_copy(source, buffer.at[p], sems.at[p, 0]).start()
                continue
            if self.plan is None:
                pltpu.make_async_copy(refs[0].at[p], buffer.at[p], sems.at[p, 0]).start()
                continue
            for number, (array, y_rel, pair_rel) in enumerate(self.plan[p]):
                pair = (where_ref[0] // 2) ^ pair_rel
                target = buffer.at[p, pl.ds(pair * 2, 2), where_ref[1] ^ y_rel]
                pltpu.make_async_copy(refs[array], target, sems.at[p, number]).start()

    def wait(self, refs, p, buffer, sems):
        if self.group is not None:
            source = refs[0].at[:, 0, self.group]
            pltpu.make_async_copy(source, buffer.at[p], sems.at[p, 0]).wait()
            return
        if self.plan is None:
            pltpu.make_async_copy(refs[0].at[0], buffer.at[p], sems.at[p, 0]).wait()
            return
        for number in range(4):
            target = buffer.at[p, pl.ds(0, 2), 0]
            pltpu.make_async_copy(refs[0], target, sems.at[p, number]).wait()

    def read(self, buffer, p, first, last):
        if self.group is not None:
            return buffer[p, :, :, first:last].reshape(self.rows, last - first)
        if self.plan is None:
            return buffer[p, :, first:last]
        return buffer[p, :, :, :, first:last].reshape(self.rows, last - first)


def tie(array, deps):
    return lax.optimization_barrier((array, tuple(deps)))[0] if deps else array


class GenericComm:
    small_inside = False

    def __init__(self, dp, tensor):
        self.dp, self.tensor = dp, tensor
        self.where = jnp.zeros((2,), jnp.int32)

    def gather(self, shard):
        return GenericGather(self, shard)

    def gather_stacked(self, shard):
        rows = shard.shape[0] // 2
        return [GenericGather(self, part).core() for part in (shard[:rows], shard[rows:])]

    def gather_small(self, vector):
        return lax.all_gather(lax.all_gather(vector, "dp", axis=0), "tensor", axis=0)

    def scatter_small(self, vectors):
        own = lax.psum_scatter(vectors, "tensor", scatter_dimension=0)
        return lax.psum_scatter(own, "dp", scatter_dimension=0)

    def total(self, values):
        return lax.psum(values, ("dp", "tensor"))

    def reduction(self, lefts, library=False):
        return GenericReduction(self, lefts)

    def block_sets(self):
        return [range(self.tensor)]


class GenericGather:
    def __init__(self, comm, shard):
        self.comm, self.shard = comm, shard

    def z(self, deps):
        return []

    def xy(self, deps):
        return []

    def diagonal(self, deps):
        pass

    def core(self):
        rows = lax.all_gather(self.shard, "dp", axis=0, tiled=True)
        blocks = lax.all_gather(rows, "tensor", axis=0)
        return Pieces([blocks], None, self.comm.where, *blocks.shape)


class GenericReduction:
    def __init__(self, comm, lefts):
        self.comm, self.lefts = comm, lefts

    def core(self, rights):
        self.rights = rights
        return []


    def last(self):
        stacked = grads(list(zip(self.lefts, self.rights)), range(self.comm.tensor))
        own = lax.psum_scatter(stacked, "tensor", scatter_dimension=0)
        return [lax.psum_scatter(own, "dp", scatter_dimension=0, tiled=True).astype(F32)]


class GridComm:
    small_inside = True

    def __init__(self):
        self.z = lax.axis_index("dp") // 2
        self.y = lax.axis_index("dp") % 2
        rank = lax.axis_index("tensor")
        self.where = jnp.stack([self.z, self.y, rank]).astype(jnp.int32)

    @staticmethod
    def send(array, dp_xor, tensor_xor):
        pairs = [
            (d * 4 + t, (d ^ dp_xor) * 4 + (t ^ tensor_xor)) for d in range(8) for t in range(4)
        ]
        return lax.ppermute(array, ("dp", "tensor"), pairs)

    def send_core(self, array):
        return self.send(array, 0, 1)

    def send_x(self, array):
        return self.send(array, 0, 2)

    def send_y(self, array):
        return self.send(array, 1, 0)

    def send_z(self, array, k):
        return self.send(array, 2 * k, 0)

    def gather(self, shard):
        return GridGather(self, shard)

    @staticmethod
    def sum_z(chunks):
        rows = chunks.reshape((-1, chunks.shape[2]))
        groups = [[2 * z + y for z in range(4)] for y in range(2)]
        return lax.psum_scatter(
            rows, "dp", scatter_dimension=0, axis_index_groups=groups, tiled=True
        )

    def gather_stacked(self, shard):
        rows, lanes = shard.shape[0] // 2, shard.shape[1]
        everything = lax.all_gather(shard, ("dp", "tensor"), axis=0, tiled=True)
        everything = everything.reshape(8, 4, 2, rows, lanes)
        return [Pieces([everything], None, self.where, 4, 8 * rows, lanes, g) for g in range(2)]

    def total(self, values):
        values = values + self.send_core(values)
        sent = self.send_x(values), self.send_y(values), self.send(values, 1, 2)
        values = values + sent[0] + (sent[1] + sent[2])
        sent = [self.send_z(values, k) for k in (1, 2, 3)]
        return values + sent[0] + (sent[1] + sent[2])

    def reduction(self, lefts, library=False):
        return Reduction(self, lefts, library)

    def block_sets(self):
        return [(1, 3), (0, 2)]


class GridGather:
    def __init__(self, comm, shard):
        self.comm, self.shard = comm, shard

    def z(self, deps):
        shard = tie(self.shard, deps)
        self.by_z = [shard] + [self.comm.send_z(shard, k) for k in (1, 2, 3)]
        return self.by_z[1:]

    def xy(self, deps):
        low = pair(self.by_z[0], self.by_z[1], self.comm.where)
        high = pair(self.by_z[2], self.by_z[3], self.comm.where)
        low, high = tie(low, deps), tie(high, deps)
        x_low, y_low = self.comm.send_x(low), self.comm.send_y(low)
        x_high, y_high = self.comm.send_x(high), self.comm.send_y(high)
        self.near, self.far = [low, high, y_low, y_high], [x_low, x_high]
        return [x_high, y_high]

    def diagonal(self, deps):
        y_low, x_high = tie(self.near[2], deps), tie(self.far[1], deps)
        self.far += [self.comm.send_x(y_low), self.comm.send_y(x_high)]

    def core(self):
        near_core = [self.comm.send_core(a) for a in self.near]
        far_core = [self.comm.send_core(a) for a in self.far]
        arrays = self.near + near_core + self.far + far_core
        plan = [[(4 * p + c, c // 2, c % 2) for c in range(4)] for p in range(4)]
        rows, lanes = self.shard.shape
        return Pieces(arrays, plan, self.comm.where, 4, 8 * rows, lanes)


class Reduction:
    def __init__(self, comm, lefts, library):
        self.comm, self.lefts, self.library = comm, lefts, library

    def core(self, rights):
        return self.send_odd(grads(list(zip(self.lefts, rights)), (1, 3)))

    def send_odd(self, odd):
        self.core_got = self.comm.send_core(odd)
        return [odd]

    def split(self, rights, extra=None, deps=()):
        terms = list(zip(self.lefts, rights))
        split = grads_split(terms, tie(self.core_got, deps), self.comm.where, extra)
        x_first, y_first, self.x_second, self.y_second, self.mine = split
        self.x_got, self.y_got = self.comm.send_x(x_first), self.comm.send_y(y_first)
        return [self.mine]

    def neighbour(self, deps=(), us=0.01):
        x_second, y_second = add_low(
            tie(self.x_second, deps), self.y_second, self.x_got, self.y_got, us
        )
        self.x_got2, self.y_got2 = self.comm.send_x(x_second), self.comm.send_y(y_second)
        return [x_second, y_second]

    def last(self, deps=(), us=0.01):
        mine = tie(self.mine, deps)[None]
        low = [(mine, 0), (self.x_got[None], 2), (self.y_got2[None], 0)]
        high = [(mine, 2), (self.y_got[None], 2), (self.x_got2[None], 0)]
        parts = combine([low, high], self.comm.where, us, self.library)
        self.done = [parts[0]]
        if self.library:
            return [self.comm.sum_z(parts[0])]
        return [parts[0]] + [self.comm.send_z(parts[k], k) for k in (1, 2, 3)]


def pair(first, second, where):
    rows, lanes = first.shape

    def kernel(where_ref, first_ref, second_ref, out_ref):
        odd = where_ref[0] % 2
        out_ref[odd] = first_ref[...]
        out_ref[1 - odd] = second_ref[...]

    return call(
        kernel, 1, [SCALARS, full(rows, lanes), full(rows, lanes)], full(2, rows, lanes),
        out((2, rows, lanes), BF), us=1.8,
    )(where, first, second)


def add_low(x_second, y_second, x_got, y_got, us):
    half = x_second.shape

    def kernel(x_ref, y_ref, xg_ref, yg_ref, xo_ref, yo_ref):
        xo_ref[...] = (x_ref[...].astype(F32) + yg_ref[...].astype(F32)).astype(BF)
        yo_ref[...] = (y_ref[...].astype(F32) + xg_ref[...].astype(F32)).astype(BF)

    return call(
        kernel, 1, [full(*half)] * 4, [full(*half)] * 2, [out(half, BF), out(half, BF)],
        us=us,
    )(x_second, y_second, x_got, y_got)


def block_of(right, p):
    if not isinstance(right, list):
        return right, p
    for ps, array in right:
        if p in ps:
            return array, list(ps).index(p)
    raise KeyError(p)


def grads(terms, ps):
    ps = list(ps)
    d, n = terms[0][0].shape
    firsts = [block_of(right, ps[0]) for _, right in terms]
    steps = [block_of(right, ps[1])[1] - first for (_, right), (_, first) in zip(terms, firsts)]
    lanes = [array.shape[2] for array, _ in firsts]

    def kernel(*refs):
        at = 0
        for number, width in enumerate(lanes):
            left, right = refs[2 * number], refs[2 * number + 1]
            refs[-1][0, :, at : at + width] = mm(left[...], right[0], NN).astype(BF)
            at += width
        if at < wide:
            refs[-1][0, :, at:] = jnp.zeros((d, wide - at), BF)

    specs, args = [], []
    for (left, _), (array, first), step, wide in zip(terms, firsts, steps, lanes):
        specs.append(full(d, n))
        specs.append(
            pl.BlockSpec((1, n, wide), lambda i, first=first, step=step: (first + step * i, 0, 0))
        )
        args += [left, array]
    wide = sum(lanes)
    wide += -wide % 128
    return call(
        kernel, len(ps), specs, per(d, wide), out((len(ps), d, wide), BF),
        us=0.01,
    )(*args)


def split_call(terms, got, where, write, outs, extra=None):
    d, n = terms[0][0].shape
    rows = d // 8
    count = len(terms)
    evens = [[block_of(right, p) for p in (0, 2)] for _, right in terms]
    lanes = [pair[0][0].shape[2] for pair in evens]
    wide = got.shape[2]

    def kernel(where_ref, *refs):
        got_ref = refs[3 * count]
        y = where_ref[1]

        def part(p, y_at):
            at = 0
            columns = []
            for number, width in enumerate(lanes):
                left, right = refs[3 * number], refs[3 * number + 1 + p // 2]
                lhs = left[:, y_at].reshape(4 * rows, n)
                value = mm(lhs, right[0], NN).reshape(4, rows, width)
                value = value + got_ref[p // 2, :, y_at, :, at : at + width].astype(F32)
                columns.append((at, width, value.astype(BF)))
                at += width
            if extra is not None:
                value = got_ref[p // 2, :, y_at, :, at:].astype(F32)
                top = value[:, 0:16] + refs[3 * count + 1][p // 2, :, y_at].astype(F32)
                value = jnp.concatenate([top, value[:, 16:]], axis=1)
                columns.append((at, EXTRA, value.astype(BF)))
            elif at < wide:
                columns.append((at, wide - at, jnp.zeros((4, rows, wide - at), BF)))
            return columns

        write(part, y, refs[3 * count + 1 + (extra is not None) :])

    specs, args = [SCALARS], [where]
    for (left, _), pair, width in zip(terms, evens, lanes):
        specs.append(full(4, 2, rows, n))
        args.append(left.reshape(4, 2, rows, n))
        for array, index in pair:
            specs.append(pl.BlockSpec((1, n, width), lambda i, index=index: (index, 0, 0)))
            args.append(array)
    specs.append(full(2, 4, 2, rows, wide))
    args.append(got.reshape(2, 4, 2, rows, wide))
    if extra is not None:
        specs.append(full(2, 4, 2, 16, EXTRA))
        args.append(extra.reshape(2, 4, 2, 16, EXTRA))
    shapes = [shape + (rows, wide) for shape in outs]
    return call(
        kernel, 1, specs, [full(*shape) for shape in shapes], [out(shape, BF) for shape in shapes],
        us=0.01,
    )(*args)


def grads_split(terms, got, where, extra=None):
    def write(part, y, refs):
        x_first, y_first, x_second, y_second, mine = refs
        for at, width, value in part(2, 1 - y):
            x_first[0:2, :, at : at + width] = value[0:2]
            y_first[0:2, :, at : at + width] = value[2:4]
        for at, width, value in part(2, y):
            x_first[2:4, :, at : at + width] = value[0:2]
            x_second[:, :, at : at + width] = value[2:4]
        for at, width, value in part(0, 1 - y):
            y_first[2:4, :, at : at + width] = value[2:4]
            y_second[:, :, at : at + width] = value[0:2]
        for at, width, value in part(0, y):
            mine[:, :, at : at + width] = value

    return split_call(terms, got, where, write, [(4,), (4,), (2,), (2,), (4,)], extra)


def combine(halves, where, us, whole):
    arrays = []
    for array in [array for half in halves for array, _ in half]:
        if not any(array is other for other in arrays):
            arrays.append(array)
    index = lambda array: [array is other for other in arrays].index(True)
    plans = [[(index(array), first) for array, first in half] for half in halves]
    chunk = arrays[0].shape[2:]

    def kernel(where_ref, *refs):
        outs, total = refs[len(arrays) :], refs[-1]
        for h, plan in enumerate(plans):
            for j in range(2):
                number, first = plan[0]
                value = refs[number][0, first + j].astype(F32)
                for number, first in plan[1:]:
                    value = value + refs[number][0, first + j].astype(F32)
                total[2 * h + j] = value.astype(total.dtype)
        if not whole:
            z = where_ref[0]
            outs[0][...] = total[z]
            for k in (1, 2, 3):
                outs[k][...] = total[z ^ k].astype(BF)

    outs = [out((4,) + chunk, BF)] if whole else [out(chunk)] + [out(chunk, BF)] * 3
    return call(
        kernel, 1,
        [SCALARS] + [full(*a.shape) for a in arrays],
        [full(*o.shape) for o in outs], outs,
        [] if whole else [pltpu.VMEM((4,) + chunk, F32)],
        us=us,
    )(where, *arrays)


def norm(summed):
    center = summed - jnp.mean(summed, axis=-1, keepdims=True)
    spread = jnp.mean(center * center, axis=-1, keepdims=True)
    scaled = lax.rsqrt(spread + 1e-05)
    return (center * scaled, scaled)


def norm_back(upstream, normal, scaled):
    inner_sum = (
        upstream
        - jnp.mean(upstream, axis=-1, keepdims=True)
        - normal * jnp.mean(upstream * normal, axis=-1, keepdims=True)
    )
    return scaled * inner_sum


G1, G2, BO, B1, C2, B2 = range(6)


def attn_fwd(pieces, width, small, tok, groups, key_open):
    n, d = tok.shape
    blocks = pieces.blocks
    heads = width // HEAD
    count = len(pieces.arrays)
    (head_own, wide_own, gain_own, dp_size), given = small
    units = wide_own * dp_size

    def kernel(where_ref, tok_ref, gq_ref, gk_ref, open_ref, *refs):
        w_refs, refs = refs[:count], refs[count:]
        if given is not None:
            bias_in, rows_in, wide_in = refs[:3]
            refs = refs[3:]
        qkv_ref, ctx_ref, e_ref, inv_ref, n1_ref, rstd_ref, low_ref, low_t_ref, tok_t_ref = refs[:9]
        rows_ref, wide_ref, att_ref, mask_ref, w_ref, sems = refs[9:]
        step = pl.program_id(0)

        @pl.when(step == 0)
        def _():
            pieces.start(w_refs, where_ref, w_ref, sems)
            seen = (open_ref[...] == 1) | (gq_ref[...] == gk_ref[...])
            mask_ref[...] = jnp.where(seen, 0.0, -1e30)
            att_ref[...] = jnp.zeros_like(att_ref)
            tok_t_ref[...] = tok_ref[...].T

        pieces.wait(w_refs, step, w_ref, sems)
        if given is None:
            first = 4 * width
            vectors = [
                w_ref[step, c // 2, c % 2, 0:16, first : first + 128].astype(F32)
                for c in range(dp_size)
            ]

            def line(row, used):
                return jnp.concatenate([v[row : row + 1, :used] for v in vectors], axis=1)

            bias_q, bias_v = line(0, head_own), line(1, head_own)
            wide_ref[0] = line(2, wide_own)

            @pl.when(step == 0)
            def _():
                for row in range(6):
                    rows_ref[row : row + 1] = line(3 + row, gain_own)

        else:
            bias_q, bias_v = bias_in[0, 0:1], bias_in[0, 1:2]
            wide_ref[0] = wide_in[0]
            rows_ref[0:6] = rows_in[...]

        qkv = mm(tok_ref[...], pieces.read(w_ref, step, 0, 3 * width), NN)
        lane = lax.broadcasted_iota(jnp.int32, (n, 128), 1)
        q_all = (qkv[:, :width] + bias_q).astype(BF)
        k_all = qkv[:, width : 2 * width].astype(BF)
        v_all = (qkv[:, 2 * width :] + bias_v).astype(BF)
        qkv_ref[0] = jnp.concatenate([q_all, k_all, v_all], axis=1)
        contexts = []
        inv_all = jnp.zeros((n, 128), F32)
        for h in range(heads):
            q = q_all[:, h * HEAD : (h + 1) * HEAD] * jnp.asarray(HEAD**-0.5, BF)
            k = k_all[:, h * HEAD : (h + 1) * HEAD]
            v = v_all[:, h * HEAD : (h + 1) * HEAD]
            s = mm(q, k, NT) + mask_ref[...]
            e = jnp.exp(s - jnp.max(s, axis=-1, keepdims=True)).astype(BF)
            e_ref[0, h] = e
            v_one = jnp.concatenate([v, jnp.ones_like(v)], axis=1)
            r = mm(e, v_one, NN)
            inv = 1.0 / r[:, HEAD : HEAD + 1]
            contexts.append((r[:, :HEAD] * inv).astype(BF))
            inv_all = jnp.where(lane == h, inv, inv_all)
        ctx = jnp.concatenate(contexts, axis=1)
        ctx_ref[0] = ctx
        inv_ref[0] = inv_all
        att_ref[...] += mm(ctx, pieces.read(w_ref, step, 3 * width, 4 * width), NT)

        @pl.when(step == blocks - 1)
        def _():
            summed = tok_ref[...].astype(F32) + (att_ref[...] + rows_ref[BO : BO + 1])
            normal, scaled = norm(summed)
            n1_ref[...] = normal
            rstd_ref[...] = scaled
            normed = normal * rows_ref[G1 : G1 + 1] + rows_ref[B1 : B1 + 1]
            low = normed.astype(BF)
            low_ref[...] = low
            low_t_ref[...] = low.T

    specs = [SCALARS, full(n, d), full(n, 1), full(1, n), full(1, n)] + [ANY] * count
    args = [pieces.where, tok, groups.reshape(n, 1), groups.reshape(1, n), key_open.reshape(1, n)]
    args += pieces.arrays
    if given is not None:
        biases = given[:, :, 0:2, :head_own].transpose(0, 2, 1, 3).reshape(blocks, 2, width)
        wide_low = given[:, :, 2, :wide_own].reshape(blocks, 1, units)
        specs += [per(2, width), full(6, d), per(1, units)]
        args += [
            biases, given[0, :, 3:9, :gain_own].transpose(1, 0, 2).reshape(6, d), wide_low,
        ]
    return call(
        kernel, blocks, specs,
        [
            per(n, 3 * width), per(n, width), per(heads, n, n), per(n, 128),
            full(n, d), full(n, 1), full(n, d), full(d, n), full(d, n), full(8, d), per(1, units),
        ],
        [
            out((blocks, n, 3 * width), BF), out((blocks, n, width), BF),
            out((blocks, heads, n, n), BF), out((blocks, n, 128)),
            out((n, d)), out((n, 1)), out((n, d), BF), out((d, n), BF), out((d, n), BF),
            out((8, d)), out((blocks, 1, units)),
        ],
        [pltpu.VMEM((n, d), F32), pltpu.VMEM((n, n), F32)] + pieces.scratch(),
        us=17,
    )(*args)


def ffn_fwd(up, down, low, wide_bias, n1, cot, rows, with_odd):
    n, d = low.shape
    blocks, units = up.blocks, up.lanes
    up_count, down_count = len(up.arrays), len(down.arrays)

    def kernel(where_ref, low_ref, bias_ref, n1_ref, cot_ref, rows_ref, *refs):
        up_refs, down_refs = refs[:up_count], refs[up_count : up_count + down_count]
        refs = refs[up_count + down_count :]
        if with_odd:
            odd_ref, kept_ref, refs = refs[0], refs[-1], refs[1:-1]
        act_ref, slope_ref, y_ref, ds_ref, df_ref, df_t_ref, sum_ref = refs[:7]
        acc_ref, wu_ref, sems_u, wd_ref, sems_d = refs[7:]
        step = pl.program_id(0)

        @pl.when(step == 0)
        def _():
            up.start(up_refs, where_ref, wu_ref, sems_u)
            down.start(down_refs, where_ref, wd_ref, sems_d)
            normed = n1_ref[...] * rows_ref[G1 : G1 + 1] + rows_ref[B1 : B1 + 1]
            acc_ref[...] = normed + rows_ref[C2 : C2 + 1]

        up.wait(up_refs, step, wu_ref, sems_u)
        down.wait(down_refs, step, wd_ref, sems_d)
        low_all = low_ref[...]
        parts = []
        for first in range(0, units, CHUNK):
            last = first + CHUNK
            h = mm(low_all, up.read(wu_ref, step, first, last), NN) + bias_ref[0, :, first:last]
            cdf = 0.5 * (1.0 + lax.erf(h * (0.5**0.5)))
            act = (h * cdf).astype(BF)
            act_ref[0, :, first:last] = act
            density = jnp.exp(h * h * -0.5) * 0.3989422804014327
            slope_ref[0, :, first:last] = (cdf + h * density).astype(BF)
            parts.append(mm(act, down.read(wd_ref, step, first, last), NT))
        acc_ref[...] += sum(parts[1:], parts[0])
        if with_odd:

            @pl.when(step % 2 == 1)
            def _():
                kept_ref[step // 2] = act_ref[0]

        @pl.when(step == blocks - 1)
        def _():
            normal, scaled = norm(acc_ref[...])
            gain = rows_ref[G2 : G2 + 1]
            y_ref[...] = (normal * gain + rows_ref[B2 : B2 + 1]).astype(BF)
            upstream = cot_ref[...].astype(F32)
            ds = norm_back(upstream * gain, normal, scaled)
            ds_ref[...] = ds
            df = ds.astype(BF)
            df_ref[...] = df
            df_t = df.T
            df_t_ref[...] = df_t
            sum_ref[...] = jnp.zeros_like(sum_ref)
            sum_ref[0:1] = jnp.sum(upstream * normal, axis=0, keepdims=True)
            sum_ref[1:2] = jnp.sum(upstream, axis=0, keepdims=True)
            sum_ref[2:3] = jnp.sum(ds, axis=0, keepdims=True)
            if with_odd:
                for k in range(2):
                    odd_ref[k] = mm(df_t, kept_ref[k], NN).astype(BF)

    outs = [
        out((blocks, n, units), BF), out((blocks, n, units), BF), out((n, d), BF), out((n, d)),
        out((n, d), BF), out((d, n), BF), out((8, d)),
    ]
    out_specs = [
        per(n, units), per(n, units), full(n, d), full(n, d), full(n, d), full(d, n), full(8, d),
    ]
    scratch = [pltpu.VMEM((n, d), F32)] + up.scratch() + down.scratch()
    if with_odd:
        outs = [out((2, d, units), BF)] + outs
        out_specs = [full(2, d, units)] + out_specs
        scratch.append(pltpu.VMEM((2, n, units), BF))
    return call(
        kernel, blocks,
        [SCALARS, full(n, d), per(1, units), full(n, d), full(n, d), full(*rows.shape)]
        + [ANY] * (up_count + down_count),
        out_specs, outs, scratch, us=20,
    )(up.where, low, wide_bias, n1, cot, rows, *up.arrays, *down.arrays)


def ffn_bwd(up, down, df, slope, ds2, n1, rstd, rows, odd=None):
    n, d = n1.shape
    blocks, units = up.blocks, up.lanes
    up_count, down_count = len(up.arrays), len(down.arrays)
    wide = 0
    if odd is not None:
        width = odd[1].shape[2]
        wide = units + width + -(units + width) % 128

    def kernel(where_ref, df_ref, slope_ref, ds2_ref, n1_ref, rstd_ref, rows_ref, *refs):
        if odd is not None:
            low_t_ref, ctx_ref, refs = refs[0], refs[1], refs[2:]
        up_refs, down_refs = refs[:up_count], refs[up_count : up_count + down_count]
        refs = refs[up_count + down_count :]
        if odd is not None:
            odd_ref, refs = refs[0], refs[1:]
        dh_ref, dc_ref, ds_ref, da_ref, da_t_ref, sum_ref = refs[:6]
        acc_ref, wu_ref, sems_u, wd_ref, sems_d = refs[6:]
        step = pl.program_id(0)

        @pl.when(step == 0)
        def _():
            down.start(down_refs, where_ref, wd_ref, sems_d)
            up.start(up_refs, where_ref, wu_ref, sems_u)
            acc_ref[...] = ds2_ref[...]

        down.wait(down_refs, step, wd_ref, sems_d)
        up.wait(up_refs, step, wu_ref, sems_u)
        df_all = df_ref[...]
        parts = []
        for first in range(0, units, CHUNK):
            last = first + CHUNK
            dact = mm(df_all, down.read(wd_ref, step, first, last), NN)
            dh = (dact * slope_ref[0, :, first:last].astype(F32)).astype(BF)
            dh_ref[0, :, first:last] = dh
            dc_ref[0, :, first:last] = jnp.sum(dh.astype(F32), axis=0, keepdims=True)
            parts.append(mm(dh, up.read(wu_ref, step, first, last), NT))
        acc_ref[...] += sum(parts[1:], parts[0])
        if odd is not None:

            @pl.when(step % 2 == 1)
            def _():
                odd_ref[step // 2, :, 0:units] = mm(low_t_ref[...], dh_ref[0], NN).astype(BF)

        @pl.when(step == blocks - 1)
        def _():
            dnormed = acc_ref[...]
            normal = n1_ref[...]
            ds = norm_back(dnormed * rows_ref[G1 : G1 + 1], normal, rstd_ref[...])
            ds_ref[...] = ds
            da = ds.astype(BF)
            da_ref[...] = da
            da_t = da.T
            da_t_ref[...] = da_t
            sum_ref[...] = jnp.zeros_like(sum_ref)
            sum_ref[0:1] = jnp.sum(dnormed * normal, axis=0, keepdims=True)
            sum_ref[1:2] = jnp.sum(dnormed, axis=0, keepdims=True)
            sum_ref[2:3] = jnp.sum(ds, axis=0, keepdims=True)
            if odd is not None:
                for k in range(2):
                    part = mm(da_t, ctx_ref[2 * k + 1], NN).astype(BF)
                    odd_ref[k, :, units : units + width] = part
                    odd_ref[k, :, units + width :] = jnp.zeros((d, wide - units - width), BF)

    specs = [SCALARS, full(n, d), per(n, units), full(n, d), full(n, d), full(n, 1), full(*rows.shape)]
    args = [up.where, df, slope, ds2, n1, rstd, rows]
    outs = [
        out((blocks, n, units), BF), out((blocks, 1, units)), out((n, d)),
        out((n, d), BF), out((d, n), BF), out((8, d)),
    ]
    out_specs = [per(n, units), per(1, units), full(n, d), full(n, d), full(d, n), full(8, d)]
    if odd is not None:
        specs += [full(*a.shape) for a in odd]
        args += list(odd)
        outs = [out((2, d, wide), BF)] + outs
        out_specs = [full(2, d, wide)] + out_specs
    return call(
        kernel, blocks, specs + [ANY] * (up_count + down_count), out_specs, outs,
        [pltpu.VMEM((n, d), F32)] + up.scratch() + down.scratch(),
        us=100,
    )(*args, *up.arrays, *down.arrays)


def fill_rows(rows_ref, qkv_sum, wide_row, one_ref, two_ref, sizes):
    head_own, wide_own, gain_own, dp_size = sizes
    width = qkv_sum.shape[1] // 3
    rows_ref[...] = jnp.zeros_like(rows_ref)
    rows = [
        wide_row, one_ref[0:1], two_ref[0:1], one_ref[2:3], one_ref[1:2], two_ref[2:3], two_ref[1:2],
    ]
    for c in range(dp_size):
        for number, first in enumerate((0, 2 * width)):
            first += c * head_own
            rows_ref[c, number : number + 1, 0:head_own] = qkv_sum[:, first : first + head_own]
        for number, row in enumerate(rows):
            own = gain_own if number else wide_own
            at, first = 2 + 2 * number, c * own
            rows_ref[c, at : at + 1, :] = row[:, first : first + EXTRA]
            rest = own - EXTRA
            rows_ref[c, at + 1 : at + 2, 0:rest] = row[:, first + EXTRA : first + own]


def attn_bwd(pieces, width, ps, da, qkv, ctx, e, inv, back, last, vectors=None, tok_t=None, carried=None):
    n, d = back.shape
    ps = list(ps)
    count = len(pieces.arrays)
    heads = width // HEAD
    stride = ps[1] - ps[0]
    at = lambda i: ps[0] + stride * i

    def kernel(where_ref, da_ref, qkv_ref, ctx_ref, e_ref, inv_ref, back_ref, *refs):
        if vectors is not None:
            wide_ref, one_ref, two_ref, refs = refs[0], refs[1], refs[2], refs[3:]
        if tok_t is not None:
            tok_t_ref, refs = refs[0], refs[1:]
        w_refs, refs = refs[:count], refs[count:]
        if carried is not None:
            source_ref, target_ref, buffer_ref, copy_sems = refs[0], refs[5], refs[-2], refs[-1]
            refs = refs[1:5] + refs[6:-2]
        if vectors is not None:
            first_ref, rows_ref, refs = refs[0], refs[-1], refs[1:-1]
        dqkv_ref, sum_ref, tg_ref, acc_ref, w_ref, sems = refs
        step = pl.program_id(0)

        @pl.when(step == 0)
        def _():
            pieces.start(w_refs, where_ref, w_ref, sems, ps)
            acc_ref[...] = back_ref[...]
            if carried is not None:
                pltpu.make_async_copy(source_ref, buffer_ref, copy_sems.at[0]).start()

        if carried is not None:

            @pl.when(step == len(ps) - 1)
            def _():
                pltpu.make_async_copy(source_ref, buffer_ref, copy_sems.at[0]).wait()
                pltpu.make_async_copy(buffer_ref, target_ref, copy_sems.at[1]).start()

        pieces.wait(w_refs, at(step), w_ref, sems)
        dctx = mm(da_ref[...], pieces.read(w_ref, at(step), 3 * width, 4 * width), NN)
        dctx = dctx.astype(BF).astype(F32)
        scale = HEAD**-0.5
        dos, deltas = [], []
        for h in range(heads):
            do = dctx[:, h * HEAD : (h + 1) * HEAD] * inv_ref[0, :, h : h + 1]
            ctx = ctx_ref[0, :, h * HEAD : (h + 1) * HEAD].astype(F32)
            deltas.append(jnp.sum(do * ctx, axis=-1, keepdims=True))
            dos.append(do.astype(BF))
        do_t = jnp.concatenate(dos, axis=1).T
        q_t = qkv_ref[0, :, 0:width].T
        dqs, dks, dvs = [], [], []
        for h in range(heads):
            k = qkv_ref[0, :, width + h * HEAD : width + (h + 1) * HEAD]
            v = qkv_ref[0, :, 2 * width + h * HEAD : 2 * width + (h + 1) * HEAD]
            e = e_ref[0, h]
            dp = mm(dos[h], v, NT)
            ds = (e.astype(F32) * (dp - deltas[h])).astype(BF)
            dvs.append(mm(do_t[h * HEAD : (h + 1) * HEAD], e, NN))
            dqs.append(mm(ds, k, NN) * scale)
            dks.append(mm(q_t[h * HEAD : (h + 1) * HEAD], ds, NN) * scale)
        dk = jnp.concatenate(dks, axis=0).astype(BF).T
        dv = jnp.concatenate(dvs, axis=0).astype(BF).T
        dqkv = jnp.concatenate([jnp.concatenate(dqs, axis=1).astype(BF), dk, dv], axis=1)
        dqkv_ref[0] = dqkv
        sums = jnp.sum(dqkv.astype(F32), axis=0, keepdims=True)
        sum_ref[0] = sums
        acc_ref[...] += mm(dqkv, pieces.read(w_ref, at(step), 0, 3 * width), NT)
        if vectors is not None:
            fill_rows(rows_ref, sums, wide_ref[0], one_ref, two_ref, vectors[3])
            rows = rows_ref[...].astype(BF)
            if tok_t is None:
                first_ref[0] = rows
            else:
                first_ref[0, :, 0 : 3 * width] = mm(tok_t_ref[...], dqkv, NN).astype(BF)
                first_ref[0, :, 3 * width :] = jnp.zeros((d, EXTRA), BF)
                for c in range(8):
                    first = c * (d // 8)
                    first_ref[0, first : first + 16, 3 * width :] = rows[c]

        @pl.when(step == len(ps) - 1)
        def _():
            tg_ref[...] = acc_ref[...].astype(tg_ref.dtype)
            if carried is not None:
                pltpu.make_async_copy(buffer_ref, target_ref, copy_sems.at[1]).wait()

    def of(*shape):
        return pl.BlockSpec((1,) + shape, lambda i: (at(i),) + (0,) * len(shape))

    specs = [SCALARS, full(n, d), of(n, 3 * width), of(n, width), of(heads, n, n), of(n, 128), full(n, d)]
    args = [pieces.where, da, qkv, ctx, e, inv, back]
    out_specs = [per(n, 3 * width), per(1, 3 * width), full(n, d)]
    outs = [
        out((len(ps), n, 3 * width), BF), out((len(ps), 1, 3 * width)), out((n, d), BF if last else F32),
    ]
    scratch = [pltpu.VMEM((n, d), F32)] + pieces.scratch()
    if vectors is not None:
        specs += [of(1, vectors[0].shape[2]), full(*vectors[1].shape), full(*vectors[2].shape)]
        args += list(vectors[:3])
        scratch.append(pltpu.VMEM((8, 16, EXTRA), F32))
        first = (8, 16, EXTRA)
        if tok_t is not None:
            specs.append(full(d, n))
            args.append(tok_t)
            first = (d, 3 * width + EXTRA)
        out_specs = [per(*first)] + out_specs
        outs = [out((len(ps),) + first, BF)] + outs
    specs += [ANY] * count
    args += pieces.arrays
    if carried is not None:
        specs.append(ANY)
        args.append(carried)
        out_specs.append(ANY)
        outs.append(out(carried.shape, carried.dtype))
        scratch += [pltpu.VMEM(carried.shape, carried.dtype), pltpu.SemaphoreType.DMA((2,))]
    return call(kernel, len(ps), specs, out_specs, outs, scratch, us=100)(*args)


def lamb(gradient, master, first, second):
    first_new = 0.5 * first + 0.5 * gradient
    second_new = 0.5 * second + 0.5 * gradient * gradient
    update = first_new / (jnp.sqrt(second_new) + 1e-06) + 0.01 * master
    return first_new, second_new, update


def whole_sum(array):
    return jnp.sum(jnp.sum(array * array, axis=1, keepdims=True), axis=0, keepdims=True)


def chunk_sum(refs, lanes):
    total = refs[0][:, lanes[0] : lanes[1]].astype(F32)
    for ref in refs[1:]:
        total = total + ref[:, lanes[0] : lanes[1]].astype(F32)
    return total


def copied(source, deps):
    source = tie(source, deps)
    count = 4
    rows = source.shape[0] // count

    def kernel(source_ref, target_ref, buffer_ref, sems):
        ins, outs = [], []
        for k in range(count):
            part = pl.ds(k * rows, rows)
            ins.append(pltpu.make_async_copy(source_ref.at[part], buffer_ref.at[part], sems.at[0, k]))
            outs.append(pltpu.make_async_copy(buffer_ref.at[part], target_ref.at[part], sems.at[1, k]))
            ins[k].start()
        for k in range(count):
            ins[k].wait()
            outs[k].start()
        for k in range(count):
            outs[k].wait()

    return call(
        kernel, 1, [ANY], ANY, out(source.shape, source.dtype),
        [pltpu.VMEM(source.shape, source.dtype), pltpu.SemaphoreType.DMA((2, count))], us=0.01,
    )(source)


def lamb_matrices(parts, entries):
    count = len(parts)

    def kernel(*refs):
        part_refs = refs[:count]
        ins, refs = refs[count : count + 3 * len(entries)], refs[count + 3 * len(entries) :]
        sum_ref = refs[3 * len(entries)]
        for number, (lane, turned, master, _, _) in enumerate(entries):
            m_ref, f_ref, s_ref = ins[3 * number : 3 * number + 3]
            fn_ref, sn_ref, u_ref = refs[3 * number : 3 * number + 3]
            gradient = chunk_sum(part_refs, (lane, lane + master.shape[0 if turned else 1]))
            if turned:
                gradient = gradient.T
            fn_ref[...], sn_ref[...], update = lamb(gradient, m_ref[...], f_ref[...], s_ref[...])
            u_ref[...] = update
            at = 2 * number
            sum_ref[at : at + 1] = jnp.broadcast_to(whole_sum(m_ref[...]), (1, 128))
            sum_ref[at + 1 : at + 2] = jnp.broadcast_to(whole_sum(update), (1, 128))

    shapes = [entry[2].shape for entry in entries for _ in range(3)]
    args = list(parts) + [array for entry in entries for array in entry[2:]]
    outs = [out(shape) for shape in shapes] + [out((8, 128))]
    return call(
        kernel, 1, [full(*a.shape) for a in args], [full(*o.shape) for o in outs], outs, us=0.01,
    )(*args)


def lamb_last(parts, attn, small_grad, small, early, share):
    count = len(parts)
    width = attn[0].shape[2]
    shapes = [group[0].shape for group in small]

    def kernel(*refs):
        part_refs, refs = refs[:count], refs[count:]
        m_ref, f_ref, s_ref = refs[:3]
        small_refs, early_refs, refs = refs[3:15], refs[15:17], refs[17:]
        if small_grad is not None:
            small_ref, refs = refs[0], refs[1:]
        fn_ref, sn_ref, u_ref = refs[:3]
        small_out, su_ref, sum_ref, pack = refs[3:11], refs[11], refs[12], refs[13]
        row = lax.broadcasted_iota(jnp.int32, (8, 128), 0)
        lane = lax.broadcasted_iota(jnp.int32, (8, 128), 1)
        sums = jnp.zeros((8, 128), F32)

        def put(sums, index, weight_sq, update_sq):
            sums = jnp.where((row == 0) & (lane == index), weight_sq, sums)
            return jnp.where((row == 1) & (lane == index), update_sq, sums)

        for k in range(3):
            gradient = chunk_sum(part_refs, (k * width, (k + 1) * width))
            fn, sn, update = lamb(gradient, m_ref[k], f_ref[k], s_ref[k])
            fn_ref[k], sn_ref[k], u_ref[k] = fn, sn, update
            sums = put(sums, k, whole_sum(m_ref[k]), whole_sum(update))
        for index, call_index, at in ((3, 0, 2), (4, 0, 0), (5, 1, 0)):
            ref = early_refs[call_index]
            sums = put(sums, index, ref[at : at + 1, 0:1], ref[at + 1 : at + 2, 0:1])
        pack[...] = jnp.zeros_like(pack)
        at = 0
        for group in range(4):
            count_rows, lanes_used = shapes[group]
            for which in range(3):
                pack[which, at : at + count_rows, 0:lanes_used] = small_refs[3 * group + which][...]
            at += count_rows
        if small_grad is not None:
            pack[3] = small_ref[...]
        else:
            total = chunk_sum([ref.at[0:16] for ref in part_refs], (3 * width, 3 * width + EXTRA))
            pack[3, 0:2, 0:EXTRA] = total[0:2]
            for number in range(7):
                at = 2 + 2 * number
                pack[3, 2 + number : 3 + number, 0:EXTRA] = total[at : at + 1]
                pack[3, 2 + number : 3 + number, EXTRA : 2 * EXTRA] = total[at + 1 : at + 2]
        fn, sn, update = lamb(pack[3], pack[0], pack[1], pack[2])
        su_ref[...] = update
        at = 0
        for group in range(4):
            count_rows, lanes_used = shapes[group]
            small_out[2 * group][...] = fn[at : at + count_rows, 0:lanes_used]
            small_out[2 * group + 1][...] = sn[at : at + count_rows, 0:lanes_used]
            at += count_rows
        weight_rows = jnp.sum(pack[0] * pack[0], axis=1, keepdims=True)
        update_rows = jnp.sum(update * update, axis=1, keepdims=True)
        for index in range(9):
            part = 1.0 if index < 3 else share
            sums = put(
                sums, 6 + index, weight_rows[index : index + 1] * part, update_rows[index : index + 1] * part
            )
        sum_ref[...] = sums

    args = list(parts) + list(attn)
    args += [array for group in small for array in group] + list(early)
    if small_grad is not None:
        args.append(small_grad)
    outs = [out(attn[0].shape)] * 3
    outs += [out(s) for s in shapes for _ in range(2)]
    outs += [out((16, 128)), out((8, 128))]
    return call(
        kernel, 1, [full(*a.shape) for a in args], [full(*o.shape) for o in outs], outs,
        [pltpu.VMEM((4, 16, 128), F32)], us=3.1,
    )(*args)


def finish(sums, matrices, updates, small, small_update):
    shapes = [a.shape for a in small]

    def kernel(*refs):
        sum_ref, refs = refs[0], refs[1:]
        m_refs, u_refs, v_refs, vu_ref = refs[:4], refs[4:8], refs[8:12], refs[12]
        m_outs, v_outs, norm_ref = refs[13:17], refs[17:21], refs[21]
        norms = jnp.sqrt(sum_ref[...])
        trust = 0.5 * (norms[0:1] / (norms[1:2] + 1e-06))
        norm_ref[...] = norms[0:2, 0:15]
        for k in range(3):
            m_outs[0][k] = m_refs[0][k] - trust[:, k : k + 1] * u_refs[0][k]
        for number in range(1, 4):
            at = 2 + number
            m_outs[number][...] = m_refs[number][...] - trust[:, at : at + 1] * u_refs[number][...]
        at = 0
        for group in range(4):
            count_rows, lanes_used = shapes[group]
            for r in range(count_rows):
                factor = trust[:, 6 + at : 7 + at]
                update = vu_ref[at : at + 1, 0:lanes_used]
                v_outs[group][r : r + 1] = v_refs[group][r : r + 1] - factor * update
                at += 1

    args = [sums] + list(matrices) + list(updates) + list(small) + [small_update]
    outs = [out(a.shape) for a in matrices] + [out(s) for s in shapes] + [out((2, 15))]
    return call(
        kernel, 1,
        [full(*a.shape) for a in args], [full(*o.shape) for o in outs], outs,
        us=0.01,
    )(*args)


def prepare(attn, mix, up, down_rows, small, inside):
    rows, width = attn.shape[1:]
    units = up.shape[1]
    lanes = 4 * width + (128 if inside else 0)

    def kernel(attn_ref, mix_ref, up_ref, down_ref, *refs):
        attn_out, ffn_out = refs[len(small)], refs[len(small) + 1]
        for k in range(3):
            attn_out[:, k * width : (k + 1) * width] = attn_ref[k].astype(BF)
        attn_out[:, 3 * width : 4 * width] = mix_ref[...].T.astype(BF)
        ffn_out[0:rows] = up_ref[...].astype(BF)
        ffn_out[rows : 2 * rows] = down_ref[...].astype(BF)
        if inside:
            pack = refs[len(small) + 2]
            pack[...] = jnp.zeros_like(pack)
            at = 0
            for ref in refs[: len(small)]:
                pack[at : at + ref.shape[0], 0 : ref.shape[1]] = ref[...]
                at += ref.shape[0]
            attn_out[:, 4 * width :] = pack[...].astype(BF)

    args = [attn, mix, up, down_rows] + list(small)
    outs = [out((rows, lanes), BF), out((2 * rows, units), BF)]
    return call(
        kernel, 1, [full(*a.shape) for a in args], [full(*o.shape) for o in outs], outs,
        [pltpu.VMEM((rows, 128), F32)], us=2.1,
    )(*args)


def pack_rows(arrays):
    rows = [jnp.pad(a, ((0, 0), (0, 128 - a.shape[1]))) for a in arrays]
    total = sum(a.shape[0] for a in arrays)
    rows.append(jnp.zeros((16 - total, 128), F32))
    return jnp.concatenate(rows, axis=0)


def spread_vectors(qkv_sum, wide_grad, sums_one, sums_two, sizes):
    head_own, wide_own, gain_own, dp_size = sizes
    blocks, width = qkv_sum.shape[0], qkv_sum.shape[2] // 3

    def lanes128(array, own):
        array = array.reshape(array.shape[:-1] + (dp_size, own))
        return jnp.pad(array, ((0, 0),) * (array.ndim - 1) + ((0, 128 - own),))

    vectors = jnp.stack(
        [sums_one[0], sums_two[0], sums_one[2], sums_one[1], sums_two[2], sums_two[1]]
    )
    vectors = jnp.broadcast_to(
        lanes128(vectors, gain_own).transpose(1, 0, 2)[None], (blocks, dp_size, 6, 128)
    )
    return jnp.concatenate(
        [
            lanes128(qkv_sum[:, 0, :width], head_own)[:, :, None],
            lanes128(qkv_sum[:, 0, 2 * width :], head_own)[:, :, None],
            lanes128(wide_grad[:, 0], wide_own)[:, :, None],
            vectors,
            jnp.zeros((blocks, dp_size, 7, 128), F32),
        ],
        axis=2,
    )


def on_device(
    dp_size, tensor_size,
    tokens, cotangent, row_lengths, present, groups,
    attn_weight, attn_first, attn_second,
    mix_weight, mix_first, mix_second,
    up_weight, up_first, up_second,
    down_weight, down_first, down_second,
    head_bias, head_first, head_second,
    wide_bias, wide_first, wide_second,
    norm_gains, gain_first, gain_second,
    shift_bias, shift_first, shift_second,
):
    comm = GridComm() if (dp_size, tensor_size) == (8, 4) else GenericComm(dp_size, tensor_size)
    rank = lax.axis_index("tensor")
    row_count, n = groups.shape
    assert row_count == tensor_size
    d = tokens.shape[1]
    width, units = attn_weight.shape[2], up_weight.shape[1]
    head_own, wide_own, gain_own = head_bias.shape[1], wide_bias.shape[0], norm_gains.shape[1]
    small_arrays = [
        (head_bias, head_first, head_second),
        tuple(a.reshape(1, -1) for a in (wide_bias, wide_first, wide_second)),
        (norm_gains, gain_first, gain_second),
        (shift_bias, shift_first, shift_second),
    ]

    down_rows = down_weight.T
    small_masters = [group[0] for group in small_arrays]
    small_all = None
    if not comm.small_inside:
        small_all = comm.gather_small(pack_rows(small_masters).astype(BF).astype(F32))
    attn_shard, ffn_shard = prepare(
        attn_weight, mix_weight, up_weight, down_rows, small_masters, comm.small_inside
    )
    attn_g = comm.gather(attn_shard)
    attn_g.z([])
    attn_g.xy([])
    attn_g.diagonal([])
    attn_w = attn_g.core()
    up_w, down_w = comm.gather_stacked(ffn_shard)

    tok = lax.dynamic_slice_in_dim(tokens, rank * n, n, 0)
    cot = lax.dynamic_slice_in_dim(cotangent, rank * n, n, 0)
    group_row = lax.dynamic_index_in_dim(groups, rank, 0, keepdims=False)
    present_row = lax.dynamic_index_in_dim(present, rank, 0, keepdims=False)
    length = lax.dynamic_index_in_dim(row_lengths, rank, 0, keepdims=False)
    feature_ids = jnp.arange(present_row.shape[0])
    present_key = jnp.sum(
        (group_row[:, None] == feature_ids[None, :]) * present_row[None, :], axis=1
    )
    key_open = ((jnp.arange(n) < length) & (present_key == 1)).astype(jnp.int32)

    qkv, ctx, e, inv, n1, rstd, low, low_t, tok_t, rows, wide_low = attn_fwd(
        attn_w, width, ((head_own, wide_own, gain_own, dp_size), small_all), tok, group_row, key_open
    )
    act, slope, layer_out, ds2, df, df_t, sums_two = (
        ffn := ffn_fwd(up_w, down_w, low, wide_low, n1, cot, rows, comm.small_inside)
    )[-7:]
    layer_out_all = lax.all_gather(layer_out, "tensor", axis=0, tiled=True)

    down_red = comm.reduction([df_t], library=True)
    if comm.small_inside:
        down_red.send_odd(ffn[0])
    else:
        down_red.core([act])
    up_red = comm.reduction([low_t, None])
    attn_red = comm.reduction([tok_t])
    sizes = (head_own, wide_own, gain_own, dp_size)
    small_sum = None
    ffn_args = (up_w, down_w, df, slope, ds2, n1, rstd, rows)
    down_entries = [(0, False, down_rows, down_first.T, down_second.T)]
    up_entries = [
        (0, False, up_weight, up_first, up_second),
        (units, True, mix_weight, mix_first, mix_second),
    ]
    if comm.small_inside:
        odd, dh, wide_grad, ds1, da, da_t, sums_one = ffn_bwd(*ffn_args, (low_t, ctx))
        up_red.lefts[1] = da_t
        up_red.send_odd(odd)
        done = down_red.split([act], deps=[da])
        vectors = (wide_grad, sums_one, sums_two, sizes)
        odd, dqkv_odd, _, back = attn_bwd(
            attn_w, width, (1, 3), tie(da, done), qkv, ctx, e, inv, ds1, False, vectors, tok_t
        )
        attn_red.send_odd(odd)
        done = down_red.neighbour([odd, layer_out_all], us=100)
        done = up_red.split([dh, ctx], deps=done + [attn_red.core_got])
        down_parts = down_red.last(done)
        extra, dqkv, _, back, layer_out_done = attn_bwd(
            attn_w, width, (0, 2), tie(da, down_red.done), qkv, ctx, e, inv, back, True, vectors,
            carried=layer_out_all,
        )
        done = attn_red.split([[([0, 2], dqkv)]], extra)
        down_parts[0] = tie(down_parts[0], done)
        down_done = lamb_matrices(down_parts, down_entries)
        done = up_red.neighbour(down_done[3:4], us=100)
        tokens_grad_all = lax.all_gather(tie(back, done), "tensor", axis=0, tiled=True)
        done = attn_red.neighbour(done, us=100)
        up_parts = up_red.last(done)
        attn_parts = attn_red.last(up_red.done)
        tokens_grad_done = copied(tokens_grad_all, attn_red.done)
        up_parts[1] = tie(up_parts[1], [tokens_grad_done])
        up_done = lamb_matrices(up_parts, up_entries)
    else:
        blocks = range(tensor_size)
        dh, wide_grad, ds1, da, da_t, sums_one = ffn_bwd(*ffn_args)
        up_red.lefts[1] = da_t
        dqkv, dqkv_sum, back = attn_bwd(attn_w, width, blocks, da, qkv, ctx, e, inv, ds1, True)
        tokens_grad_all = lax.all_gather(back, "tensor", axis=0, tiled=True)
        up_red.core([dh, ctx])
        attn_red.core([dqkv])
        layer_out_done = layer_out_all
        down_done = lamb_matrices(down_red.last(), down_entries)
        tokens_grad_done = tokens_grad_all
        up_done = lamb_matrices(up_red.last(), up_entries)
        attn_parts = attn_red.last()
        small_sum = comm.scatter_small(
            spread_vectors(dqkv_sum, wide_grad, sums_one, sums_two, sizes)
        )

    last = lamb_last(
        attn_parts, (attn_weight, attn_first, attn_second), small_sum, small_arrays,
        (up_done[6], down_done[3]), 1.0 / tensor_size,
    )
    small_moments, small_u, sums = last[3:11], last[11], last[12]
    done = finish(
        comm.total(sums),
        (attn_weight, mix_weight, up_weight, down_rows),
        (last[2], up_done[5], up_done[2], down_done[2]),
        small_masters,
        small_u,
    )
    moments = [last[0:2], up_done[3:5], up_done[0:2], down_done[0:2]]
    moments += [small_moments[2 * k : 2 * k + 2] for k in range(4)]
    result = [layer_out_done, tokens_grad_done]
    for number, (first_new, second_new) in enumerate(moments):
        group = [done[number], first_new, second_new]
        if number == 3:
            group = [a.T for a in group]
        result += [a.reshape(-1) for a in group] if number == 5 else group
    return tuple(result) + (done[8],)


def solution(mesh):
    rows = P("dp", None)
    attn, mix, up = P(None, "dp", "tensor"), P("tensor", "dp"), P("dp", "tensor")
    head, wide, col = P(None, ("tensor", "dp")), P(("tensor", "dp")), P(None, "dp")
    params = tuple(spec for spec in (attn, mix, up, mix, head, wide, col, col) for _ in range(3))
    return jax.shard_map(
        functools.partial(on_device, mesh.shape["dp"], mesh.shape["tensor"]),
        mesh=mesh,
        in_specs=(rows, rows, P("dp"), rows, rows) + params,
        out_specs=(rows, rows) + params + (P(),),
        check_vma=False,
    )
```

```python
import functools

import jax
import jax.numpy as jnp
from jax import lax
from jax.experimental import pallas as pl
from jax.experimental.pallas import tpu as pltpu
from jax.sharding import PartitionSpec as P

HEAD = 64
BF = jnp.bfloat16
F32 = jnp.float32
NN = (((1,), (0,)), ((), ()))
NT = (((1,), (1,)), ((), ()))
TN = (((0,), (0,)), ((), ()))
VMEM_LIMIT = 58 << 20
EXTRA = 64
CHUNK = 256
COST = 0.5e9


def mm(a, b, dims):
    return lax.dot_general(a, b, dims, preferred_element_type=F32)


def full(*shape):
    return pl.BlockSpec(shape, lambda i: (0,) * len(shape))


def per(*shape):
    return pl.BlockSpec((1,) + shape, lambda i: (i,) + (0,) * len(shape))


ANY = pl.BlockSpec(memory_space=pl.ANY)
SCALARS = pl.BlockSpec(memory_space=pltpu.SMEM)


def out(shape, dtype=F32):
    return jax.ShapeDtypeStruct(shape, dtype)


def call(kernel, grid, in_specs, out_specs, out_shape, scratch=(), us=2.0):
    return pl.pallas_call(
        kernel,
        grid=(grid,),
        in_specs=in_specs,
        out_specs=out_specs,
        out_shape=out_shape,
        scratch_shapes=list(scratch),
        compiler_params=pltpu.CompilerParams(vmem_limit_bytes=VMEM_LIMIT),
        cost_estimate=pl.CostEstimate(
            flops=int(us * COST), bytes_accessed=1000, transcendentals=0
        ),
    )


class Pieces:
    def __init__(self, arrays, plan, where, blocks, rows, lanes, group=None):
        self.arrays, self.plan, self.where, self.group = arrays, plan, where, group
        self.blocks, self.rows, self.lanes = blocks, rows, lanes

    def scratch(self):
        if self.group is not None:
            shape, count = (self.blocks, 8, self.rows // 8, self.lanes), 1
        elif self.plan is None:
            shape, count = (self.blocks, self.rows, self.lanes), 1
        else:
            shape, count = (self.blocks, 4, 2, self.rows // 8, self.lanes), 4
        return [pltpu.VMEM(shape, BF), pltpu.SemaphoreType.DMA((self.blocks, count))]

    def start(self, refs, where_ref, buffer, sems, ps=None):
        for p in range(self.blocks) if ps is None else ps:
            if self.group is not None:
                source = refs[0].at[:, where_ref[2] ^ p, self.group]
                pltpu.make_async_copy(source, buffer.at[p], sems.at[p, 0]).start()
                continue
            if self.plan is None:
                pltpu.make_async_copy(refs[0].at[p], buffer.at[p], sems.at[p, 0]).start()
                continue
            for number, (array, y_rel, pair_rel) in enumerate(self.plan[p]):
                pair = (where_ref[0] // 2) ^ pair_rel
                target = buffer.at[p, pl.ds(pair * 2, 2), where_ref[1] ^ y_rel]
                pltpu.make_async_copy(refs[array], target, sems.at[p, number]).start()

    def wait(self, refs, p, buffer, sems):
        if self.group is not None:
            source = refs[0].at[:, 0, self.group]
            pltpu.make_async_copy(source, buffer.at[p], sems.at[p, 0]).wait()
            return
        if self.plan is None:
            pltpu.make_async_copy(refs[0].at[0], buffer.at[p], sems.at[p, 0]).wait()
            return
        for number in range(4):
            target = buffer.at[p, pl.ds(0, 2), 0]
            pltpu.make_async_copy(refs[0], target, sems.at[p, number]).wait()

    def read(self, buffer, p, first, last):
        if self.group is not None:
            return buffer[p, :, :, first:last].reshape(self.rows, last - first)
        if self.plan is None:
            return buffer[p, :, first:last]
        return buffer[p, :, :, :, first:last].reshape(self.rows, last - first)


def tie(array, deps):
    return lax.optimization_barrier((array, tuple(deps)))[0] if deps else array


class GenericComm:
    small_inside = False

    def __init__(self, dp, tensor):
        self.dp, self.tensor = dp, tensor
        self.where = jnp.zeros((2,), jnp.int32)

    def gather(self, shard):
        return GenericGather(self, shard)

    def gather_stacked(self, shard):
        rows = shard.shape[0] // 2
        return [GenericGather(self, part).core() for part in (shard[:rows], shard[rows:])]

    def gather_small(self, vector):
        return lax.all_gather(lax.all_gather(vector, "dp", axis=0), "tensor", axis=0)

    def scatter_small(self, vectors):
        own = lax.psum_scatter(vectors, "tensor", scatter_dimension=0)
        return lax.psum_scatter(own, "dp", scatter_dimension=0)

    def total(self, values):
        return lax.psum(values, ("dp", "tensor"))

    def reduction(self, lefts, library=False):
        return GenericReduction(self, lefts)

    def block_sets(self):
        return [range(self.tensor)]


class GenericGather:
    def __init__(self, comm, shard):
        self.comm, self.shard = comm, shard

    def z(self, deps):
        return []

    def xy(self, deps):
        return []

    def diagonal(self, deps):
        pass

    def core(self):
        rows = lax.all_gather(self.shard, "dp", axis=0, tiled=True)
        blocks = lax.all_gather(rows, "tensor", axis=0)
        return Pieces([blocks], None, self.comm.where, *blocks.shape)


class GenericReduction:
    def __init__(self, comm, lefts):
        self.comm, self.lefts = comm, lefts

    def core(self, rights):
        self.rights = rights
        return []


    def last(self):
        stacked = grads(list(zip(self.lefts, self.rights)), range(self.comm.tensor))
        own = lax.psum_scatter(stacked, "tensor", scatter_dimension=0)
        return [lax.psum_scatter(own, "dp", scatter_dimension=0, tiled=True).astype(F32)]


class GridComm:
    small_inside = True

    def __init__(self):
        self.z = lax.axis_index("dp") // 2
        self.y = lax.axis_index("dp") % 2
        rank = lax.axis_index("tensor")
        self.where = jnp.stack([self.z, self.y, rank]).astype(jnp.int32)

    @staticmethod
    def send(array, dp_xor, tensor_xor):
        pairs = [
            (d * 4 + t, (d ^ dp_xor) * 4 + (t ^ tensor_xor)) for d in range(8) for t in range(4)
        ]
        return lax.ppermute(array, ("dp", "tensor"), pairs)

    def send_core(self, array):
        return self.send(array, 0, 1)

    def send_x(self, array):
        return self.send(array, 0, 2)

    def send_y(self, array):
        return self.send(array, 1, 0)

    def send_z(self, array, k):
        return self.send(array, 2 * k, 0)

    def gather(self, shard):
        return GridGather(self, shard)

    @staticmethod
    def sum_z(chunks):
        rows = chunks.reshape((-1, chunks.shape[2]))
        groups = [[2 * z + y for z in range(4)] for y in range(2)]
        return lax.psum_scatter(
            rows, "dp", scatter_dimension=0, axis_index_groups=groups, tiled=True
        )

    def gather_stacked(self, shard):
        rows, lanes = shard.shape[0] // 2, shard.shape[1]
        everything = lax.all_gather(shard, ("dp", "tensor"), axis=0, tiled=True)
        everything = everything.reshape(8, 4, 2, rows, lanes)
        return [Pieces([everything], None, self.where, 4, 8 * rows, lanes, g) for g in range(2)]

    def total(self, values):
        values = values + self.send_core(values)
        sent = self.send_x(values), self.send_y(values), self.send(values, 1, 2)
        values = values + sent[0] + (sent[1] + sent[2])
        sent = [self.send_z(values, k) for k in (1, 2, 3)]
        return values + sent[0] + (sent[1] + sent[2])

    def reduction(self, lefts, library=False):
        return Reduction(self, lefts, library)

    def block_sets(self):
        return [(1, 3), (0, 2)]


class GridGather:
    def __init__(self, comm, shard):
        self.comm, self.shard = comm, shard

    def z(self, deps):
        shard = tie(self.shard, deps)
        self.by_z = [shard] + [self.comm.send_z(shard, k) for k in (1, 2, 3)]
        return self.by_z[1:]

    def xy(self, deps):
        low = pair(self.by_z[0], self.by_z[1], self.comm.where)
        high = pair(self.by_z[2], self.by_z[3], self.comm.where)
        low, high = tie(low, deps), tie(high, deps)
        x_low, y_low = self.comm.send_x(low), self.comm.send_y(low)
        x_high, y_high = self.comm.send_x(high), self.comm.send_y(high)
        self.near, self.far = [low, high, y_low, y_high], [x_low, x_high]
        return [x_high, y_high]

    def diagonal(self, deps):
        y_low, x_high = tie(self.near[2], deps), tie(self.far[1], deps)
        self.far += [self.comm.send_x(y_low), self.comm.send_y(x_high)]

    def core(self):
        near_core = [self.comm.send_core(a) for a in self.near]
        far_core = [self.comm.send_core(a) for a in self.far]
        arrays = self.near + near_core + self.far + far_core
        plan = [[(4 * p + c, c // 2, c % 2) for c in range(4)] for p in range(4)]
        rows, lanes = self.shard.shape
        return Pieces(arrays, plan, self.comm.where, 4, 8 * rows, lanes)


class Reduction:
    def __init__(self, comm, lefts, library):
        self.comm, self.lefts, self.library = comm, lefts, library

    def core(self, rights):
        return self.send_odd(grads(list(zip(self.lefts, rights)), (1, 3)))

    def send_odd(self, odd):
        self.core_got = self.comm.send_core(odd)
        return [odd]

    def split(self, rights, extra=None, deps=()):
        terms = list(zip(self.lefts, rights))
        split = grads_split(terms, tie(self.core_got, deps), self.comm.where, extra)
        x_first, y_first, self.x_second, self.y_second, self.mine = split
        self.x_got, self.y_got = self.comm.send_x(x_first), self.comm.send_y(y_first)
        return [self.mine]

    def neighbour(self, deps=(), us=0.01):
        x_second, y_second = add_low(
            tie(self.x_second, deps), self.y_second, self.x_got, self.y_got, us
        )
        self.x_got2, self.y_got2 = self.comm.send_x(x_second), self.comm.send_y(y_second)
        return [x_second, y_second]

    def last(self, deps=(), us=0.01):
        mine = tie(self.mine, deps)[None]
        low = [(mine, 0), (self.x_got[None], 2), (self.y_got2[None], 0)]
        high = [(mine, 2), (self.y_got[None], 2), (self.x_got2[None], 0)]
        parts = combine([low, high], self.comm.where, us, self.library)
        self.done = [parts[0]]
        if self.library:
            return [self.comm.sum_z(parts[0])]
        return [parts[0]] + [self.comm.send_z(parts[k], k) for k in (1, 2, 3)]


def pair(first, second, where):
    rows, lanes = first.shape

    def kernel(where_ref, first_ref, second_ref, out_ref):
        odd = where_ref[0] % 2
        out_ref[odd] = first_ref[...]
        out_ref[1 - odd] = second_ref[...]

    return call(
        kernel, 1, [SCALARS, full(rows, lanes), full(rows, lanes)], full(2, rows, lanes),
        out((2, rows, lanes), BF), us=1.8,
    )(where, first, second)


def add_low(x_second, y_second, x_got, y_got, us):
    half = x_second.shape

    def kernel(x_ref, y_ref, xg_ref, yg_ref, xo_ref, yo_ref):
        xo_ref[...] = (x_ref[...].astype(F32) + yg_ref[...].astype(F32)).astype(BF)
        yo_ref[...] = (y_ref[...].astype(F32) + xg_ref[...].astype(F32)).astype(BF)

    return call(
        kernel, 1, [full(*half)] * 4, [full(*half)] * 2, [out(half, BF), out(half, BF)],
        us=us,
    )(x_second, y_second, x_got, y_got)


def block_of(right, p):
    if not isinstance(right, list):
        return right, p
    for ps, array in right:
        if p in ps:
            return array, list(ps).index(p)
    raise KeyError(p)


def grads(terms, ps):
    ps = list(ps)
    d, n = terms[0][0].shape
    firsts = [block_of(right, ps[0]) for _, right in terms]
    steps = [block_of(right, ps[1])[1] - first for (_, right), (_, first) in zip(terms, firsts)]
    lanes = [array.shape[2] for array, _ in firsts]

    def kernel(*refs):
        at = 0
        for number, width in enumerate(lanes):
            left, right = refs[2 * number], refs[2 * number + 1]
            refs[-1][0, :, at : at + width] = mm(left[...], right[0], NN).astype(BF)
            at += width
        if at < wide:
            refs[-1][0, :, at:] = jnp.zeros((d, wide - at), BF)

    specs, args = [], []
    for (left, _), (array, first), step, wide in zip(terms, firsts, steps, lanes):
        specs.append(full(d, n))
        specs.append(
            pl.BlockSpec((1, n, wide), lambda i, first=first, step=step: (first + step * i, 0, 0))
        )
        args += [left, array]
    wide = sum(lanes)
    wide += -wide % 128
    return call(
        kernel, len(ps), specs, per(d, wide), out((len(ps), d, wide), BF),
        us=0.01,
    )(*args)


def split_call(terms, got, where, write, outs, extra=None):
    d, n = terms[0][0].shape
    rows = d // 8
    count = len(terms)
    evens = [[block_of(right, p) for p in (0, 2)] for _, right in terms]
    lanes = [pair[0][0].shape[2] for pair in evens]
    wide = got.shape[2]

    def kernel(where_ref, *refs):
        got_ref = refs[3 * count]
        y = where_ref[1]

        def part(p, y_at):
            at = 0
            columns = []
            for number, width in enumerate(lanes):
                left, right = refs[3 * number], refs[3 * number + 1 + p // 2]
                lhs = left[:, y_at].reshape(4 * rows, n)
                value = mm(lhs, right[0], NN).reshape(4, rows, width)
                value = value + got_ref[p // 2, :, y_at, :, at : at + width].astype(F32)
                columns.append((at, width, value.astype(BF)))
                at += width
            if extra is not None:
                value = got_ref[p // 2, :, y_at, :, at:].astype(F32)
                top = value[:, 0:16] + refs[3 * count + 1][p // 2, :, y_at].astype(F32)
                value = jnp.concatenate([top, value[:, 16:]], axis=1)
                columns.append((at, EXTRA, value.astype(BF)))
            elif at < wide:
                columns.append((at, wide - at, jnp.zeros((4, rows, wide - at), BF)))
            return columns

        write(part, y, refs[3 * count + 1 + (extra is not None) :])

    specs, args = [SCALARS], [where]
    for (left, _), pair, width in zip(terms, evens, lanes):
        specs.append(full(4, 2, rows, n))
        args.append(left.reshape(4, 2, rows, n))
        for array, index in pair:
            specs.append(pl.BlockSpec((1, n, width), lambda i, index=index: (index, 0, 0)))
            args.append(array)
    specs.append(full(2, 4, 2, rows, wide))
    args.append(got.reshape(2, 4, 2, rows, wide))
    if extra is not None:
        specs.append(full(2, 4, 2, 16, EXTRA))
        args.append(extra.reshape(2, 4, 2, 16, EXTRA))
    shapes = [shape + (rows, wide) for shape in outs]
    return call(
        kernel, 1, specs, [full(*shape) for shape in shapes], [out(shape, BF) for shape in shapes],
        us=0.01,
    )(*args)


def grads_split(terms, got, where, extra=None):
    def write(part, y, refs):
        x_first, y_first, x_second, y_second, mine = refs
        for at, width, value in part(2, 1 - y):
            x_first[0:2, :, at : at + width] = value[0:2]
            y_first[0:2, :, at : at + width] = value[2:4]
        for at, width, value in part(2, y):
            x_first[2:4, :, at : at + width] = value[0:2]
            x_second[:, :, at : at + width] = value[2:4]
        for at, width, value in part(0, 1 - y):
            y_first[2:4, :, at : at + width] = value[2:4]
            y_second[:, :, at : at + width] = value[0:2]
        for at, width, value in part(0, y):
            mine[:, :, at : at + width] = value

    return split_call(terms, got, where, write, [(4,), (4,), (2,), (2,), (4,)], extra)


def combine(halves, where, us, whole):
    arrays = []
    for array in [array for half in halves for array, _ in half]:
        if not any(array is other for other in arrays):
            arrays.append(array)
    index = lambda array: [array is other for other in arrays].index(True)
    plans = [[(index(array), first) for array, first in half] for half in halves]
    chunk = arrays[0].shape[2:]

    def kernel(where_ref, *refs):
        outs, total = refs[len(arrays) :], refs[-1]
        for h, plan in enumerate(plans):
            for j in range(2):
                number, first = plan[0]
                value = refs[number][0, first + j].astype(F32)
                for number, first in plan[1:]:
                    value = value + refs[number][0, first + j].astype(F32)
                total[2 * h + j] = value.astype(total.dtype)
        if not whole:
            z = where_ref[0]
            outs[0][...] = total[z]
            for k in (1, 2, 3):
                outs[k][...] = total[z ^ k].astype(BF)

    outs = [out((4,) + chunk, BF)] if whole else [out(chunk)] + [out(chunk, BF)] * 3
    return call(
        kernel, 1,
        [SCALARS] + [full(*a.shape) for a in arrays],
        [full(*o.shape) for o in outs], outs,
        [] if whole else [pltpu.VMEM((4,) + chunk, F32)],
        us=us,
    )(where, *arrays)


def norm(summed):
    center = summed - jnp.mean(summed, axis=-1, keepdims=True)
    spread = jnp.mean(center * center, axis=-1, keepdims=True)
    scaled = lax.rsqrt(spread + 1e-05)
    return (center * scaled, scaled)


def norm_back(upstream, normal, scaled):
    inner_sum = (
        upstream
        - jnp.mean(upstream, axis=-1, keepdims=True)
        - normal * jnp.mean(upstream * normal, axis=-1, keepdims=True)
    )
    return scaled * inner_sum


G1, G2, BO, B1, C2, B2 = range(6)


def attn_fwd(pieces, width, small, tok, groups, key_open):
    n, d = tok.shape
    blocks = pieces.blocks
    heads = width // HEAD
    count = len(pieces.arrays)
    (head_own, wide_own, gain_own, dp_size), given = small
    units = wide_own * dp_size

    def kernel(where_ref, tok_ref, gq_ref, gk_ref, open_ref, *refs):
        w_refs, refs = refs[:count], refs[count:]
        if given is not None:
            bias_in, rows_in, wide_in = refs[:3]
            refs = refs[3:]
        qkv_ref, ctx_ref, e_ref, inv_ref, n1_ref, rstd_ref, low_ref, low_t_ref, tok_t_ref = refs[:9]
        rows_ref, wide_ref, att_ref, mask_ref, w_ref, sems = refs[9:]
        step = pl.program_id(0)

        @pl.when(step == 0)
        def _():
            pieces.start(w_refs, where_ref, w_ref, sems)
            seen = (open_ref[...] == 1) | (gq_ref[...] == gk_ref[...])
            mask_ref[...] = jnp.where(seen, 0.0, -1e30)
            att_ref[...] = jnp.zeros_like(att_ref)
            tok_t_ref[...] = tok_ref[...].T

        pieces.wait(w_refs, step, w_ref, sems)
        if given is None:
            first = 4 * width
            vectors = [
                w_ref[step, c // 2, c % 2, 0:16, first : first + 128].astype(F32)
                for c in range(dp_size)
            ]

            def line(row, used):
                return jnp.concatenate([v[row : row + 1, :used] for v in vectors], axis=1)

            bias_q, bias_v = line(0, head_own), line(1, head_own)
            wide_ref[0] = line(2, wide_own)

            @pl.when(step == 0)
            def _():
                for row in range(6):
                    rows_ref[row : row + 1] = line(3 + row, gain_own)

        else:
            bias_q, bias_v = bias_in[0, 0:1], bias_in[0, 1:2]
            wide_ref[0] = wide_in[0]
            rows_ref[0:6] = rows_in[...]

        qkv = mm(tok_ref[...], pieces.read(w_ref, step, 0, 3 * width), NN)
        lane = lax.broadcasted_iota(jnp.int32, (n, 128), 1)
        q_all = (qkv[:, :width] + bias_q).astype(BF)
        k_all = qkv[:, width : 2 * width].astype(BF)
        v_all = (qkv[:, 2 * width :] + bias_v).astype(BF)
        qkv_ref[0] = jnp.concatenate([q_all, k_all, v_all], axis=1)
        contexts = []
        inv_all = jnp.zeros((n, 128), F32)
        for h in range(heads):
            q = q_all[:, h * HEAD : (h + 1) * HEAD] * jnp.asarray(HEAD**-0.5, BF)
            k = k_all[:, h * HEAD : (h + 1) * HEAD]
            v = v_all[:, h * HEAD : (h + 1) * HEAD]
            s = mm(q, k, NT) + mask_ref[...]
            e = jnp.exp(s - jnp.max(s, axis=-1, keepdims=True)).astype(BF)
            e_ref[0, h] = e
            v_one = jnp.concatenate([v, jnp.ones_like(v)], axis=1)
            r = mm(e, v_one, NN)
            inv = 1.0 / r[:, HEAD : HEAD + 1]
            contexts.append((r[:, :HEAD] * inv).astype(BF))
            inv_all = jnp.where(lane == h, inv, inv_all)
        ctx = jnp.concatenate(contexts, axis=1)
        ctx_ref[0] = ctx
        inv_ref[0] = inv_all
        att_ref[...] += mm(ctx, pieces.read(w_ref, step, 3 * width, 4 * width), NT)

        @pl.when(step == blocks - 1)
        def _():
            summed = tok_ref[...].astype(F32) + (att_ref[...] + rows_ref[BO : BO + 1])
            normal, scaled = norm(summed)
            n1_ref[...] = normal
            rstd_ref[...] = scaled
            normed = normal * rows_ref[G1 : G1 + 1] + rows_ref[B1 : B1 + 1]
            low = normed.astype(BF)
            low_ref[...] = low
            low_t_ref[...] = low.T

    specs = [SCALARS, full(n, d), full(n, 1), full(1, n), full(1, n)] + [ANY] * count
    args = [pieces.where, tok, groups.reshape(n, 1), groups.reshape(1, n), key_open.reshape(1, n)]
    args += pieces.arrays
    if given is not None:
        biases = given[:, :, 0:2, :head_own].transpose(0, 2, 1, 3).reshape(blocks, 2, width)
        wide_low = given[:, :, 2, :wide_own].reshape(blocks, 1, units)
        specs += [per(2, width), full(6, d), per(1, units)]
        args += [
            biases, given[0, :, 3:9, :gain_own].transpose(1, 0, 2).reshape(6, d), wide_low,
        ]
    return call(
        kernel, blocks, specs,
        [
            per(n, 3 * width), per(n, width), per(heads, n, n), per(n, 128),
            full(n, d), full(n, 1), full(n, d), full(d, n), full(d, n), full(8, d), per(1, units),
        ],
        [
            out((blocks, n, 3 * width), BF), out((blocks, n, width), BF),
            out((blocks, heads, n, n), BF), out((blocks, n, 128)),
            out((n, d)), out((n, 1)), out((n, d), BF), out((d, n), BF), out((d, n), BF),
            out((8, d)), out((blocks, 1, units)),
        ],
        [pltpu.VMEM((n, d), F32), pltpu.VMEM((n, n), F32)] + pieces.scratch(),
        us=17,
    )(*args)


def ffn_fwd(up, down, low, wide_bias, n1, cot, rows, with_odd):
    n, d = low.shape
    blocks, units = up.blocks, up.lanes
    up_count, down_count = len(up.arrays), len(down.arrays)

    def kernel(where_ref, low_ref, bias_ref, n1_ref, cot_ref, rows_ref, *refs):
        up_refs, down_refs = refs[:up_count], refs[up_count : up_count + down_count]
        refs = refs[up_count + down_count :]
        if with_odd:
            odd_ref, kept_ref, refs = refs[0], refs[-1], refs[1:-1]
        act_ref, slope_ref, y_ref, ds_ref, df_ref, df_t_ref, sum_ref = refs[:7]
        acc_ref, wu_ref, sems_u, wd_ref, sems_d = refs[7:]
        step = pl.program_id(0)

        @pl.when(step == 0)
        def _():
            up.start(up_refs, where_ref, wu_ref, sems_u)
            down.start(down_refs, where_ref, wd_ref, sems_d)
            normed = n1_ref[...] * rows_ref[G1 : G1 + 1] + rows_ref[B1 : B1 + 1]
            acc_ref[...] = normed + rows_ref[C2 : C2 + 1]

        up.wait(up_refs, step, wu_ref, sems_u)
        down.wait(down_refs, step, wd_ref, sems_d)
        low_all = low_ref[...]
        parts = []
        for first in range(0, units, CHUNK):
            last = first + CHUNK
            h = mm(low_all, up.read(wu_ref, step, first, last), NN) + bias_ref[0, :, first:last]
            cdf = 0.5 * (1.0 + lax.erf(h * (0.5**0.5)))
            act = (h * cdf).astype(BF)
            act_ref[0, :, first:last] = act
            density = jnp.exp(h * h * -0.5) * 0.3989422804014327
            slope_ref[0, :, first:last] = (cdf + h * density).astype(BF)
            parts.append(mm(act, down.read(wd_ref, step, first, last), NT))
        acc_ref[...] += sum(parts[1:], parts[0])
        if with_odd:

            @pl.when(step % 2 == 1)
            def _():
                kept_ref[step // 2] = act_ref[0]

        @pl.when(step == blocks - 1)
        def _():
            normal, scaled = norm(acc_ref[...])
            gain = rows_ref[G2 : G2 + 1]
            y_ref[...] = (normal * gain + rows_ref[B2 : B2 + 1]).astype(BF)
            upstream = cot_ref[...].astype(F32)
            ds = norm_back(upstream * gain, normal, scaled)
            ds_ref[...] = ds
            df = ds.astype(BF)
            df_ref[...] = df
            df_t = df.T
            df_t_ref[...] = df_t
            sum_ref[...] = jnp.zeros_like(sum_ref)
            sum_ref[0:1] = jnp.sum(upstream * normal, axis=0, keepdims=True)
            sum_ref[1:2] = jnp.sum(upstream, axis=0, keepdims=True)
            sum_ref[2:3] = jnp.sum(ds, axis=0, keepdims=True)
            if with_odd:
                for k in range(2):
                    odd_ref[k] = mm(df_t, kept_ref[k], NN).astype(BF)

    outs = [
        out((blocks, n, units), BF), out((blocks, n, units), BF), out((n, d), BF), out((n, d)),
        out((n, d), BF), out((d, n), BF), out((8, d)),
    ]
    out_specs = [
        per(n, units), per(n, units), full(n, d), full(n, d), full(n, d), full(d, n), full(8, d),
    ]
    scratch = [pltpu.VMEM((n, d), F32)] + up.scratch() + down.scratch()
    if with_odd:
        outs = [out((2, d, units), BF)] + outs
        out_specs = [full(2, d, units)] + out_specs
        scratch.append(pltpu.VMEM((2, n, units), BF))
    return call(
        kernel, blocks,
        [SCALARS, full(n, d), per(1, units), full(n, d), full(n, d), full(*rows.shape)]
        + [ANY] * (up_count + down_count),
        out_specs, outs, scratch, us=20,
    )(up.where, low, wide_bias, n1, cot, rows, *up.arrays, *down.arrays)


def ffn_bwd(up, down, df, slope, ds2, n1, rstd, rows, odd=None):
    n, d = n1.shape
    blocks, units = up.blocks, up.lanes
    up_count, down_count = len(up.arrays), len(down.arrays)
    wide = 0
    if odd is not None:
        width = odd[1].shape[2]
        wide = units + width + -(units + width) % 128

    def kernel(where_ref, df_ref, slope_ref, ds2_ref, n1_ref, rstd_ref, rows_ref, *refs):
        if odd is not None:
            low_t_ref, ctx_ref, refs = refs[0], refs[1], refs[2:]
        up_refs, down_refs = refs[:up_count], refs[up_count : up_count + down_count]
        refs = refs[up_count + down_count :]
        if odd is not None:
            odd_ref, refs = refs[0], refs[1:]
        dh_ref, dc_ref, ds_ref, da_ref, da_t_ref, sum_ref = refs[:6]
        acc_ref, wu_ref, sems_u, wd_ref, sems_d = refs[6:]
        step = pl.program_id(0)

        @pl.when(step == 0)
        def _():
            down.start(down_refs, where_ref, wd_ref, sems_d)
            up.start(up_refs, where_ref, wu_ref, sems_u)
            acc_ref[...] = ds2_ref[...]

        down.wait(down_refs, step, wd_ref, sems_d)
        up.wait(up_refs, step, wu_ref, sems_u)
        df_all = df_ref[...]
        parts = []
        for first in range(0, units, CHUNK):
            last = first + CHUNK
            dact = mm(df_all, down.read(wd_ref, step, first, last), NN)
            dh = (dact * slope_ref[0, :, first:last].astype(F32)).astype(BF)
            dh_ref[0, :, first:last] = dh
            dc_ref[0, :, first:last] = jnp.sum(dh.astype(F32), axis=0, keepdims=True)
            parts.append(mm(dh, up.read(wu_ref, step, first, last), NT))
        acc_ref[...] += sum(parts[1:], parts[0])
        if odd is not None:

            @pl.when(step % 2 == 1)
            def _():
                odd_ref[step // 2, :, 0:units] = mm(low_t_ref[...], dh_ref[0], NN).astype(BF)

        @pl.when(step == blocks - 1)
        def _():
            dnormed = acc_ref[...]
            normal = n1_ref[...]
            ds = norm_back(dnormed * rows_ref[G1 : G1 + 1], normal, rstd_ref[...])
            ds_ref[...] = ds
            da = ds.astype(BF)
            da_ref[...] = da
            da_t = da.T
            da_t_ref[...] = da_t
            sum_ref[...] = jnp.zeros_like(sum_ref)
            sum_ref[0:1] = jnp.sum(dnormed * normal, axis=0, keepdims=True)
            sum_ref[1:2] = jnp.sum(dnormed, axis=0, keepdims=True)
            sum_ref[2:3] = jnp.sum(ds, axis=0, keepdims=True)
            if odd is not None:
                for k in range(2):
                    part = mm(da_t, ctx_ref[2 * k + 1], NN).astype(BF)
                    odd_ref[k, :, units : units + width] = part
                    odd_ref[k, :, units + width :] = jnp.zeros((d, wide - units - width), BF)

    specs = [SCALARS, full(n, d), per(n, units), full(n, d), full(n, d), full(n, 1), full(*rows.shape)]
    args = [up.where, df, slope, ds2, n1, rstd, rows]
    outs = [
        out((blocks, n, units), BF), out((blocks, 1, units)), out((n, d)),
        out((n, d), BF), out((d, n), BF), out((8, d)),
    ]
    out_specs = [per(n, units), per(1, units), full(n, d), full(n, d), full(d, n), full(8, d)]
    if odd is not None:
        specs += [full(*a.shape) for a in odd]
        args += list(odd)
        outs = [out((2, d, wide), BF)] + outs
        out_specs = [full(2, d, wide)] + out_specs
    return call(
        kernel, blocks, specs + [ANY] * (up_count + down_count), out_specs, outs,
        [pltpu.VMEM((n, d), F32)] + up.scratch() + down.scratch(),
        us=100,
    )(*args, *up.arrays, *down.arrays)


def fill_rows(rows_ref, qkv_sum, wide_row, one_ref, two_ref, sizes):
    head_own, wide_own, gain_own, dp_size = sizes
    width = qkv_sum.shape[1] // 3
    rows_ref[...] = jnp.zeros_like(rows_ref)
    rows = [
        wide_row, one_ref[0:1], two_ref[0:1], one_ref[2:3], one_ref[1:2], two_ref[2:3], two_ref[1:2],
    ]
    for c in range(dp_size):
        for number, first in enumerate((0, 2 * width)):
            first += c * head_own
            rows_ref[c, number : number + 1, 0:head_own] = qkv_sum[:, first : first + head_own]
        for number, row in enumerate(rows):
            own = gain_own if number else wide_own
            at, first = 2 + 2 * number, c * own
            rows_ref[c, at : at + 1, :] = row[:, first : first + EXTRA]
            rest = own - EXTRA
            rows_ref[c, at + 1 : at + 2, 0:rest] = row[:, first + EXTRA : first + own]


def attn_bwd(pieces, width, ps, da, qkv, ctx, e, inv, back, last, vectors=None, tok_t=None, carried=None):
    n, d = back.shape
    ps = list(ps)
    count = len(pieces.arrays)
    heads = width // HEAD
    stride = ps[1] - ps[0]
    at = lambda i: ps[0] + stride * i

    def kernel(where_ref, da_ref, qkv_ref, ctx_ref, e_ref, inv_ref, back_ref, *refs):
        if vectors is not None:
            wide_ref, one_ref, two_ref, refs = refs[0], refs[1], refs[2], refs[3:]
        if tok_t is not None:
            tok_t_ref, refs = refs[0], refs[1:]
        w_refs, refs = refs[:count], refs[count:]
        if carried is not None:
            source_ref, target_ref, buffer_ref, copy_sems = refs[0], refs[5], refs[-2], refs[-1]
            refs = refs[1:5] + refs[6:-2]
        if vectors is not None:
            first_ref, rows_ref, refs = refs[0], refs[-1], refs[1:-1]
        dqkv_ref, sum_ref, tg_ref, acc_ref, w_ref, sems = refs
        step = pl.program_id(0)

        @pl.when(step == 0)
        def _():
            pieces.start(w_refs, where_ref, w_ref, sems, ps)
            acc_ref[...] = back_ref[...]
            if carried is not None:
                pltpu.make_async_copy(source_ref, buffer_ref, copy_sems.at[0]).start()

        if carried is not None:

            @pl.when(step == len(ps) - 1)
            def _():
                pltpu.make_async_copy(source_ref, buffer_ref, copy_sems.at[0]).wait()
                pltpu.make_async_copy(buffer_ref, target_ref, copy_sems.at[1]).start()

        pieces.wait(w_refs, at(step), w_ref, sems)
        dctx = mm(da_ref[...], pieces.read(w_ref, at(step), 3 * width, 4 * width), NN)
        dctx = dctx.astype(BF).astype(F32)
        scale = HEAD**-0.5
        dos, deltas = [], []
        for h in range(heads):
            do = dctx[:, h * HEAD : (h + 1) * HEAD] * inv_ref[0, :, h : h + 1]
            ctx = ctx_ref[0, :, h * HEAD : (h + 1) * HEAD].astype(F32)
            deltas.append(jnp.sum(do * ctx, axis=-1, keepdims=True))
            dos.append(do.astype(BF))
        do_t = jnp.concatenate(dos, axis=1).T
        q_t = qkv_ref[0, :, 0:width].T
        dqs, dks, dvs = [], [], []
        for h in range(heads):
            k = qkv_ref[0, :, width + h * HEAD : width + (h + 1) * HEAD]
            v = qkv_ref[0, :, 2 * width + h * HEAD : 2 * width + (h + 1) * HEAD]
            e = e_ref[0, h]
            dp = mm(dos[h], v, NT)
            ds = (e.astype(F32) * (dp - deltas[h])).astype(BF)
            dvs.append(mm(do_t[h * HEAD : (h + 1) * HEAD], e, NN))
            dqs.append(mm(ds, k, NN) * scale)
            dks.append(mm(q_t[h * HEAD : (h + 1) * HEAD], ds, NN) * scale)
        dk = jnp.concatenate(dks, axis=0).astype(BF).T
        dv = jnp.concatenate(dvs, axis=0).astype(BF).T
        dqkv = jnp.concatenate([jnp.concatenate(dqs, axis=1).astype(BF), dk, dv], axis=1)
        dqkv_ref[0] = dqkv
        sums = jnp.sum(dqkv.astype(F32), axis=0, keepdims=True)
        sum_ref[0] = sums
        acc_ref[...] += mm(dqkv, pieces.read(w_ref, at(step), 0, 3 * width), NT)
        if vectors is not None:
            fill_rows(rows_ref, sums, wide_ref[0], one_ref, two_ref, vectors[3])
            rows = rows_ref[...].astype(BF)
            if tok_t is None:
                first_ref[0] = rows
            else:
                first_ref[0, :, 0 : 3 * width] = mm(tok_t_ref[...], dqkv, NN).astype(BF)
                first_ref[0, :, 3 * width :] = jnp.zeros((d, EXTRA), BF)
                for c in range(8):
                    first = c * (d // 8)
                    first_ref[0, first : first + 16, 3 * width :] = rows[c]

        @pl.when(step == len(ps) - 1)
        def _():
            tg_ref[...] = acc_ref[...].astype(tg_ref.dtype)
            if carried is not None:
                pltpu.make_async_copy(buffer_ref, target_ref, copy_sems.at[1]).wait()

    def of(*shape):
        return pl.BlockSpec((1,) + shape, lambda i: (at(i),) + (0,) * len(shape))

    specs = [SCALARS, full(n, d), of(n, 3 * width), of(n, width), of(heads, n, n), of(n, 128), full(n, d)]
    args = [pieces.where, da, qkv, ctx, e, inv, back]
    out_specs = [per(n, 3 * width), per(1, 3 * width), full(n, d)]
    outs = [
        out((len(ps), n, 3 * width), BF), out((len(ps), 1, 3 * width)), out((n, d), BF if last else F32),
    ]
    scratch = [pltpu.VMEM((n, d), F32)] + pieces.scratch()
    if vectors is not None:
        specs += [of(1, vectors[0].shape[2]), full(*vectors[1].shape), full(*vectors[2].shape)]
        args += list(vectors[:3])
        scratch.append(pltpu.VMEM((8, 16, EXTRA), F32))
        first = (8, 16, EXTRA)
        if tok_t is not None:
            specs.append(full(d, n))
            args.append(tok_t)
            first = (d, 3 * width + EXTRA)
        out_specs = [per(*first)] + out_specs
        outs = [out((len(ps),) + first, BF)] + outs
    specs += [ANY] * count
    args += pieces.arrays
    if carried is not None:
        specs.append(ANY)
        args.append(carried)
        out_specs.append(ANY)
        outs.append(out(carried.shape, carried.dtype))
        scratch += [pltpu.VMEM(carried.shape, carried.dtype), pltpu.SemaphoreType.DMA((2,))]
    return call(kernel, len(ps), specs, out_specs, outs, scratch, us=100)(*args)


def lamb(gradient, master, first, second):
    first_new = 0.5 * first + 0.5 * gradient
    second_new = 0.5 * second + 0.5 * gradient * gradient
    update = first_new / (jnp.sqrt(second_new) + 1e-06) + 0.01 * master
    return first_new, second_new, update


def whole_sum(array):
    return jnp.sum(jnp.sum(array * array, axis=1, keepdims=True), axis=0, keepdims=True)


def chunk_sum(refs, lanes):
    total = refs[0][:, lanes[0] : lanes[1]].astype(F32)
    for ref in refs[1:]:
        total = total + ref[:, lanes[0] : lanes[1]].astype(F32)
    return total


def copied(source, deps):
    source = tie(source, deps)
    count = 4
    rows = source.shape[0] // count

    def kernel(source_ref, target_ref, buffer_ref, sems):
        ins, outs = [], []
        for k in range(count):
            part = pl.ds(k * rows, rows)
            ins.append(pltpu.make_async_copy(source_ref.at[part], buffer_ref.at[part], sems.at[0, k]))
            outs.append(pltpu.make_async_copy(buffer_ref.at[part], target_ref.at[part], sems.at[1, k]))
            ins[k].start()
        for k in range(count):
            ins[k].wait()
            outs[k].start()
        for k in range(count):
            outs[k].wait()

    return call(
        kernel, 1, [ANY], ANY, out(source.shape, source.dtype),
        [pltpu.VMEM(source.shape, source.dtype), pltpu.SemaphoreType.DMA((2, count))], us=0.01,
    )(source)


def lamb_matrices(parts, entries):
    count = len(parts)

    def kernel(*refs):
        part_refs = refs[:count]
        ins, refs = refs[count : count + 3 * len(entries)], refs[count + 3 * len(entries) :]
        sum_ref = refs[3 * len(entries)]
        for number, (lane, turned, master, _, _) in enumerate(entries):
            m_ref, f_ref, s_ref = ins[3 * number : 3 * number + 3]
            fn_ref, sn_ref, u_ref = refs[3 * number : 3 * number + 3]
            gradient = chunk_sum(part_refs, (lane, lane + master.shape[0 if turned else 1]))
            if turned:
                gradient = gradient.T
            fn_ref[...], sn_ref[...], update = lamb(gradient, m_ref[...], f_ref[...], s_ref[...])
            u_ref[...] = update
            at = 2 * number
            sum_ref[at : at + 1] = jnp.broadcast_to(whole_sum(m_ref[...]), (1, 128))
            sum_ref[at + 1 : at + 2] = jnp.broadcast_to(whole_sum(update), (1, 128))

    shapes = [entry[2].shape for entry in entries for _ in range(3)]
    args = list(parts) + [array for entry in entries for array in entry[2:]]
    outs = [out(shape) for shape in shapes] + [out((8, 128))]
    return call(
        kernel, 1, [full(*a.shape) for a in args], [full(*o.shape) for o in outs], outs, us=0.01,
    )(*args)


def lamb_last(parts, attn, small_grad, small, early, share):
    count = len(parts)
    width = attn[0].shape[2]
    shapes = [group[0].shape for group in small]

    def kernel(*refs):
        part_refs, refs = refs[:count], refs[count:]
        m_ref, f_ref, s_ref = refs[:3]
        small_refs, early_refs, refs = refs[3:15], refs[15:17], refs[17:]
        if small_grad is not None:
            small_ref, refs = refs[0], refs[1:]
        fn_ref, sn_ref, u_ref = refs[:3]
        small_out, su_ref, sum_ref, pack = refs[3:11], refs[11], refs[12], refs[13]
        row = lax.broadcasted_iota(jnp.int32, (8, 128), 0)
        lane = lax.broadcasted_iota(jnp.int32, (8, 128), 1)
        sums = jnp.zeros((8, 128), F32)

        def put(sums, index, weight_sq, update_sq):
            sums = jnp.where((row == 0) & (lane == index), weight_sq, sums)
            return jnp.where((row == 1) & (lane == index), update_sq, sums)

        for k in range(3):
            gradient = chunk_sum(part_refs, (k * width, (k + 1) * width))
            fn, sn, update = lamb(gradient, m_ref[k], f_ref[k], s_ref[k])
            fn_ref[k], sn_ref[k], u_ref[k] = fn, sn, update
            sums = put(sums, k, whole_sum(m_ref[k]), whole_sum(update))
        for index, call_index, at in ((3, 0, 2), (4, 0, 0), (5, 1, 0)):
            ref = early_refs[call_index]
            sums = put(sums, index, ref[at : at + 1, 0:1], ref[at + 1 : at + 2, 0:1])
        pack[...] = jnp.zeros_like(pack)
        at = 0
        for group in range(4):
            count_rows, lanes_used = shapes[group]
            for which in range(3):
                pack[which, at : at + count_rows, 0:lanes_used] = small_refs[3 * group + which][...]
            at += count_rows
        if small_grad is not None:
            pack[3] = small_ref[...]
        else:
            total = chunk_sum([ref.at[0:16] for ref in part_refs], (3 * width, 3 * width + EXTRA))
            pack[3, 0:2, 0:EXTRA] = total[0:2]
            for number in range(7):
                at = 2 + 2 * number
                pack[3, 2 + number : 3 + number, 0:EXTRA] = total[at : at + 1]
                pack[3, 2 + number : 3 + number, EXTRA : 2 * EXTRA] = total[at + 1 : at + 2]
        fn, sn, update = lamb(pack[3], pack[0], pack[1], pack[2])
        su_ref[...] = update
        at = 0
        for group in range(4):
            count_rows, lanes_used = shapes[group]
            small_out[2 * group][...] = fn[at : at + count_rows, 0:lanes_used]
            small_out[2 * group + 1][...] = sn[at : at + count_rows, 0:lanes_used]
            at += count_rows
        weight_rows = jnp.sum(pack[0] * pack[0], axis=1, keepdims=True)
        update_rows = jnp.sum(update * update, axis=1, keepdims=True)
        for index in range(9):
            part = 1.0 if index < 3 else share
            sums = put(
                sums, 6 + index, weight_rows[index : index + 1] * part, update_rows[index : index + 1] * part
            )
        sum_ref[...] = sums

    args = list(parts) + list(attn)
    args += [array for group in small for array in group] + list(early)
    if small_grad is not None:
        args.append(small_grad)
    outs = [out(attn[0].shape)] * 3
    outs += [out(s) for s in shapes for _ in range(2)]
    outs += [out((16, 128)), out((8, 128))]
    return call(
        kernel, 1, [full(*a.shape) for a in args], [full(*o.shape) for o in outs], outs,
        [pltpu.VMEM((4, 16, 128), F32)], us=3.1,
    )(*args)


def finish(sums, matrices, updates, small, small_update):
    shapes = [a.shape for a in small]

    def kernel(*refs):
        sum_ref, refs = refs[0], refs[1:]
        m_refs, u_refs, v_refs, vu_ref = refs[:4], refs[4:8], refs[8:12], refs[12]
        m_outs, v_outs, norm_ref = refs[13:17], refs[17:21], refs[21]
        norms = jnp.sqrt(sum_ref[...])
        trust = 0.5 * (norms[0:1] / (norms[1:2] + 1e-06))
        norm_ref[...] = norms[0:2, 0:15]
        for k in range(3):
            m_outs[0][k] = m_refs[0][k] - trust[:, k : k + 1] * u_refs[0][k]
        for number in range(1, 4):
            at = 2 + number
            m_outs[number][...] = m_refs[number][...] - trust[:, at : at + 1] * u_refs[number][...]
        at = 0
        for group in range(4):
            count_rows, lanes_used = shapes[group]
            for r in range(count_rows):
                factor = trust[:, 6 + at : 7 + at]
                update = vu_ref[at : at + 1, 0:lanes_used]
                v_outs[group][r : r + 1] = v_refs[group][r : r + 1] - factor * update
                at += 1

    args = [sums] + list(matrices) + list(updates) + list(small) + [small_update]
    outs = [out(a.shape) for a in matrices] + [out(s) for s in shapes] + [out((2, 15))]
    return call(
        kernel, 1,
        [full(*a.shape) for a in args], [full(*o.shape) for o in outs], outs,
        us=0.01,
    )(*args)


def prepare_ffn(up, down_rows):
    rows, units = up.shape

    def kernel(up_ref, down_ref, out_ref):
        out_ref[0:rows] = up_ref[...].astype(BF)
        out_ref[rows : 2 * rows] = down_ref[...].astype(BF)

    return call(
        kernel, 1, [full(rows, units)] * 2, full(2 * rows, units), out((2 * rows, units), BF), us=0.01,
    )(up, down_rows)


def prepare(attn, mix, small, inside):
    rows, width = attn.shape[1:]
    lanes = 4 * width + (128 if inside else 0)

    def kernel(attn_ref, mix_ref, *refs):
        attn_out = refs[len(small)]
        for k in range(3):
            attn_out[:, k * width : (k + 1) * width] = attn_ref[k].astype(BF)
        attn_out[:, 3 * width : 4 * width] = mix_ref[...].T.astype(BF)
        if inside:
            pack = refs[len(small) + 1]
            pack[...] = jnp.zeros_like(pack)
            at = 0
            for ref in refs[: len(small)]:
                pack[at : at + ref.shape[0], 0 : ref.shape[1]] = ref[...]
                at += ref.shape[0]
            attn_out[:, 4 * width :] = pack[...].astype(BF)

    args = [attn, mix] + list(small)
    outs = [out((rows, lanes), BF)]
    return call(
        kernel, 1, [full(*a.shape) for a in args], [full(*o.shape) for o in outs], outs,
        [pltpu.VMEM((rows, 128), F32)], us=2.1,
    )(*args)


def pack_rows(arrays):
    rows = [jnp.pad(a, ((0, 0), (0, 128 - a.shape[1]))) for a in arrays]
    total = sum(a.shape[0] for a in arrays)
    rows.append(jnp.zeros((16 - total, 128), F32))
    return jnp.concatenate(rows, axis=0)


def spread_vectors(qkv_sum, wide_grad, sums_one, sums_two, sizes):
    head_own, wide_own, gain_own, dp_size = sizes
    blocks, width = qkv_sum.shape[0], qkv_sum.shape[2] // 3

    def lanes128(array, own):
        array = array.reshape(array.shape[:-1] + (dp_size, own))
        return jnp.pad(array, ((0, 0),) * (array.ndim - 1) + ((0, 128 - own),))

    vectors = jnp.stack(
        [sums_one[0], sums_two[0], sums_one[2], sums_one[1], sums_two[2], sums_two[1]]
    )
    vectors = jnp.broadcast_to(
        lanes128(vectors, gain_own).transpose(1, 0, 2)[None], (blocks, dp_size, 6, 128)
    )
    return jnp.concatenate(
        [
            lanes128(qkv_sum[:, 0, :width], head_own)[:, :, None],
            lanes128(qkv_sum[:, 0, 2 * width :], head_own)[:, :, None],
            lanes128(wide_grad[:, 0], wide_own)[:, :, None],
            vectors,
            jnp.zeros((blocks, dp_size, 7, 128), F32),
        ],
        axis=2,
    )


def on_device(
    dp_size, tensor_size,
    tokens, cotangent, row_lengths, present, groups,
    attn_weight, attn_first, attn_second,
    mix_weight, mix_first, mix_second,
    up_weight, up_first, up_second,
    down_weight, down_first, down_second,
    head_bias, head_first, head_second,
    wide_bias, wide_first, wide_second,
    norm_gains, gain_first, gain_second,
    shift_bias, shift_first, shift_second,
):
    comm = GridComm() if (dp_size, tensor_size) == (8, 4) else GenericComm(dp_size, tensor_size)
    rank = lax.axis_index("tensor")
    row_count, n = groups.shape
    assert row_count == tensor_size
    d = tokens.shape[1]
    width, units = attn_weight.shape[2], up_weight.shape[1]
    head_own, wide_own, gain_own = head_bias.shape[1], wide_bias.shape[0], norm_gains.shape[1]
    small_arrays = [
        (head_bias, head_first, head_second),
        tuple(a.reshape(1, -1) for a in (wide_bias, wide_first, wide_second)),
        (norm_gains, gain_first, gain_second),
        (shift_bias, shift_first, shift_second),
    ]

    down_rows = down_weight.T
    small_masters = [group[0] for group in small_arrays]
    small_all = None
    if not comm.small_inside:
        small_all = comm.gather_small(pack_rows(small_masters).astype(BF).astype(F32))
    ffn_shard = prepare_ffn(up_weight, down_rows)
    (attn_shard,) = prepare(
        attn_weight, mix_weight, small_masters, comm.small_inside
    )
    attn_g = comm.gather(attn_shard)
    attn_g.z([])
    attn_g.xy([])
    attn_g.diagonal([])
    attn_w = attn_g.core()
    up_w, down_w = comm.gather_stacked(ffn_shard)

    tok = lax.dynamic_slice_in_dim(tokens, rank * n, n, 0)
    cot = lax.dynamic_slice_in_dim(cotangent, rank * n, n, 0)
    group_row = lax.dynamic_index_in_dim(groups, rank, 0, keepdims=False)
    present_row = lax.dynamic_index_in_dim(present, rank, 0, keepdims=False)
    length = lax.dynamic_index_in_dim(row_lengths, rank, 0, keepdims=False)
    feature_ids = jnp.arange(present_row.shape[0])
    present_key = jnp.sum(
        (group_row[:, None] == feature_ids[None, :]) * present_row[None, :], axis=1
    )
    key_open = ((jnp.arange(n) < length) & (present_key == 1)).astype(jnp.int32)

    qkv, ctx, e, inv, n1, rstd, low, low_t, tok_t, rows, wide_low = attn_fwd(
        attn_w, width, ((head_own, wide_own, gain_own, dp_size), small_all), tok, group_row, key_open
    )
    act, slope, layer_out, ds2, df, df_t, sums_two = (
        ffn := ffn_fwd(up_w, down_w, low, wide_low, n1, cot, rows, comm.small_inside)
    )[-7:]
    layer_out_all = lax.all_gather(layer_out, "tensor", axis=0, tiled=True)

    down_red = comm.reduction([df_t], library=True)
    if comm.small_inside:
        down_red.send_odd(ffn[0])
    else:
        down_red.core([act])
    up_red = comm.reduction([low_t, None])
    attn_red = comm.reduction([tok_t])
    sizes = (head_own, wide_own, gain_own, dp_size)
    small_sum = None
    ffn_args = (up_w, down_w, df, slope, ds2, n1, rstd, rows)
    down_entries = [(0, False, down_rows, down_first.T, down_second.T)]
    up_entries = [
        (0, False, up_weight, up_first, up_second),
        (units, True, mix_weight, mix_first, mix_second),
    ]
    if comm.small_inside:
        odd, dh, wide_grad, ds1, da, da_t, sums_one = ffn_bwd(*ffn_args, (low_t, ctx))
        up_red.lefts[1] = da_t
        up_red.send_odd(odd)
        done = down_red.split([act], deps=[da])
        vectors = (wide_grad, sums_one, sums_two, sizes)
        odd, dqkv_odd, _, back = attn_bwd(
            attn_w, width, (1, 3), tie(da, done), qkv, ctx, e, inv, ds1, False, vectors, tok_t
        )
        attn_red.send_odd(odd)
        done = down_red.neighbour([odd, layer_out_all], us=100)
        done = up_red.split([dh, ctx], deps=done + [attn_red.core_got])
        down_parts = down_red.last(done)
        extra, dqkv, _, back, layer_out_done = attn_bwd(
            attn_w, width, (0, 2), tie(da, down_red.done), qkv, ctx, e, inv, back, True, vectors,
            carried=layer_out_all,
        )
        done = attn_red.split([[([0, 2], dqkv)]], extra)
        down_parts[0] = tie(down_parts[0], done)
        down_done = lamb_matrices(down_parts, down_entries)
        done = up_red.neighbour(down_done[3:4], us=100)
        tokens_grad_all = lax.all_gather(tie(back, done), "tensor", axis=0, tiled=True)
        done = attn_red.neighbour(done, us=100)
        up_parts = up_red.last(done)
        attn_parts = attn_red.last(up_red.done)
        tokens_grad_done = copied(tokens_grad_all, attn_red.done)
        up_parts[1] = tie(up_parts[1], [tokens_grad_done])
        up_done = lamb_matrices(up_parts, up_entries)
    else:
        blocks = range(tensor_size)
        dh, wide_grad, ds1, da, da_t, sums_one = ffn_bwd(*ffn_args)
        up_red.lefts[1] = da_t
        dqkv, dqkv_sum, back = attn_bwd(attn_w, width, blocks, da, qkv, ctx, e, inv, ds1, True)
        tokens_grad_all = lax.all_gather(back, "tensor", axis=0, tiled=True)
        up_red.core([dh, ctx])
        attn_red.core([dqkv])
        layer_out_done = layer_out_all
        down_done = lamb_matrices(down_red.last(), down_entries)
        tokens_grad_done = tokens_grad_all
        up_done = lamb_matrices(up_red.last(), up_entries)
        attn_parts = attn_red.last()
        small_sum = comm.scatter_small(
            spread_vectors(dqkv_sum, wide_grad, sums_one, sums_two, sizes)
        )

    last = lamb_last(
        attn_parts, (attn_weight, attn_first, attn_second), small_sum, small_arrays,
        (up_done[6], down_done[3]), 1.0 / tensor_size,
    )
    small_moments, small_u, sums = last[3:11], last[11], last[12]
    done = finish(
        comm.total(sums),
        (attn_weight, mix_weight, up_weight, down_rows),
        (last[2], up_done[5], up_done[2], down_done[2]),
        small_masters,
        small_u,
    )
    moments = [last[0:2], up_done[3:5], up_done[0:2], down_done[0:2]]
    moments += [small_moments[2 * k : 2 * k + 2] for k in range(4)]
    result = [layer_out_done, tokens_grad_done]
    for number, (first_new, second_new) in enumerate(moments):
        group = [done[number], first_new, second_new]
        if number == 3:
            group = [a.T for a in group]
        result += [a.reshape(-1) for a in group] if number == 5 else group
    return tuple(result) + (done[8],)


def solution(mesh):
    rows = P("dp", None)
    attn, mix, up = P(None, "dp", "tensor"), P("tensor", "dp"), P("dp", "tensor")
    head, wide, col = P(None, ("tensor", "dp")), P(("tensor", "dp")), P(None, "dp")
    params = tuple(spec for spec in (attn, mix, up, mix, head, wide, col, col) for _ in range(3))
    return jax.shard_map(
        functools.partial(on_device, mesh.shape["dp"], mesh.shape["tensor"]),
        mesh=mesh,
        in_specs=(rows, rows, P("dp"), rows, rows) + params,
        out_specs=(rows, rows) + params + (P(),),
        check_vma=False,
    )
```
